32 devices in a mesh: clip: 8 (over z, x), st: 4 (over y, core).
Axes of the slice: x: 2, y: 2, z: 4, core: 2. Of those that a mesh axis runs over, the one named last changes fastest.
Arguments:
- clips: bfloat16 [8, 8, 196, 768], P('clip', 'st'), may hold values from -6 to 6
- time_gain: bfloat16 [768], P(('clip', 'st')), may hold values from 0.5 to 1.5
- time_shift: bfloat16 [768], P(('clip', 'st')), may hold values from -2 to 2
- time_heads: bfloat16 [768, 2304], P(('clip', 'st')), may hold values from -0.3125 to 0.3125
- time_merge: bfloat16 [768, 768], P(('clip', 'st')), may hold values from -0.4375 to 0.4375
- merge_bias: bfloat16 [768], P(('clip', 'st')), may hold values from -2 to 2
- time_mixer: bfloat16 [768, 768], P(('clip', 'st')), may hold values from -0.21875 to 0.21875
- mixer_bias: bfloat16 [768], P(('clip', 'st')), may hold values from -2 to 2
- space_gain: bfloat16 [768], P(('clip', 'st')), may hold values from 0.5 to 1.5
- space_shift: bfloat16 [768], P(('clip', 'st')), may hold values from -2 to 2
- space_heads: bfloat16 [768, 2304], P(('clip', 'st')), may hold values from -0.3125 to 0.3125
- space_merge: bfloat16 [768, 768], P(('clip', 'st')), may hold values from -0.875 to 0.875
- space_bias: bfloat16 [768], P(('clip', 'st')), may hold values from -2 to 2
- feed_gain: bfloat16 [768], P(('clip', 'st')), may hold values from 0.5 to 1.5
- feed_shift: bfloat16 [768], P(('clip', 'st')), may hold values from -2 to 2
- feed_expand: bfloat16 [768, 3072], P(('clip', 'st')), may hold values from -0.21875 to 0.21875
- expand_bias: bfloat16 [3072], P(('clip', 'st')), may hold values from -2 to 2
- feed_reduce: bfloat16 [3072, 768], P(('clip', 'st')), may hold values from -0.109375 to 0.109375
- reduce_bias: bfloat16 [768], P(('clip', 'st')), may hold values from -2 to 2
- cotangent: bfloat16 [8, 8, 196, 768], P('clip', 'st'), may hold values from -6 to 6
Outputs:
- layer_output: bfloat16 [8, 8, 196, 768], P('clip', 'st')
- grad_clips: bfloat16 [8, 8, 196, 768], P('clip', 'st')
- grad_time_gain: float32 [768], P(('clip', 'st'))
- grad_time_shift: float32 [768], P(('clip', 'st'))
- grad_time_heads: float32 [768, 2304], P(('clip', 'st'))
- grad_time_merge: float32 [768, 768], P(('clip', 'st'))
- grad_merge_bias: float32 [768], P(('clip', 'st'))
- grad_time_mixer: float32 [768, 768], P(('clip', 'st'))
- grad_mixer_bias: float32 [768], P(('clip', 'st'))
- grad_space_gain: float32 [768], P(('clip', 'st'))
- grad_space_shift: float32 [768], P(('clip', 'st'))
- grad_space_heads: float32 [768, 2304], P(('clip', 'st'))
- grad_space_merge: float32 [768, 768], P(('clip', 'st'))
- grad_space_bias: float32 [768], P(('clip', 'st'))
- grad_feed_gain: float32 [768], P(('clip', 'st'))
- grad_feed_shift: float32 [768], P(('clip', 'st'))
- grad_feed_expand: float32 [768, 3072], P(('clip', 'st'))
- grad_expand_bias: float32 [3072], P(('clip', 'st'))
- grad_feed_reduce: float32 [3072, 768], P(('clip', 'st'))
- grad_reduce_bias: float32 [768], P(('clip', 'st'))
The draws below stay inside these ranges and needn't reach their ends.
All inputs are finite; a program needn't handle non-finite values.
Results may differ from the reference program's by a relative error of at most 0.025.
The reference program's roundings to bfloat16 on the way count: a program that leaves them out, or rounds other values in their place, can miss the bound.
Values may be sent and summed in bfloat16 or wider, within the bound.
No kernel may reach another device: no remote copies, remote signals or barrier semaphores. Data moves between devices by JAX's collectives and lax.ppermute only.
A program may use at most 192 MiB of HBM per device.

```python
import jax
import jax.numpy as jnp
from jax import lax

D = 768
HEADS = 12
HEAD_DIM = 64
FF = 3072
FRAMES = 8
PLACES = 196
CLIP_GROUP = 1
CLIPS = 8
N_CLIP = 8


def shard_levels(stream_key, extent, shards, smallest, high):
    level = 1.0
    for axis_at, shards_of in shards:
        draws = jax.random.uniform(jax.random.fold_in(jax.random.fold_in(stream_key, 6), axis_at), (shards_of,), jnp.float32, smallest / len(shards), high / len(shards))
        level = level * jnp.repeat(jnp.exp(draws), extent[axis_at] // shards_of).reshape((-1,) + (1,) * (len(extent) - 1 - axis_at))
    return level


def scatter_about(stream_key, dims, scale, bound, pieces=(), held_as=jnp.bfloat16):
    level = shard_levels(stream_key, dims, pieces, -0.22, 0.18) if pieces else 1.0
    drawn = jax.random.normal(stream_key, dims, jnp.float32) * scale * level
    return jnp.minimum(jnp.maximum(drawn, -bound), bound).astype(held_as)


def setup_inputs(seed: int = 0) -> dict:
    key_list = jax.random.split(jax.random.key(seed), 21)
    return {
        "clips": scatter_about(key_list[0], (CLIPS, FRAMES, PLACES, D), 1.0, 6.0, ((0, 8), (1, 4))),
        "time_gain": jnp.clip(1.0 + 0.1 * jax.random.normal(key_list[1], (D,), jnp.float32), 0.5, 1.5).astype(jnp.bfloat16),
        "time_shift": scatter_about(key_list[2], (D,), 0.3, 2.0, ((0, 32),)),
        "time_heads": scatter_about(key_list[3], (D, 3 * D), (D // 2) ** -0.5, 0.3125, ((0, 32),)),
        "time_merge": scatter_about(key_list[4], (D, D), (D // 4) ** -0.5, 0.4375, ((0, 32),)),
        "merge_bias": scatter_about(key_list[5], (D,), 0.3, 2.0, ((0, 32),)),
        "time_mixer": scatter_about(key_list[6], (D, D), D ** -0.5, 0.21875, ((0, 32),)),
        "mixer_bias": scatter_about(key_list[7], (D,), 0.3, 2.0, ((0, 32),)),
        "space_gain": jnp.clip(1.0 + 0.1 * jax.random.normal(key_list[8], (D,), jnp.float32), 0.5, 1.5).astype(jnp.bfloat16),
        "space_shift": scatter_about(key_list[9], (D,), 0.3, 2.0, ((0, 32),)),
        "space_heads": scatter_about(key_list[10], (D, 3 * D), (D // 2) ** -0.5, 0.3125, ((0, 32),)),
        "space_merge": scatter_about(key_list[11], (D, D), (D // 16) ** -0.5, 0.875, ((0, 32),)),
        "space_bias": scatter_about(key_list[12], (D,), 0.3, 2.0, ((0, 32),)),
        "feed_gain": jnp.clip(1.0 + 0.1 * jax.random.normal(key_list[13], (D,), jnp.float32), 0.5, 1.5).astype(jnp.bfloat16),
        "feed_shift": scatter_about(key_list[14], (D,), 0.3, 2.0, ((0, 32),)),
        "feed_expand": scatter_about(key_list[15], (D, FF), D ** -0.5, 0.21875, ((0, 32),)),
        "expand_bias": scatter_about(key_list[16], (FF,), 0.3, 2.0, ((0, 32),)),
        "feed_reduce": scatter_about(key_list[17], (FF, D), FF ** -0.5, 0.109375, ((0, 32),)),
        "reduce_bias": scatter_about(key_list[18], (D,), 0.3, 2.0, ((0, 32),)),
        "cotangent": scatter_about(key_list[19], (CLIPS, FRAMES, PLACES, D), 1.0, 6.0, ((0, 8), (1, 4))),
    }


@jax.custom_vjp
def low(v):
    return lax.optimization_barrier(v.astype(jnp.bfloat16)).astype(jnp.float32)

@jax.custom_vjp
def low_back(v):
    return v

def low_keep(v):
    return (low(v), None)

def low_pass(kept, grad):
    return (grad,)

def back_keep(v):
    return (v, None)

def back_low(kept, grad):
    return (low(grad),)
low.defvjp(low_keep, low_pass)
low_back.defvjp(back_keep, back_low)
HIGHEST = lax.Precision.HIGHEST
EPSILON = 1e-06
SCALE = 0.125

def rounded(value):
    return low_back(low(value))

def layer_norm(value, gain, shift):
    centred = value - lax.optimization_barrier(jnp.mean(value, -1, keepdims=True))
    inverse = lax.rsqrt(lax.optimization_barrier(jnp.mean(centred * centred, -1, keepdims=True)) + EPSILON)
    return centred * inverse * gain + shift

def product(left, matrix):
    return jnp.dot(left, matrix, precision=HIGHEST, preferred_element_type=jnp.float32)

def attention(packed):
    heads = packed.reshape(packed.shape[:-1] + (3, HEADS, HEAD_DIM))
    queries = heads[..., 0, :, :]
    key_rows = heads[..., 1, :, :]
    value_rows = heads[..., 2, :, :]
    scores = low_back(jnp.einsum('bqphd,bkphd->bphqk', queries, key_rows, precision=HIGHEST) * SCALE)
    shares = low(jax.nn.softmax(scores, axis=-1))
    mixed = jnp.einsum('bphqk,bkphd->bqphd', shares, value_rows, precision=HIGHEST)
    return mixed.reshape(packed.shape[:-1] + (HEADS * HEAD_DIM,))

def layer(block, params):
    time_gain, time_shift, time_heads, time_merge, merge_bias, time_mixer, mixer_bias, space_gain, space_shift, space_heads, space_merge, space_bias, feed_gain, feed_shift, feed_expand, expand_bias, feed_reduce, reduce_bias = params
    groups, frames, places, width = block.shape
    entry = low_back(block)
    normed = low(layer_norm(entry, time_gain, time_shift))
    packed = rounded(product(normed, time_heads))
    mixed = rounded(attention(packed))
    middle = rounded(product(mixed, time_merge) + merge_bias)
    branch = rounded(product(middle, time_mixer) + mixer_bias)
    after_time = block + branch
    normed = low(layer_norm(after_time, space_gain, space_shift))
    packed = rounded(product(normed, space_heads)).reshape(groups * frames, places, 1, 3 * width)
    mixed = rounded(attention(packed)).reshape(groups, frames, places, width)
    after_space = after_time + low_back(product(mixed, space_merge) + space_bias)
    normed = low(layer_norm(after_space, feed_gain, feed_shift))
    hidden = low_back(product(normed, feed_expand) + expand_bias)
    active = low(jax.nn.gelu(hidden, approximate=False))
    return after_space + product(active, feed_reduce) + reduce_bias

def reference(clips, time_gain, time_shift, time_heads, time_merge, merge_bias, time_mixer, mixer_bias, space_gain, space_shift, space_heads, space_merge, space_bias, feed_gain, feed_shift, feed_expand, expand_bias, feed_reduce, reduce_bias, cotangent):
    params = tuple((weight.astype(jnp.float32) for weight in (time_gain, time_shift, time_heads, time_merge, merge_bias, time_mixer, mixer_bias, space_gain, space_shift, space_heads, space_merge, space_bias, feed_gain, feed_shift, feed_expand, expand_bias, feed_reduce, reduce_bias)))
    blocks = clips.astype(jnp.float32).reshape(N_CLIP, CLIP_GROUP, FRAMES, PLACES, D)
    upstream = cotangent.astype(jnp.float32).reshape(N_CLIP, CLIP_GROUP, FRAMES, PLACES, D)

    def step(totals, pair):
        block, incoming = pair
        result, pullback = jax.vjp(layer, block, params)
        grad_block, grad_params = pullback(incoming)
        totals = tuple((total + grad for total, grad in zip(totals, grad_params)))
        return (totals, (result.astype(jnp.bfloat16), grad_block.astype(jnp.bfloat16)))
    zeros = tuple((jnp.zeros(weight.shape, jnp.float32) for weight in params))
    totals, (results, grads) = lax.scan(step, zeros, (blocks, upstream))
    layer_output = results.reshape(clips.shape)
    grad_clips = grads.reshape(clips.shape)
    return (layer_output, grad_clips, totals[0], totals[1], totals[2], totals[3], totals[4], totals[5], totals[6], totals[7], totals[8], totals[9], totals[10], totals[11], totals[12], totals[13], totals[14], totals[15], totals[16], totals[17])
```

```python
import functools

import jax
import jax.numpy as jnp
from jax import lax
from jax.experimental import pallas as pl
from jax.experimental.pallas import tpu as pltpu
from jax.sharding import Mesh
from jax.sharding import PartitionSpec as P

HEADS = 12
HEAD_DIM = 64
LANES = 128
EPSILON = 1e-06
SCALE = 0.125
ROOT_HALF = 0.7071067811865476
DENSITY = 0.3989422804014327
LOW = jnp.bfloat16
HIGH = jnp.float32
VMEM_BYTES = 56 * 1024 * 1024

TIME_GAIN, TIME_SHIFT, MERGE_BIAS, MIXER_BIAS = 0, 1, 2, 3
SPACE_GAIN, SPACE_SHIFT, SPACE_BIAS = 4, 5, 6
FEED_GAIN, FEED_SHIFT, REDUCE_BIAS, EXPAND_BIAS = 7, 8, 9, 10
VECTORS = 14
ROWS_OF_VECTORS = 16


def dot(left, right):
    return jnp.dot(left, right, preferred_element_type=HIGH)


def dot_nt(left, right):
    return lax.dot_general(left, right, (((1,), (1,)), ((), ())), preferred_element_type=HIGH)


def dot_tn(left, right):
    return lax.dot_general(left, right, (((0,), (0,)), ((), ())), preferred_element_type=HIGH)


def norm(values, gain, shift):
    centred = values - jnp.mean(values, -1, keepdims=True)
    inverse = lax.rsqrt(jnp.mean(centred * centred, -1, keepdims=True) + EPSILON)
    normed = centred * inverse
    return normed * gain + shift, normed, inverse


def norm_back(upstream, normed, inverse, gain):
    scaled = upstream * gain
    return inverse * (
        scaled
        - jnp.mean(scaled, -1, keepdims=True)
        - normed * jnp.mean(scaled * normed, -1, keepdims=True)
    )


def column_sum(values):
    return jnp.sum(values, 0, keepdims=True)


def stacked(pair):
    lane = lax.broadcasted_iota(jnp.int32, (1, LANES), 1)
    first = jnp.where(lane < HEAD_DIM, 1.0, 0.0).astype(LOW)
    second = jnp.where(lane < HEAD_DIM, 0.0, 1.0).astype(LOW)
    return jnp.concatenate([pair * first, pair * second], 0)


def joined(both):
    rows = both.shape[0] // 2
    lane = lax.broadcasted_iota(jnp.int32, (rows, LANES), 1)
    return jnp.where(lane < HEAD_DIM, both[:rows], both[rows:])


def shares_of(queries, key_rows, valid):
    scores = jnp.where(valid, dot_nt(queries, key_rows) * SCALE, -1e30)
    raised = jnp.exp(scores - jnp.max(scores, -1, keepdims=True))
    return raised * (1.0 / jnp.sum(raised, -1, keepdims=True))


def pair_forward(packed_ref, mixed_ref, rows, pair, width, valid):
    at = [pl.ds(pl.multiple_of(pair * LANES + part * width, LANES), LANES) for part in range(3)]
    queries = stacked(packed_ref[rows, at[0]])
    shares = shares_of(queries, packed_ref[rows, at[1]], valid)
    mixed = dot(shares.astype(LOW), packed_ref[rows, at[2]])
    mixed_ref[rows, at[0]] = joined(mixed).astype(LOW)


def pair_backward(packed_ref, up_ref, grad_ref, rows, pair, width, valid):
    at = [pl.ds(pl.multiple_of(pair * LANES + part * width, LANES), LANES) for part in range(3)]
    queries = stacked(packed_ref[rows, at[0]])
    key_rows = packed_ref[rows, at[1]]
    upstream = stacked(up_ref[rows, at[0]])
    shares = shares_of(queries, key_rows, valid)
    grad_shares = dot_nt(upstream, packed_ref[rows, at[2]])
    grad_scores = (
        shares * (grad_shares - jnp.sum(grad_shares * shares, -1, keepdims=True))
    ).astype(LOW)
    grad_ref[rows, at[0]] = (joined(dot(grad_scores, key_rows)) * SCALE).astype(LOW)
    grad_ref[rows, at[1]] = (dot_tn(grad_scores, queries) * SCALE).astype(LOW)
    grad_ref[rows, at[2]] = dot_tn(shares.astype(LOW), upstream).astype(LOW)


def time_valid(block, frames):
    row = lax.broadcasted_iota(jnp.int32, (2 * block, block), 0)
    col = lax.broadcasted_iota(jnp.int32, (2 * block, block), 1)
    return (row % block) // frames == col // frames


def space_valid(rows, pad, places):
    col = lax.broadcasted_iota(jnp.int32, (2 * rows, rows), 1)
    return col % pad < places


def vector(vec_ref, row):
    return vec_ref[row : row + 1, :]


def to_places(tokens_ref, tiles_ref):
    frames, places, width = tokens_ref.shape
    tiles_ref[...] = jnp.zeros_like(tiles_ref)
    for frame in range(frames):
        rows = tokens_ref[frame].astype(HIGH)
        for tile in range(width // LANES):
            at = slice(tile * LANES, (tile + 1) * LANES)
            tiles_ref[tile, pl.ds(frame, places, stride=frames), :] = rows[:, at]
    return jnp.concatenate([tiles_ref[tile] for tile in range(width // LANES)], 1)


def from_places(values, tiles_ref, tokens_ref):
    frames, places, width = tokens_ref.shape
    for tile in range(width // LANES):
        tiles_ref[tile] = values[:, tile * LANES : (tile + 1) * LANES]
    for frame in range(frames):
        for tile in range(width // LANES):
            at = slice(tile * LANES, (tile + 1) * LANES)
            rows = tiles_ref[tile, pl.ds(frame, places, stride=frames), :]
            tokens_ref[frame, :, at] = rows.astype(LOW)


def to_frames(tokens_ref, held_ref, pad):
    quarters, frames, places, _ = tokens_ref.shape
    held_ref[...] = jnp.zeros_like(held_ref)
    for frame in range(frames):
        for quarter in range(quarters):
            start = (frame * quarters + quarter) * pad
            held_ref[start : start + places, :] = tokens_ref[quarter, frame].astype(held_ref.dtype)


def from_frames(held, tokens_ref, pad):
    quarters, frames, places, _ = tokens_ref.shape
    for frame in range(frames):
        for quarter in range(quarters):
            start = (frame * quarters + quarter) * pad
            tokens_ref[quarter, frame] = held[start : start + places].astype(LOW)


def put(core, half, keep_ref, send_ref, at, value):
    @pl.when(core == half)
    def _():
        keep_ref[:, at] = value

    @pl.when(core != half)
    def _():
        send_ref[:, at] = value


def time_forward_kernel(
    tokens_ref, weight_ref, vec_ref, branch_ref, entry_ref, packed_ref, mixed_ref, middle_ref, tiles_ref
):
    frames = tokens_ref.shape[0]
    width = tokens_ref.shape[-1]
    rows = entry_ref.shape[0]
    block = 64
    tokens = to_places(tokens_ref, tiles_ref)
    entry, _, _ = norm(tokens, vector(vec_ref, TIME_GAIN), vector(vec_ref, TIME_SHIFT))
    entry_ref[...] = entry.astype(LOW)
    for part in range(3):
        at = slice(part * width, (part + 1) * width)
        packed_ref[:, at] = dot(entry_ref[...], weight_ref[:, at]).astype(LOW)
    valid = time_valid(block, frames)

    def step(pair, carry):
        for start in range(0, rows, block):
            pair_forward(packed_ref, mixed_ref, slice(start, start + block), pair, width, valid)
        return carry

    lax.fori_loop(0, HEADS // 2, step, 0)
    merge = weight_ref[:, 3 * width : 4 * width]
    middle_ref[...] = (dot(mixed_ref[...], merge) + vector(vec_ref, MERGE_BIAS)).astype(LOW)
    mixer = weight_ref[:, 4 * width : 5 * width]
    branch = dot(middle_ref[...], mixer) + vector(vec_ref, MIXER_BIAS)
    from_places(branch, tiles_ref, branch_ref)


def space_forward_kernel(
    clips_ref, branch_ref, weight_ref, vec_ref, after_time_ref, after_space_ref, entry_ref, packed_ref, mixed_ref, held_ref
):
    _, frames, places, width = clips_ref.shape
    rows = held_ref.shape[0]
    pad = rows // (frames * clips_ref.shape[0])
    to_frames(clips_ref, after_time_ref, pad)
    to_frames(branch_ref, held_ref, pad)
    after_time = after_time_ref[...] + held_ref[...]
    after_time_ref[...] = after_time
    entry, _, _ = norm(after_time, vector(vec_ref, SPACE_GAIN), vector(vec_ref, SPACE_SHIFT))
    entry_ref[...] = entry.astype(LOW)
    for part in range(3):
        at = slice(part * width, (part + 1) * width)
        packed_ref[:, at] = dot(entry_ref[...], weight_ref[:, at]).astype(LOW)
    each = rows // frames
    valid = space_valid(each, pad, places)

    def step(pair, carry):
        for start in range(0, rows, each):
            pair_forward(packed_ref, mixed_ref, slice(start, start + each), pair, width, valid)
        return carry

    lax.fori_loop(0, HEADS // 2, step, 0)
    merge = weight_ref[:, 3 * width : 4 * width]
    after_space_ref[...] = (
        after_time_ref[...] + dot(mixed_ref[...], merge) + vector(vec_ref, SPACE_BIAS)
    )


def feed_kernel(
    core_ref, after_space_ref, upstream_ref, weight_ref, vec_ref,
    result_ref, space_sum_ref, keep_ref, send_ref, grad_vec_ref,
    held_ref, up_ref, entry_ref, out_ref, back_ref,
):
    width = after_space_ref.shape[-1]
    rows = held_ref.shape[0]
    quarters, frames = upstream_ref.shape[:2]
    pad = rows // (quarters * frames)
    blocks = weight_ref.shape[1] // (2 * width)
    core = core_ref[0]
    to_frames(upstream_ref, held_ref, pad)
    up_ref[...] = held_ref[...].astype(LOW)
    entry, _, _ = norm(after_space_ref[...], vector(vec_ref, FEED_GAIN), vector(vec_ref, FEED_SHIFT))
    entry_ref[...] = entry.astype(LOW)
    out_ref[...] = after_space_ref[...] + vector(vec_ref, REDUCE_BIAS)
    back_ref[...] = jnp.zeros_like(back_ref)
    grad_vec_ref[...] = jnp.zeros_like(grad_vec_ref)

    def step(block, carry):
        at = pl.ds(pl.multiple_of(block * width, LANES), width)
        reduce_at = pl.ds(pl.multiple_of((blocks + block) * width, LANES), width)
        expand = weight_ref[:, at]
        reduce = weight_ref[:, reduce_at]
        hidden = dot(entry_ref[...], expand) + vec_ref[pl.ds(EXPAND_BIAS + block, 1), :]
        normal = 0.5 * (1.0 + lax.erf(hidden * ROOT_HALF))
        active = (hidden * normal).astype(LOW)
        out_ref[...] += dot(active, reduce)
        put(core, 1, keep_ref, send_ref, at, dot_tn(active, up_ref[...]).astype(LOW))
        slope = normal + hidden * DENSITY * jnp.exp(-0.5 * hidden * hidden)
        hidden_grad = (dot_nt(up_ref[...], reduce) * slope).astype(LOW)
        grad_vec_ref[pl.ds(3 + block, 1), :] = column_sum(hidden_grad.astype(HIGH))
        put(core, 0, keep_ref, send_ref, at, dot_tn(entry_ref[...], hidden_grad).astype(LOW))
        back_ref[...] += dot_nt(hidden_grad, expand)
        return carry

    lax.fori_loop(0, blocks, step, 0)
    from_frames(out_ref, result_ref, pad)
    gain = vector(vec_ref, FEED_GAIN)
    _, normed, inverse = norm(after_space_ref[...], gain, vector(vec_ref, FEED_SHIFT))
    upstream = back_ref[...]
    grad_vec_ref[0:1, :] = column_sum(upstream * normed)
    grad_vec_ref[1:2, :] = column_sum(upstream)
    grad_vec_ref[2:3, :] = column_sum(held_ref[...])
    space_sum_ref[...] = held_ref[...] + norm_back(upstream, normed, inverse, gain)


def space_backward_kernel(
    core_ref, space_sum_ref, after_time_ref, entry_ref, packed_ref, mixed_ref, weight_ref, vec_ref,
    time_sum_ref, time_round_ref, keep_ref, send_ref, grad_vec_ref,
    round_ref, up_ref, grad_ref,
):
    width = space_sum_ref.shape[-1]
    rows = space_sum_ref.shape[0]
    quarters, frames, places, _ = time_round_ref.shape
    pad = rows // (quarters * frames)
    core = core_ref[0]
    half = keep_ref.shape[1]
    round_ref[...] = space_sum_ref[...].astype(LOW)
    merge = weight_ref[:, 3 * width : 4 * width]
    up_ref[...] = dot_nt(round_ref[...], merge).astype(LOW)
    put(core, 1, keep_ref, send_ref, slice(half - width, half), dot_tn(mixed_ref[...], round_ref[...]).astype(LOW))
    each = rows // frames
    valid = space_valid(each, pad, places)

    def step(pair, carry):
        for start in range(0, rows, each):
            pair_backward(packed_ref, up_ref, grad_ref, slice(start, start + each), pair, width, valid)
        return carry

    lax.fori_loop(0, HEADS // 2, step, 0)
    back = dot_nt(grad_ref[:, 0:width], weight_ref[:, 0:width])
    for part in range(3):
        at = slice(part * width, (part + 1) * width)
        if part:
            back += dot_nt(grad_ref[:, at], weight_ref[:, at])
        value = dot_tn(entry_ref[...], grad_ref[:, at]).astype(LOW)
        start = part * width % half
        put(core, part * width // half, keep_ref, send_ref, slice(start, start + width), value)
    gain = vector(vec_ref, SPACE_GAIN)
    _, normed, inverse = norm(after_time_ref[...], gain, vector(vec_ref, SPACE_SHIFT))
    grad_vec_ref[...] = jnp.zeros_like(grad_vec_ref)
    grad_vec_ref[0:1, :] = column_sum(back * normed)
    grad_vec_ref[1:2, :] = column_sum(back)
    grad_vec_ref[2:3, :] = column_sum(round_ref[...].astype(HIGH))
    time_sum_ref[...] = space_sum_ref[...] + norm_back(back, normed, inverse, gain)
    from_frames(time_sum_ref, time_round_ref, pad)


def time_backward_kernel(
    core_ref, time_round_ref, tokens_ref, entry_ref, packed_ref, mixed_ref, middle_ref, weight_ref, vec_ref,
    space_vec_ref, feed_vec_ref,
    inward_ref, keep_ref, send_ref,
    tiles_ref, round_ref, up_ref, grad_ref, vectors_ref,
):
    frames = tokens_ref.shape[0]
    width = tokens_ref.shape[-1]
    rows = round_ref.shape[0]
    block = 64
    core = core_ref[0]
    half = keep_ref.shape[1]
    rounded = to_places(time_round_ref, tiles_ref)
    round_ref[...] = rounded.astype(LOW)
    vectors_ref[...] = jnp.zeros_like(vectors_ref)
    vectors_ref[MIXER_BIAS : MIXER_BIAS + 1, :] = column_sum(rounded)
    mixer = weight_ref[:, 4 * width : 5 * width]
    merge = weight_ref[:, 3 * width : 4 * width]
    tail = 3 * width - half
    at = slice(tail + width, tail + 2 * width)
    put(core, 1, keep_ref, send_ref, at, dot_tn(middle_ref[...], round_ref[...]).astype(LOW))
    up_ref[...] = dot_nt(round_ref[...], mixer).astype(LOW)
    vectors_ref[MERGE_BIAS : MERGE_BIAS + 1, :] = column_sum(up_ref[...].astype(HIGH))
    at = slice(tail, tail + width)
    put(core, 1, keep_ref, send_ref, at, dot_tn(mixed_ref[...], up_ref[...]).astype(LOW))
    up_ref[...] = dot_nt(up_ref[...], merge).astype(LOW)
    valid = time_valid(block, frames)

    def step(pair, carry):
        for start in range(0, rows, block):
            pair_backward(packed_ref, up_ref, grad_ref, slice(start, start + block), pair, width, valid)
        return carry

    lax.fori_loop(0, HEADS // 2, step, 0)
    for start, stop in ((0, half // 2), (half // 2, half), (half, 3 * width)):
        value = dot_tn(entry_ref[...], grad_ref[:, start:stop]).astype(LOW)
        put(core, start // half, keep_ref, send_ref, slice(start % half, start % half + stop - start), value)
    back = dot_nt(grad_ref[:, 0:width], weight_ref[:, 0:width])
    for part in range(1, 3):
        at = slice(part * width, (part + 1) * width)
        back += dot_nt(grad_ref[:, at], weight_ref[:, at])
    tokens = to_places(tokens_ref, tiles_ref)
    gain = vector(vec_ref, TIME_GAIN)
    _, normed, inverse = norm(tokens, gain, vector(vec_ref, TIME_SHIFT))
    vectors_ref[TIME_GAIN : TIME_GAIN + 1, :] = column_sum(back * normed)
    vectors_ref[TIME_SHIFT : TIME_SHIFT + 1, :] = column_sum(back)
    for row in range(3):
        vectors_ref[SPACE_GAIN + row : SPACE_GAIN + row + 1, :] = space_vec_ref[row : row + 1, :]
    for row in range(VECTORS - FEED_GAIN):
        vectors_ref[FEED_GAIN + row : FEED_GAIN + row + 1, :] = feed_vec_ref[row : row + 1, :]
    columns = jnp.transpose(vectors_ref[...]).astype(LOW)
    put(core, 1, keep_ref, send_ref, slice(half - 2 * LANES, half - LANES), columns)
    put(core, 1, keep_ref, send_ref, slice(half - LANES, half), jnp.zeros_like(columns))
    from_places(norm_back(back, normed, inverse, gain), tiles_ref, inward_ref)


def call(kernel, outs, scratch, flops, name):
    in_vmem = pl.BlockSpec(memory_space=pltpu.VMEM)
    in_smem = pl.BlockSpec(memory_space=pltpu.SMEM)

    def run(*args):
        moved = sum(a.size * a.dtype.itemsize for a in args)
        moved += sum(s.size * s.dtype.itemsize for s in outs)
        return pl.pallas_call(
            kernel,
            out_shape=outs,
            in_specs=[in_smem if a.ndim == 1 else in_vmem for a in args],
            out_specs=tuple(in_vmem for _ in outs),
            scratch_shapes=scratch,
            compiler_params=pltpu.CompilerParams(vmem_limit_bytes=VMEM_BYTES),
            cost_estimate=pl.CostEstimate(flops=flops, bytes_accessed=moved, transcendentals=0),
            name=name,
        )(*args)

    return run


def shape(dims, dtype=LOW):
    return jax.ShapeDtypeStruct(dims, dtype)


SWAP = ((0, 1), (1, 0))


def swapped(value, axis):
    return lax.ppermute(value, axis, SWAP)


def added(left, right, dtype=LOW):
    return (left.astype(HIGH) + right.astype(HIGH)).astype(dtype)


def picked(value, index, axis):
    return lax.dynamic_index_in_dim(value, index, axis, keepdims=False)


def scatter_sum(keep, send):
    core, x, y = lax.axis_index("core"), lax.axis_index("x"), lax.axis_index("y")
    count = lax.axis_size("z")
    half = keep.shape[1]
    rows = keep.shape[0] // (count * 4)
    received = swapped(send, "core")
    grid = (count, 2, 2, rows, half)
    keep, received = keep.reshape(grid), received.reshape(grid)

    def first(columns, index, axis):
        return added(
            picked(keep[..., columns], index, axis), picked(received[..., columns], index, axis)
        )

    left, right = slice(0, half // 2), slice(half // 2, half)
    left_got = swapped(first(left, 1 - y, 2), "y")
    right_got = swapped(first(right, 1 - x, 1), "x")
    left_kept, right_kept = first(left, y, 2), first(right, x, 1)

    def second(kept, got, index):
        return added(picked(kept, index, 1), picked(got, index, 1))

    left_last = swapped(second(left_kept, left_got, 1 - x), "x")
    right_last = swapped(second(right_kept, right_got, 1 - y), "y")
    column = jnp.concatenate(
        [
            added(second(left_kept, left_got, x), left_last),
            added(second(right_kept, right_got, y), right_last),
        ],
        -1,
    )
    arrived = lax.all_to_all(column, "z", split_axis=0, concat_axis=0, tiled=True)
    total = arrived.astype(HIGH).sum(0).reshape(2, rows // 2, half)
    mine = picked(total, core, 0)
    other = swapped(picked(total, 1 - core, 0), "core")
    return jnp.where(
        core == 0, jnp.concatenate([mine, other], -1), jnp.concatenate([other, mine], -1)
    )


def regrouped(tokens):
    return lax.all_to_all(tokens, ("y", "core"), split_axis=0, concat_axis=0, tiled=True)


def in_quarters(tokens, quarters):
    _, frames, places, width = tokens.shape
    return tokens.reshape(frames, quarters, places // quarters, width).swapaxes(0, 1)


def body(
    clips, time_gain, time_shift, time_heads, time_merge, merge_bias, time_mixer, mixer_bias,
    space_gain, space_shift, space_heads, space_merge, space_bias,
    feed_gain, feed_shift, feed_expand, expand_bias, feed_reduce, reduce_bias, cotangent,
):
    everyone = ("z", "x", "y", "core")
    _, near, all_places, width = clips.shape
    quarters = lax.axis_size("y") * lax.axis_size("core")
    frames, places = near * quarters, all_places // quarters
    pad = -(-places // 8) * 8
    rows = frames * pad
    hidden = feed_expand.shape[1]
    blocks = hidden // width
    share = feed_expand.shape[0]
    count = width // share
    core = lax.axis_index("core").astype(jnp.int32).reshape(1)

    vectors = jnp.stack(
        [
            time_gain, time_shift, merge_bias, mixer_bias, space_gain, space_shift, space_bias,
            feed_gain, feed_shift, reduce_bias, *expand_bias.reshape(blocks, share),
        ],
        1,
    )
    time_pack = jnp.concatenate(
        [time_heads, time_merge, time_mixer, jnp.pad(vectors, ((0, 0), (0, 2 * LANES - VECTORS)))], 1
    )
    space_pack = jnp.concatenate([space_heads, space_merge], 1)
    expand_shuffled = feed_expand.reshape(share, count, blocks, share).swapaxes(1, 2).reshape(share, hidden)
    feed_pack = jnp.concatenate([expand_shuffled, *feed_reduce.reshape(blocks, share, width)], 1)

    def gathered(shard):
        return lax.all_gather(shard, everyone, axis=0, tiled=True)

    time_weight = gathered(time_pack)
    rest = gathered(jnp.concatenate([space_pack, feed_pack], 1))
    space_weight, feed_weight = rest[:, : 4 * width], rest[:, 4 * width :]
    vec = jnp.pad(
        time_weight[:, 5 * width : 5 * width + VECTORS].astype(HIGH).T,
        ((0, ROWS_OF_VECTORS - VECTORS), (0, 0)),
    )

    clips_in = in_quarters(clips, quarters)
    upstream_in = in_quarters(cotangent, quarters)
    by_place = regrouped(clips_in).reshape(frames, places, width)
    tall, tokens = (rows, width), (frames, places, width)
    tiles = (width // LANES, rows, LANES)
    token_flops = 2 * rows * width * width

    branch, time_entry, time_packed, time_mixed, time_middle = call(
        time_forward_kernel,
        (shape(tokens), shape(tall), shape((rows, 3 * width)), shape(tall), shape(tall)),
        [pltpu.VMEM(tiles, HIGH)],
        6 * token_flops,
        "time_forward",
    )(by_place, time_weight, vec)
    by_frame = regrouped(branch.reshape(quarters, near, places, width))
    after_time, after_space, space_entry, space_packed, space_mixed = call(
        space_forward_kernel,
        (shape(tall, HIGH), shape(tall, HIGH), shape(tall), shape((rows, 3 * width)), shape(tall)),
        [pltpu.VMEM(tall, HIGH)],
        6 * token_flops,
        "space_forward",
    )(clips_in, by_frame, space_weight, vec)
    vec_shape = shape((ROWS_OF_VECTORS, width), HIGH)
    result, space_sum, feed_keep, feed_send, feed_vec = call(
        feed_kernel,
        (shape(clips_in.shape), shape(tall, HIGH), shape((width, hidden)), shape((width, hidden)), vec_shape),
        [pltpu.VMEM(tall, HIGH), pltpu.VMEM(tall, LOW), pltpu.VMEM(tall, LOW), pltpu.VMEM(tall, HIGH), pltpu.VMEM(tall, HIGH)],
        24 * token_flops,
        "feed",
    )(core, after_space, upstream_in, feed_weight, vec)
    feed_owned = scatter_sum(feed_keep, feed_send)
    time_sum, time_round, space_keep, space_send, space_vec = call(
        space_backward_kernel,
        (shape(tall, HIGH), shape(clips_in.shape), shape((width, 2 * width)), shape((width, 2 * width)), vec_shape),
        [pltpu.VMEM(tall, LOW), pltpu.VMEM(tall, LOW), pltpu.VMEM((rows, 3 * width), LOW)],
        12 * token_flops,
        "space_backward",
    )(core, space_sum, after_time, space_entry, space_packed, space_mixed, space_weight, vec)
    space_owned = scatter_sum(space_keep, space_send)
    time_half = time_pack.shape[1] // 2
    inward, time_keep, time_send = call(
        time_backward_kernel,
        (shape(tokens), shape((width, time_half)), shape((width, time_half))),
        [
            pltpu.VMEM(tiles, HIGH), pltpu.VMEM(tall, LOW), pltpu.VMEM(tall, LOW),
            pltpu.VMEM((rows, 3 * width), LOW), pltpu.VMEM((LANES, width), HIGH),
        ],
        14 * token_flops,
        "time_backward",
    )(
        core, regrouped(time_round).reshape(tokens), by_place, time_entry, time_packed, time_mixed,
        time_middle, time_weight, vec, space_vec, feed_vec,
    )
    entry_round = regrouped(inward.reshape(quarters, near, places, width))
    time_owned = scatter_sum(time_keep, time_send)

    time_sum = time_sum.reshape(near, quarters, pad, width)[:, :, :places]
    grad_clips = (time_sum + entry_round.swapaxes(0, 1).astype(HIGH)).astype(LOW).reshape(clips.shape)
    layer_output = result.swapaxes(0, 1).reshape(clips.shape)

    vector_grads = time_owned[:, 5 * width : 5 * width + VECTORS].T
    grad_expand = feed_owned[:, :hidden].reshape(share, blocks, count, share).swapaxes(1, 2).reshape(share, hidden)
    grad_reduce = jnp.concatenate(
        [feed_owned[:, hidden + k * width : hidden + (k + 1) * width] for k in range(blocks)], 0
    )
    return (
        layer_output,
        grad_clips,
        vector_grads[TIME_GAIN],
        vector_grads[TIME_SHIFT],
        time_owned[:, : 3 * width],
        time_owned[:, 3 * width : 4 * width],
        vector_grads[MERGE_BIAS],
        time_owned[:, 4 * width : 5 * width],
        vector_grads[MIXER_BIAS],
        vector_grads[SPACE_GAIN],
        vector_grads[SPACE_SHIFT],
        space_owned[:, : 3 * width],
        space_owned[:, 3 * width : 4 * width],
        vector_grads[SPACE_BIAS],
        vector_grads[FEED_GAIN],
        vector_grads[FEED_SHIFT],
        grad_expand,
        vector_grads[EXPAND_BIAS:].reshape(-1),
        grad_reduce,
        vector_grads[REDUCE_BIAS],
    )


def solution(mesh):
    clip, st = mesh.shape["clip"], mesh.shape["st"]
    finer = Mesh(mesh.devices.reshape(clip // 2, 2, st // 2, 2), ("z", "x", "y", "core"))
    token = P(("z", "x"), ("y", "core"), None, None)
    vec = P(("z", "x", "y", "core"))
    mat = P(("z", "x", "y", "core"), None)
    in_specs = (
        token, vec, vec, mat, mat, vec, mat, vec, vec, vec, mat, mat, vec, vec, vec, mat, vec, mat, vec, token,
    )
    out_specs = (
        token, token, vec, vec, mat, mat, vec, mat, vec, vec, vec, mat, mat, vec, vec, vec, mat, vec, mat, vec,
    )
    return jax.shard_map(body, mesh=finer, in_specs=in_specs, out_specs=out_specs, check_vma=False)
```

```python
import functools

import jax
import jax.numpy as jnp
from jax import lax
from jax.experimental import pallas as pl
from jax.experimental.pallas import tpu as pltpu
from jax.sharding import Mesh
from jax.sharding import PartitionSpec as P

HEADS = 12
HEAD_DIM = 64
LANES = 128
EPSILON = 1e-06
SCALE = 0.125
ROOT_HALF = 0.7071067811865476
DENSITY = 0.3989422804014327
LOW = jnp.bfloat16
HIGH = jnp.float32
TIME_BLOCK = 112
VMEM_BYTES = 24 * 1024 * 1024

TIME_GAIN, TIME_SHIFT, MERGE_BIAS, MIXER_BIAS = 0, 1, 2, 3
SPACE_GAIN, SPACE_SHIFT, SPACE_BIAS = 4, 5, 6
FEED_GAIN, FEED_SHIFT, REDUCE_BIAS, EXPAND_BIAS = 7, 8, 9, 10
VECTORS = 14
ROWS_OF_VECTORS = 16


def dot(left, right):
    return jnp.dot(left, right, preferred_element_type=HIGH)


def dot_nt(left, right):
    return lax.dot_general(left, right, (((1,), (1,)), ((), ())), preferred_element_type=HIGH)


def dot_tn(left, right):
    return lax.dot_general(left, right, (((0,), (0,)), ((), ())), preferred_element_type=HIGH)


def norm(values, gain, shift):
    centred = values - jnp.mean(values, -1, keepdims=True)
    inverse = lax.rsqrt(jnp.mean(centred * centred, -1, keepdims=True) + EPSILON)
    normed = centred * inverse
    return normed * gain + shift, normed, inverse


def norm_back(upstream, normed, inverse, gain):
    scaled = upstream * gain
    return inverse * (
        scaled
        - jnp.mean(scaled, -1, keepdims=True)
        - normed * jnp.mean(scaled * normed, -1, keepdims=True)
    )


def column_sum(values):
    return jnp.sum(values, 0, keepdims=True)


def stacked(pair):
    lane = lax.broadcasted_iota(jnp.int32, (1, LANES), 1)
    first = jnp.where(lane < HEAD_DIM, 1.0, 0.0).astype(LOW)
    second = jnp.where(lane < HEAD_DIM, 0.0, 1.0).astype(LOW)
    return jnp.concatenate([pair * first, pair * second], 0)


def joined(both):
    rows = both.shape[0] // 2
    lane = lax.broadcasted_iota(jnp.int32, (rows, LANES), 1)
    return jnp.where(lane < HEAD_DIM, both[:rows], both[rows:])


def shares_of(queries, key_rows, valid):
    scores = jnp.where(valid, dot_nt(queries, key_rows) * SCALE, -1e30)
    raised = jnp.exp(scores - jnp.max(scores, -1, keepdims=True))
    return raised * (1.0 / jnp.sum(raised, -1, keepdims=True))


def pair_forward(packed_ref, mixed_ref, rows, pair, width, valid):
    at = [pl.ds(pl.multiple_of(pair * LANES + part * width, LANES), LANES) for part in range(3)]
    queries = stacked(packed_ref[rows, at[0]])
    shares = shares_of(queries, packed_ref[rows, at[1]], valid)
    mixed = dot(shares.astype(LOW), packed_ref[rows, at[2]])
    mixed_ref[rows, at[0]] = joined(mixed).astype(LOW)


def pair_backward(packed_ref, up_ref, grad_ref, rows, pair, width, valid):
    at = [pl.ds(pl.multiple_of(pair * LANES + part * width, LANES), LANES) for part in range(3)]
    queries = stacked(packed_ref[rows, at[0]])
    key_rows = packed_ref[rows, at[1]]
    upstream = stacked(up_ref[rows, at[0]])
    shares = shares_of(queries, key_rows, valid)
    grad_shares = dot_nt(upstream, packed_ref[rows, at[2]])
    grad_scores = (
        shares * (grad_shares - jnp.sum(grad_shares * shares, -1, keepdims=True))
    ).astype(LOW)
    grad_ref[rows, at[0]] = (joined(dot(grad_scores, key_rows)) * SCALE).astype(LOW)
    grad_ref[rows, at[1]] = (dot_tn(grad_scores, queries) * SCALE).astype(LOW)
    grad_ref[rows, at[2]] = dot_tn(shares.astype(LOW), upstream).astype(LOW)


def time_valid(block, frames):
    row = lax.broadcasted_iota(jnp.int32, (2 * block, block), 0)
    col = lax.broadcasted_iota(jnp.int32, (2 * block, block), 1)
    return (row % block) // frames == col // frames


def space_valid(rows, pad, places):
    col = lax.broadcasted_iota(jnp.int32, (2 * rows, rows), 1)
    return col % pad < places


def vector(vec_ref, row):
    return vec_ref[row : row + 1, :]


def to_places(tokens_ref, tiles_ref):
    frames, places, width = tokens_ref.shape
    for frame in range(frames):
        rows = tokens_ref[frame].astype(HIGH)
        for tile in range(width // LANES):
            at = slice(tile * LANES, (tile + 1) * LANES)
            tiles_ref[tile, pl.ds(frame, places, stride=frames), :] = rows[:, at]
    return jnp.concatenate([tiles_ref[tile] for tile in range(width // LANES)], 1)


def from_places(values, tiles_ref, tokens_ref):
    frames, places, width = tokens_ref.shape
    for tile in range(width // LANES):
        tiles_ref[tile] = values[:, tile * LANES : (tile + 1) * LANES]
    for frame in range(frames):
        for tile in range(width // LANES):
            at = slice(tile * LANES, (tile + 1) * LANES)
            rows = tiles_ref[tile, pl.ds(frame, places, stride=frames), :]
            tokens_ref[frame, :, at] = rows.astype(LOW)


def to_frames(tokens_ref, held_ref):
    quarters, frames, places, _ = tokens_ref.shape
    for frame in range(frames):
        for quarter in range(quarters):
            start = (frame * quarters + quarter) * places
            held_ref[start : start + places, :] = tokens_ref[quarter, frame].astype(held_ref.dtype)


def from_frames(held_ref, tokens_ref):
    quarters, frames, places, _ = tokens_ref.shape
    for frame in range(frames):
        for quarter in range(quarters):
            start = (frame * quarters + quarter) * places
            tokens_ref[quarter, frame] = held_ref[start : start + places, :].astype(LOW)


def weight_copies(place_ref, pieces, weight_ref, sems, spans=None):
    if len(pieces) == 1:
        copies = []
        for number, (start, size) in enumerate(spans or ((0, weight_ref.shape[1]),)):
            to = sum(other for _, other in (spans or ())[:number])
            copies.append(
                pltpu.make_async_copy(
                    pieces[0].at[:, pl.ds(start, size)], weight_ref.at[:, pl.ds(to, size)], sems.at[number]
                )
            )
        return copies
    core, x, y = place_ref[0], place_ref[1], place_ref[2]
    quarter = pieces[0].shape[-1]
    copies = []
    for number, piece in enumerate(pieces):
        whose, side, far = number // 4, number // 2 % 2, number % 2
        half = core if whose == 0 else 1 - core
        start = pl.multiple_of(half * (2 * quarter) + side * quarter, LANES)
        for near in range(2):
            far_y, far_x = (far, near) if side == 0 else (near, far)
            at_x = 1 - x if far_x else x
            at_y = 1 - y if far_y else y
            copies.append(
                pltpu.make_async_copy(
                    piece.at[near],
                    weight_ref.at[:, at_x * 2 + at_y, :, pl.ds(start, quarter)],
                    sems.at[len(copies)],
                )
            )
    return copies


def columns_of(weight_ref, at):
    if len(weight_ref.shape) == 2:
        return weight_ref[:, at]
    value = weight_ref[:, :, :, at]
    return value.reshape(-1, value.shape[-1])


def put(core, half, keep_ref, send_ref, at, value):
    @pl.when(core == half)
    def _():
        keep_ref[:, at] = value

    @pl.when(core != half)
    def _():
        send_ref[:, at] = value


def time_forward_kernel(
    place_ref, tokens_ref, *refs
):
    *pieces, branch_ref, entry_ref, packed_ref, mixed_ref, middle_ref, vec_ref, tiles_ref, weight_ref, sems = refs
    frames, _, width = tokens_ref.shape
    rows = entry_ref.shape[0]
    block = TIME_BLOCK
    copies = weight_copies(place_ref, pieces, weight_ref, sems)
    for copy in copies:
        copy.start()
    tokens = to_places(tokens_ref, tiles_ref)
    for copy in copies:
        copy.wait()
    vec_at = slice(5 * width, 5 * width + LANES)
    vec_ref[...] = jnp.transpose(columns_of(weight_ref, vec_at).astype(HIGH))[:ROWS_OF_VECTORS]
    entry, _, _ = norm(tokens, vector(vec_ref, TIME_GAIN), vector(vec_ref, TIME_SHIFT))
    entry_ref[...] = entry.astype(LOW)
    for part in range(3):
        at = slice(part * width, (part + 1) * width)
        packed_ref[:, at] = dot(entry_ref[...], columns_of(weight_ref, at)).astype(LOW)
    valid = time_valid(block, frames)

    def step(pair, carry):
        for start in range(0, rows, block):
            pair_forward(packed_ref, mixed_ref, slice(start, start + block), pair, width, valid)
        return carry

    lax.fori_loop(0, HEADS // 2, step, 0)
    merge = columns_of(weight_ref, slice(3 * width, 4 * width))
    middle_ref[...] = (dot(mixed_ref[...], merge) + vector(vec_ref, MERGE_BIAS)).astype(LOW)
    mixer = columns_of(weight_ref, slice(4 * width, 5 * width))
    branch = dot(middle_ref[...], mixer) + vector(vec_ref, MIXER_BIAS)
    from_places(branch, tiles_ref, branch_ref)


def space_forward_kernel(all_places, place_ref, clips_ref, branch_ref, vec_ref, *refs):
    *pieces, after_time_ref, after_space_ref, entry_ref, packed_ref, mixed_ref, held_ref, weight_ref, sems = refs
    quarters, frames, pad, width = clips_ref.shape
    rows = held_ref.shape[0]
    copies = weight_copies(place_ref, pieces, weight_ref, sems)
    for copy in copies:
        copy.start()
    to_frames(clips_ref, after_time_ref)
    to_frames(branch_ref, held_ref)
    after_time = after_time_ref[...] + held_ref[...]
    after_time_ref[...] = after_time
    entry, _, _ = norm(after_time, vector(vec_ref, SPACE_GAIN), vector(vec_ref, SPACE_SHIFT))
    entry_ref[...] = entry.astype(LOW)
    for copy in copies:
        copy.wait()
    for part in range(3):
        at = slice(part * width, (part + 1) * width)
        packed_ref[:, at] = dot(entry_ref[...], columns_of(weight_ref, at)).astype(LOW)
    each = rows // frames
    valid = space_valid(each, pad, all_places // quarters)

    def step(pair, carry):
        for start in range(0, rows, each):
            pair_forward(packed_ref, mixed_ref, slice(start, start + each), pair, width, valid)
        return carry

    lax.fori_loop(0, HEADS // 2, step, 0)
    merge = columns_of(weight_ref, slice(3 * width, 4 * width))
    after_space_ref[...] = (
        after_time_ref[...] + dot(mixed_ref[...], merge) + vector(vec_ref, SPACE_BIAS)
    )


def feed_blocks(core, first, weight_ref, vec_ref, entry_ref, up_ref, out_ref, back_ref, keep_ref, send_ref, expand_vec_ref):
    width = entry_ref.shape[-1]
    half = keep_ref.shape[1]

    def step(block, carry):
        at = pl.ds(pl.multiple_of(block * width, LANES), width)
        expand = columns_of(weight_ref, at)
        reduce = columns_of(weight_ref, pl.ds(pl.multiple_of(half + block * width, LANES), width))
        hidden = dot(entry_ref[...], expand) + vec_ref[pl.ds(EXPAND_BIAS + first + block, 1), :]
        normal = 0.5 * (1.0 + lax.erf(hidden * ROOT_HALF))
        active = (hidden * normal).astype(LOW)
        out_ref[...] += dot(active, reduce)
        put(core, 1, keep_ref, send_ref, at, dot_tn(active, up_ref[...]).astype(LOW))
        slope = normal + hidden * DENSITY * jnp.exp(-0.5 * hidden * hidden)
        hidden_grad = (dot_nt(up_ref[...], reduce) * slope).astype(LOW)
        expand_vec_ref[pl.ds(block, 1), :] = column_sum(hidden_grad.astype(HIGH))
        put(core, 0, keep_ref, send_ref, at, dot_tn(entry_ref[...], hidden_grad).astype(LOW))
        back_ref[...] += dot_nt(hidden_grad, expand)
        return carry

    lax.fori_loop(0, half // width, step, 0)


def feed_spans(pieces, weight_ref, part):
    half = weight_ref.shape[1] // 2
    return ((part * half, half), (pieces[0].shape[1] // 2 + part * half, half))


def feed_first_kernel(place_ref, after_space_ref, upstream_ref, vec_ref, *refs):
    *pieces, entry_ref, up_ref, out_ref, back_ref, keep_ref, send_ref, expand_vec_ref, held_ref, weight_ref, sems = refs
    copies = weight_copies(place_ref, pieces, weight_ref, sems, feed_spans(pieces, weight_ref, 0))
    for copy in copies:
        copy.start()
    to_frames(upstream_ref, held_ref)
    up_ref[...] = held_ref[...].astype(LOW)
    entry, _, _ = norm(after_space_ref[...], vector(vec_ref, FEED_GAIN), vector(vec_ref, FEED_SHIFT))
    entry_ref[...] = entry.astype(LOW)
    out_ref[...] = after_space_ref[...] + vector(vec_ref, REDUCE_BIAS)
    back_ref[...] = jnp.zeros_like(back_ref)
    expand_vec_ref[...] = jnp.zeros_like(expand_vec_ref)
    for copy in copies:
        copy.wait()
    feed_blocks(
        place_ref[0], 0, weight_ref, vec_ref, entry_ref, up_ref, out_ref, back_ref, keep_ref, send_ref, expand_vec_ref
    )


def feed_second_kernel(
    blocks, place_ref, after_space_ref, vec_ref, entry_ref, up_ref, first_out_ref, first_back_ref, first_vec_ref, *refs
):
    *pieces, result_ref, space_sum_ref, keep_ref, send_ref, grad_vec_ref, out_ref, back_ref, expand_vec_ref, weight_ref, sems = refs
    copies = weight_copies(place_ref, pieces, weight_ref, sems, feed_spans(pieces, weight_ref, 1))
    for copy in copies:
        copy.start()
    out_ref[...] = first_out_ref[...]
    back_ref[...] = first_back_ref[...]
    for copy in copies:
        copy.wait()
    feed_blocks(
        place_ref[0], blocks, weight_ref, vec_ref, entry_ref, up_ref, out_ref, back_ref, keep_ref, send_ref, expand_vec_ref
    )
    from_frames(out_ref, result_ref)
    gain = vector(vec_ref, FEED_GAIN)
    _, normed, inverse = norm(after_space_ref[...], gain, vector(vec_ref, FEED_SHIFT))
    upstream = back_ref[...]
    held = up_ref[...].astype(HIGH)
    grad_vec_ref[...] = jnp.zeros_like(grad_vec_ref)
    grad_vec_ref[0:1, :] = column_sum(upstream * normed)
    grad_vec_ref[1:2, :] = column_sum(upstream)
    grad_vec_ref[2:3, :] = column_sum(held)
    for block in range(blocks):
        grad_vec_ref[3 + block : 4 + block, :] = first_vec_ref[block : block + 1, :]
        grad_vec_ref[3 + blocks + block : 4 + blocks + block, :] = expand_vec_ref[block : block + 1, :]
    space_sum_ref[...] = held + norm_back(upstream, normed, inverse, gain)


def space_backward_kernel(
    all_places, place_ref, space_sum_ref, after_time_ref, entry_ref, packed_ref, mixed_ref, vec_ref, *refs
):
    *pieces, time_sum_ref, time_round_ref, keep_ref, send_ref, grad_vec_ref, round_ref, up_ref, grad_ref, weight_ref, sems = refs
    rows, width = space_sum_ref.shape
    quarters, frames, pad, _ = time_round_ref.shape
    core = place_ref[0]
    half = keep_ref.shape[1]
    copies = weight_copies(place_ref, pieces, weight_ref, sems)
    for copy in copies:
        copy.start()
    round_ref[...] = space_sum_ref[...].astype(LOW)
    put(core, 1, keep_ref, send_ref, slice(half - width, half), dot_tn(mixed_ref[...], round_ref[...]).astype(LOW))
    for copy in copies:
        copy.wait()
    up_ref[...] = dot_nt(round_ref[...], columns_of(weight_ref, slice(3 * width, 4 * width))).astype(LOW)
    each = rows // frames
    valid = space_valid(each, pad, all_places // quarters)

    def step(pair, carry):
        for start in range(0, rows, each):
            pair_backward(packed_ref, up_ref, grad_ref, slice(start, start + each), pair, width, valid)
        return carry

    lax.fori_loop(0, HEADS // 2, step, 0)
    back = dot_nt(grad_ref[:, 0:width], columns_of(weight_ref, slice(0, width)))
    for part in range(3):
        at = slice(part * width, (part + 1) * width)
        if part:
            back += dot_nt(grad_ref[:, at], columns_of(weight_ref, at))
        value = dot_tn(entry_ref[...], grad_ref[:, at]).astype(LOW)
        start = part * width % half
        put(core, part * width // half, keep_ref, send_ref, slice(start, start + width), value)
    gain = vector(vec_ref, SPACE_GAIN)
    _, normed, inverse = norm(after_time_ref[...], gain, vector(vec_ref, SPACE_SHIFT))
    grad_vec_ref[...] = jnp.zeros_like(grad_vec_ref)
    grad_vec_ref[0:1, :] = column_sum(back * normed)
    grad_vec_ref[1:2, :] = column_sum(back)
    grad_vec_ref[2:3, :] = column_sum(round_ref[...].astype(HIGH))
    time_sum_ref[...] = space_sum_ref[...] + norm_back(back, normed, inverse, gain)
    from_frames(time_sum_ref, time_round_ref)


def time_mixer_backward_kernel(place_ref, time_round_ref, mixed_ref, middle_ref, *refs):
    *pieces, up_ref, keep_ref, send_ref, grad_vec_ref, tiles_ref, round_ref, weight_ref, sems = refs
    width = mixed_ref.shape[-1]
    core = place_ref[0]
    copies = weight_copies(place_ref, pieces, weight_ref, sems)
    for copy in copies:
        copy.start()
    rounded = to_places(time_round_ref, tiles_ref)
    round_ref[...] = rounded.astype(LOW)
    grad_vec_ref[...] = jnp.zeros_like(grad_vec_ref)
    grad_vec_ref[1:2, :] = column_sum(rounded)
    at = slice(0, width)
    put(core, 1, keep_ref, send_ref, at, dot_tn(middle_ref[...], round_ref[...]).astype(LOW))
    for copy in copies:
        copy.wait()
    up_ref[...] = dot_nt(round_ref[...], columns_of(weight_ref, slice(4 * width, 5 * width))).astype(LOW)
    grad_vec_ref[0:1, :] = column_sum(up_ref[...].astype(HIGH))
    put(core, 0, keep_ref, send_ref, at, dot_tn(mixed_ref[...], up_ref[...]).astype(LOW))
    up_ref[...] = dot_nt(up_ref[...], columns_of(weight_ref, slice(3 * width, 4 * width))).astype(LOW)


def time_heads_backward_kernel(
    place_ref, tokens_ref, entry_ref, packed_ref, up_ref, vec_ref, time_vec_ref, space_vec_ref, feed_vec_ref, *refs
):
    *pieces, inward_ref, keep_ref, send_ref, tiles_ref, grad_ref, vectors_ref, weight_ref, sems = refs
    frames, _, width = tokens_ref.shape
    rows = entry_ref.shape[0]
    block = TIME_BLOCK
    core = place_ref[0]
    half = keep_ref.shape[1]
    copies = weight_copies(place_ref, pieces, weight_ref, sems)
    for copy in copies:
        copy.start()
    valid = time_valid(block, frames)

    def step(pair, carry):
        for start in range(0, rows, block):
            pair_backward(packed_ref, up_ref, grad_ref, slice(start, start + block), pair, width, valid)
        return carry

    lax.fori_loop(0, HEADS // 2, step, 0)
    for start, stop in ((0, half), (half, 3 * width)):
        value = dot_tn(entry_ref[...], grad_ref[:, start:stop]).astype(LOW)
        put(core, start // half, keep_ref, send_ref, slice(0, stop - start), value)
    for copy in copies:
        copy.wait()
    back = dot_nt(grad_ref[:, 0:width], columns_of(weight_ref, slice(0, width)))
    for part in range(1, 3):
        at = slice(part * width, (part + 1) * width)
        back += dot_nt(grad_ref[:, at], columns_of(weight_ref, at))
    tokens = to_places(tokens_ref, tiles_ref)
    gain = vector(vec_ref, TIME_GAIN)
    _, normed, inverse = norm(tokens, gain, vector(vec_ref, TIME_SHIFT))
    vectors_ref[...] = jnp.zeros_like(vectors_ref)
    vectors_ref[TIME_GAIN : TIME_GAIN + 1, :] = column_sum(back * normed)
    vectors_ref[TIME_SHIFT : TIME_SHIFT + 1, :] = column_sum(back)
    for start, stop, source in (
        (MERGE_BIAS, SPACE_GAIN, time_vec_ref), (SPACE_GAIN, FEED_GAIN, space_vec_ref), (FEED_GAIN, VECTORS, feed_vec_ref)
    ):
        for row in range(start, stop):
            vectors_ref[row : row + 1, :] = source[row - start : row - start + 1, :]
    columns = jnp.transpose(vectors_ref[...]).astype(LOW)
    put(core, 1, keep_ref, send_ref, slice(half - 2 * LANES, half - LANES), columns)
    put(core, 1, keep_ref, send_ref, slice(half - LANES, half), jnp.zeros_like(columns))
    from_places(norm_back(back, normed, inverse, gain), tiles_ref, inward_ref)


def first_route_kernel(place_ref, *refs):
    *pairs, left_send, left_keep, right_send, right_keep = refs
    x, y = place_ref[1], place_ref[2]
    begin = 0
    for keep_ref, got_ref in zip(pairs[::2], pairs[1::2]):
        quarter = keep_ref.shape[-1] // 2
        left, right = slice(0, quarter), slice(quarter, 2 * quarter)
        to = slice(begin, begin + quarter)
        begin += quarter

        def total(at_x, at_y, columns):
            return added(keep_ref[0, at_x, at_y, :, columns], got_ref[0, at_x, at_y, :, columns])

        for other in range(2):
            left_send[0, other, :, to] = total(other, 1 - y, left)
            right_send[0, other, :, to] = total(1 - x, other, right)
            left_keep[0, other, :, to] = total(other, y, left)
            right_keep[0, other, :, to] = total(x, other, right)


def second_route_kernel(place_ref, *refs):
    *fours, left_send, left_keep, right_send, right_keep = refs
    x, y = place_ref[1], place_ref[2]
    begin = 0
    for at in range(0, len(fours), 4):
        left_ref, left_got, right_ref, right_got = fours[at : at + 4]
        to = slice(begin, begin + left_ref.shape[-1])
        begin = to.stop
        left_send[0, :, to] = added(left_ref[0, 1 - x], left_got[0, 1 - x])
        right_send[0, :, to] = added(right_ref[0, 1 - y], right_got[0, 1 - y])
        left_keep[0, :, to] = added(left_ref[0, x], left_got[0, x])
        right_keep[0, :, to] = added(right_ref[0, y], right_got[0, y])


def third_route_kernel(place_ref, left_ref, left_got, right_ref, right_got, *sends):
    quarter = left_ref.shape[-1]
    count = left_ref.shape[0]
    for distance, send in enumerate(sends):
        at = lax.rem(place_ref[3] + distance, count) if len(sends) > 1 else 0
        rows = at if len(sends) > 1 else slice(None)
        send[..., 0:quarter] = added(left_ref[rows], left_got[rows], send.dtype)
        send[..., quarter : 2 * quarter] = added(right_ref[rows], right_got[rows], send.dtype)


def last_kernel(place_ref, *refs):
    *parts, mine_ref, other_ref = refs
    total = sum(part[...].astype(HIGH) for part in parts)
    rows = mine_ref.shape[0]
    near, far = total[:rows], total[rows:]
    mine_ref[...] = jnp.where(place_ref[0] == 0, near, far)
    other_ref[...] = jnp.where(place_ref[0] == 0, far, near)


def owned_kernel(halves, spans, place_ref, mine_ref, other_ref, *refs):
    core = place_ref[0]
    half = sum(halves)
    outs, table_ref = refs[:-1], refs[-1]
    begin, wholes = 0, []
    for each in halves:
        quarters = [slice(at, at + each // 2) for at in (begin, half // 2 + begin)]
        begin += each // 2
        low = [jnp.where(core == 0, mine_ref[:, at], other_ref[:, at]) for at in quarters]
        high = [jnp.where(core == 0, other_ref[:, at], mine_ref[:, at]) for at in quarters]
        wholes.append(jnp.concatenate(low + high, 1))
    for (matrix, start, stop), out_ref in zip(spans, outs):
        value = wholes[matrix][:, start:stop]
        if out_ref.shape == value.shape:
            out_ref[...] = value
        else:
            table_ref[...] = jnp.zeros_like(table_ref)
            table_ref[0 : value.shape[0], :] = value
            out_ref[...] = jnp.transpose(table_ref[...])[: out_ref.shape[0], : out_ref.shape[1]]


def arranged_kernel(place_ref, *refs):
    *blocks, left_ref, right_ref = refs
    count, _, quarter = left_ref.shape
    for distance, block in enumerate(blocks):
        at = lax.rem(place_ref[3] + distance, count)
        left_ref[at] = block[:, 0:quarter]
        right_ref[at] = block[:, quarter : 2 * quarter]


def prepare_kernel(place_ref, heads_ref, merge_ref, mixer_ref, vectors_ref, space_heads_ref, space_merge_ref, *refs):
    time_mine, time_send, space_mine, space_send, table_ref = refs
    width = merge_ref.shape[1]
    rows, half = time_mine.shape
    table_ref[...] = jnp.zeros_like(table_ref)
    table_ref[0 : vectors_ref.shape[0], 0:rows] = vectors_ref[...].astype(HIGH)
    columns = jnp.transpose(table_ref[...])[0:rows].astype(LOW)

    def fill(low, high, space_low, space_high):
        low[...] = heads_ref[:, 0:half]
        rest = 3 * width - half
        high[:, 0:rest] = heads_ref[:, half:]
        high[:, rest : rest + width] = merge_ref[...]
        high[:, rest + width : rest + 2 * width] = mixer_ref[...]
        high[:, half - 2 * LANES : half - LANES] = columns
        high[:, half - LANES :] = jnp.zeros_like(columns)
        space_half = space_low.shape[1]
        space_low[...] = space_heads_ref[:, 0:space_half]
        space_high[:, 0 : 3 * width - space_half] = space_heads_ref[:, space_half:]
        space_high[:, 3 * width - space_half :] = space_merge_ref[...]

    @pl.when(place_ref[0] == 0)
    def _():
        fill(time_mine, time_send, space_mine, space_send)

    @pl.when(place_ref[0] != 0)
    def _():
        fill(time_send, time_mine, space_send, space_mine)


def call(kernel, outs, scratch, flops, name):
    in_vmem = pl.BlockSpec(memory_space=pltpu.VMEM)

    def run(place, blocks, pieces, columns=None):
        args = (place, *blocks, *pieces)
        moved = sum(a.size * a.dtype.itemsize for a in args)
        moved += sum(s.size * s.dtype.itemsize for s in outs)
        return pl.pallas_call(
            kernel,
            out_shape=outs,
            in_specs=[pl.BlockSpec(memory_space=pltpu.SMEM)]
            + [in_vmem] * len(blocks)
            + [pl.BlockSpec(memory_space=pltpu.HBM)] * len(pieces),
            out_specs=tuple(in_vmem for _ in outs),
            scratch_shapes=scratch + [weight_scratch(pieces, columns), pltpu.SemaphoreType.DMA((16,))],
            compiler_params=pltpu.CompilerParams(vmem_limit_bytes=VMEM_BYTES),
            cost_estimate=pl.CostEstimate(flops=flops, bytes_accessed=moved, transcendentals=0),
            name=name,
        )(*args)

    return run


def weight_scratch(pieces, columns):
    if len(pieces) == 1:
        return pltpu.VMEM((pieces[0].shape[0], columns or pieces[0].shape[1]), LOW)
    _, count, rows, quarter = pieces[0].shape
    return pltpu.VMEM((count, 4, rows, 4 * quarter), LOW)


def route(kernel, outs, name, place, blocks, whole=False, scratch=()):
    def spec(dims):
        if whole:
            return pl.BlockSpec(memory_space=pltpu.VMEM)
        return pl.BlockSpec((1,) + tuple(dims[1:]), lambda step: (step,) + (0,) * (len(dims) - 1))

    return pl.pallas_call(
        kernel,
        grid=() if whole else (blocks[0].shape[0],),
        out_shape=outs,
        in_specs=[pl.BlockSpec(memory_space=pltpu.SMEM)] + [spec(b.shape) for b in blocks],
        out_specs=tuple(spec(o.shape) for o in outs),
        scratch_shapes=scratch,
        compiler_params=pltpu.CompilerParams(vmem_limit_bytes=VMEM_BYTES),
        name=name,
    )(place, *blocks)


def shape(dims, dtype=LOW):
    return jax.ShapeDtypeStruct(dims, dtype)


SWAP = ((0, 1), (1, 0))


def swapped(value, axis):
    return lax.ppermute(value, axis, SWAP)


def added(left, right, dtype=LOW):
    return (left.astype(HIGH) + right.astype(HIGH)).astype(dtype)


def picked(value, index, axis):
    return lax.dynamic_index_in_dim(value, index, axis, keepdims=False)


def tied(value):
    return lax.optimization_barrier(value)


def synced(groups, *others):
    states, others = tied(([group.state for group in groups], others))
    for group, state in zip(groups, states):
        group.state = state
    return others if len(others) != 1 else others[0]


def shifted(value, distance):
    count = lax.axis_size("z")
    return lax.ppermute(value, "z", [(k, (k - distance) % count) for k in range(count)])


FEW = 4


class Sum:
    def __init__(self, place, keep, send, name):
        self.place, self.name = place, name
        self.count = lax.axis_size("z")
        self.rows = keep.shape[0] // (self.count * 4)
        self.halves = (keep.shape[1],)
        self.state = (keep, swapped(send, "core"))

    def joined(self, other):
        self.halves += other.halves
        self.state += other.state

    def first(self):
        part = shape((self.count, 2, self.rows, sum(self.halves) // 2))
        left, left_keep, right, right_keep = route(
            first_route_kernel, (part,) * 4, self.name + "_first", self.place,
            [value.reshape(self.count, 2, 2, self.rows, -1) for value in self.state],
        )
        self.state = (left_keep, swapped(left, "y"), right_keep, swapped(right, "x"))

    def second(self):
        self.half = sum(self.halves)
        part = shape((self.count, self.rows, self.half // 2))
        left, left_keep, right, right_keep = route(
            second_route_kernel, (part,) * 4, self.name + "_second", self.place, self.state
        )
        self.state = (left_keep, swapped(left, "x"), right_keep, swapped(right, "y"))

    def third(self):
        one = (self.rows, self.half)
        if self.count > FEW:
            outs = (shape((self.count, *one)),)
        else:
            outs = (shape(one, HIGH),) + (shape(one),) * (self.count - 1)
        mine, *sends = route(third_route_kernel, outs, self.name + "_third", self.place, self.state, True)
        if sends:
            self.state = (mine, *(shifted(send, -1 - k) for k, send in enumerate(sends)))
        else:
            arrived = lax.all_to_all(mine, "z", split_axis=0, concat_axis=0, tiled=True)
            self.state = (arrived.astype(HIGH).sum(0),)

    def last(self):
        part = shape((self.rows // 2, self.half), HIGH)
        mine, other = route(last_kernel, (part, part), self.name + "_last", self.place, self.state, True)
        self.state = (mine, swapped(other, "core"))

    def owned(self, spans):
        rows = self.rows // 2
        outs = tuple(
            shape((ROWS_OF_VECTORS, rows) if stop is None else (rows, stop - start), HIGH)
            for _, start, stop in spans
        )
        spans = tuple((which, start, start + LANES if stop is None else stop) for which, start, stop in spans)
        kernel = functools.partial(owned_kernel, self.halves, spans)
        table = [pltpu.VMEM((LANES, LANES), HIGH)]
        return route(kernel, outs, self.name + "_owned", self.place, self.state, True, table)


class Spread:
    def __init__(self, place, chip):
        self.place = place
        self.state = chip
        self.rows, self.half = chip.shape

    def first(self):
        count = lax.axis_size("z")
        if count > FEW:
            column = jnp.broadcast_to(self.state[None], (count, self.rows, self.half))
            self.state = lax.all_to_all(column, "z", split_axis=0, concat_axis=0, tiled=True)
        else:
            self.state = (self.state, *(shifted(self.state, k) for k in range(1, count)))

    def second(self):
        if isinstance(self.state, tuple):
            part = shape((len(self.state), self.rows, self.half // 2))
            left, right = route(arranged_kernel, (part, part), "arranged", self.place, self.state, True)
        else:
            left, right = self.state[..., : self.half // 2], self.state[..., self.half // 2 :]
        self.state = (left, swapped(left, "x"), right, swapped(right, "y"))

    def third(self):
        left, right = jnp.stack(self.state[:2]), jnp.stack(self.state[2:])
        own = (left, swapped(left, "y"), right, swapped(right, "x"))
        self.state = own + (swapped(left, "core"), swapped(right, "core"))

    def fourth(self):
        left, left_got, right, right_got, left_far, right_far = self.state
        far = (left_far, swapped(left_got, "core"), right_far, swapped(right_got, "core"))
        self.state = (left, left_got, right, right_got) + far

    def pieces(self):
        if self.rows % 16 == 0:
            return self.state
        core, x, y = lax.axis_index("core"), lax.axis_index("x"), lax.axis_index("y")

        def placed(near, far, side):
            piece = jnp.stack([near, far], side)
            piece = jnp.where(y == 0, piece, piece[::-1])
            return jnp.where(x == 0, piece, piece[:, ::-1])

        own, far = (
            jnp.concatenate(
                [placed(*self.state[k : k + 2], 0), placed(*self.state[k + 2 : k + 4], 1)], -1
            )
            for k in (0, 4)
        )
        whole = jnp.where(core == 0, jnp.concatenate([own, far], -1), jnp.concatenate([far, own], -1))
        return (whole.transpose(2, 1, 0, 3, 4).reshape(-1, 2 * self.half),)


def regrouped(tokens):
    return lax.all_to_all(tokens, ("y", "core"), split_axis=0, concat_axis=0, tiled=True)


def in_quarters(tokens, quarters, pad):
    _, frames, places, width = tokens.shape
    tokens = tokens.reshape(frames, quarters, places // quarters, width).swapaxes(0, 1)
    return jnp.pad(tokens, ((0, 0), (0, 0), (0, pad - places // quarters), (0, 0)))


def body(
    clips, time_gain, time_shift, time_heads, time_merge, merge_bias, time_mixer, mixer_bias,
    space_gain, space_shift, space_heads, space_merge, space_bias,
    feed_gain, feed_shift, feed_expand, expand_bias, feed_reduce, reduce_bias, cotangent,
):
    _, near, all_places, width = clips.shape
    quarters = lax.axis_size("y") * lax.axis_size("core")
    frames, places = near * quarters, all_places // quarters
    pad = -(-places // 8) * 8
    rows = frames * pad
    hidden = feed_expand.shape[1]
    blocks = hidden // width
    some = blocks // 2
    share = feed_expand.shape[0]
    count = width // share
    core = lax.axis_index("core")
    place = jnp.stack([core, *(lax.axis_index(axis) for axis in ("x", "y", "z"))]).astype(jnp.int32)

    tall, tokens = (rows, width), (frames, pad, width)
    tiles = (width // LANES, rows, LANES)
    token_flops = 2 * rows * width * width
    vec_shape = shape((ROWS_OF_VECTORS, width), HIGH)
    some_vec = shape((8, width), HIGH)
    space_half, feed_half = 2 * width, some * width
    heads_half = -(-(3 * width + LANES) // (4 * LANES)) * 2 * LANES

    vectors = jnp.concatenate(
        [
            jnp.stack(
                [
                    time_gain, time_shift, merge_bias, mixer_bias, space_gain, space_shift, space_bias,
                    feed_gain, feed_shift, reduce_bias,
                ]
            ),
            expand_bias.reshape(blocks, share),
        ],
        0,
    )
    time_half = 5 * width // 2 + LANES
    time_part, space_part = shape((share, time_half)), shape((share, space_half))
    time_mine, time_send, space_mine, space_send = route(
        prepare_kernel, (time_part, time_part, space_part, space_part), "prepare", place,
        (time_heads, time_merge, time_mixer, vectors, space_heads, space_merge), True,
        [pltpu.VMEM((LANES, LANES), HIGH)],
    )

    def spread(mine, send):
        got = swapped(send, "core")
        chip = jnp.where(core == 0, jnp.concatenate([mine, got], 0), jnp.concatenate([got, mine], 0))
        return Spread(place, chip)

    time = spread(time_mine, time_send)
    feed_expand, feed_reduce, clips_in = synced([time], feed_expand, feed_reduce, clips)
    time.first()
    space = spread(space_mine, space_send)
    expand = feed_expand.reshape(share, count, blocks, share).swapaxes(1, 2).reshape(share, hidden)
    feed_pack = jnp.concatenate([expand, *feed_reduce.reshape(blocks, share, width)], 1)
    clips_in = in_quarters(clips_in, quarters, pad)
    feed_pack, clips_in = synced([time, space], feed_pack, clips_in)
    feed = (lax.all_gather(feed_pack, ("z", "x", "y", "core"), axis=0, tiled=True),)
    time.second()
    space.first()
    synced([time, space])
    time.third()
    space.second()
    by_place = regrouped(clips_in).reshape(tokens)
    upstream_in = in_quarters(cotangent, quarters, pad)
    by_place, upstream_in = synced([time, space], by_place, upstream_in)
    time.fourth()
    space.third()
    branch, time_entry, time_packed, time_mixed, time_middle, vec = call(
        time_forward_kernel,
        (shape(tokens), shape(tall), shape((rows, 3 * width)), shape(tall), shape(tall), vec_shape),
        [pltpu.VMEM(tiles, HIGH)],
        6 * token_flops,
        "time_forward",
    )(place, (by_place,), time.pieces())
    branch = synced([space], branch)
    by_frame = regrouped(branch.reshape(clips_in.shape))
    space.fourth()
    after_time, after_space, space_entry, space_packed, space_mixed = call(
        functools.partial(space_forward_kernel, all_places),
        (shape(tall, HIGH), shape(tall, HIGH), shape(tall), shape((rows, 3 * width)), shape(tall)),
        [pltpu.VMEM(tall, HIGH)],
        6 * token_flops,
        "space_forward",
    )(place, (clips_in, by_frame, vec), space.pieces())
    feed_part = (shape((width, feed_half)), shape((width, feed_half)))
    entry, upstream, out, back, feed_keep, feed_send, first_vec = call(
        feed_first_kernel,
        (shape(tall), shape(tall), shape(tall, HIGH), shape(tall, HIGH), *feed_part, some_vec),
        [pltpu.VMEM(tall, HIGH)],
        12 * token_flops,
        "feed_first",
    )(place, (after_space, upstream_in, vec), feed, 2 * feed_half)
    feed_sum = Sum(place, feed_keep, feed_send, "feed")
    result, space_sum, more_keep, more_send, feed_vec = call(
        functools.partial(feed_second_kernel, some),
        (shape(clips_in.shape), shape(tall, HIGH), *feed_part, vec_shape),
        [pltpu.VMEM(tall, HIGH), pltpu.VMEM(tall, HIGH), pltpu.VMEM((8, width), HIGH)],
        12 * token_flops,
        "feed_second",
    )(place, (after_space, vec, entry, upstream, out, back, first_vec), feed, 2 * feed_half)
    space_sum, more_keep, more_send = synced([feed_sum], space_sum, more_keep, more_send)
    more_sum = Sum(place, more_keep, more_send, "more")
    feed_sum.first()
    more_sum.first()
    time_sum, time_round, space_keep, space_send, space_vec = call(
        functools.partial(space_backward_kernel, all_places),
        (shape(tall, HIGH), shape(clips_in.shape), shape((width, space_half)), shape((width, space_half)), vec_shape),
        [pltpu.VMEM(tall, LOW), pltpu.VMEM(tall, LOW), pltpu.VMEM((rows, 3 * width), LOW)],
        12 * token_flops,
        "space_backward",
    )(place, (space_sum, after_time, space_entry, space_packed, space_mixed, vec), space.pieces())
    time_round, space_keep, space_send = synced([feed_sum, more_sum], time_round, space_keep, space_send)
    time_round = regrouped(time_round)
    space_sums = Sum(place, space_keep, space_send, "space")
    feed_sum.joined(more_sum)
    feed_sum.second()
    mixed_grad, mixing_keep, mixing_send, time_vec = call(
        time_mixer_backward_kernel,
        (shape(tall), shape((width, width)), shape((width, width)), some_vec),
        [pltpu.VMEM(tiles, HIGH), pltpu.VMEM(tall, LOW)],
        4 * token_flops,
        "time_mixer_backward",
    )(place, (time_round.reshape(tokens), time_mixed, time_middle), time.pieces())
    mixed_grad, mixing_keep, mixing_send = synced([space_sums, feed_sum], mixed_grad, mixing_keep, mixing_send)
    space_sums.joined(Sum(place, mixing_keep, mixing_send, "mixing"))
    feed_sum.third()
    space_sums.first()
    inward, heads_keep, heads_send = call(
        time_heads_backward_kernel,
        (shape(tokens), shape((width, heads_half)), shape((width, heads_half))),
        [pltpu.VMEM(tiles, HIGH), pltpu.VMEM((rows, 3 * width), LOW), pltpu.VMEM((LANES, width), HIGH)],
        9 * token_flops,
        "time_heads_backward",
    )(
        place, (by_place, time_entry, time_packed, mixed_grad, vec, time_vec, space_vec, feed_vec), time.pieces()
    )
    inward, heads_keep, heads_send = synced([space_sums, feed_sum], inward, heads_keep, heads_send)
    heads_sum = Sum(place, heads_keep, heads_send, "heads")
    entry_round = regrouped(inward.reshape(clips_in.shape))
    synced([heads_sum])
    heads_sum.first()
    space_sums.second()
    feed_sum.last()
    entry_round = synced([heads_sum, feed_sum], entry_round)
    heads_sum.second()

    feed_grads = feed_sum.owned(
        [(k, 0, feed_half) for k in range(2)]
        + [(k, feed_half + j * width, feed_half + (j + 1) * width) for k in range(2) for j in range(some)]
    )
    grad_expand = jnp.concatenate(feed_grads[:2], 1)
    grad_expand = grad_expand.reshape(share, blocks, count, share).swapaxes(1, 2).reshape(share, hidden)
    grad_reduce = jnp.concatenate(feed_grads[2:], 0)
    time_sum = time_sum.reshape(near, quarters, pad, width)
    grad_clips = (time_sum + entry_round.swapaxes(0, 1).astype(HIGH)).astype(LOW)
    grad_clips = grad_clips[:, :, :places].reshape(clips.shape)
    layer_output = result[:, :, :places].swapaxes(0, 1).reshape(clips.shape)

    grad_expand, grad_reduce = synced([heads_sum, space_sums], grad_expand, grad_reduce)
    space_sums.third()
    heads_sum.third()
    layer_output, grad_clips = synced([heads_sum, space_sums], layer_output, grad_clips)
    heads_sum.last()
    space_sums.last()
    grad_space_heads, grad_space_merge, grad_time_merge, grad_time_mixer = space_sums.owned(
        [(0, 0, 3 * width), (0, 3 * width, 4 * width), (1, 0, width), (1, width, 2 * width)]
    )
    grad_time_heads, vector_grads = heads_sum.owned([(0, 0, 3 * width), (0, 2 * heads_half - 2 * LANES, None)])
    vector_grads = vector_grads[:VECTORS]
    return (
        layer_output,
        grad_clips,
        vector_grads[TIME_GAIN],
        vector_grads[TIME_SHIFT],
        grad_time_heads,
        grad_time_merge,
        vector_grads[MERGE_BIAS],
        grad_time_mixer,
        vector_grads[MIXER_BIAS],
        vector_grads[SPACE_GAIN],
        vector_grads[SPACE_SHIFT],
        grad_space_heads,
        grad_space_merge,
        vector_grads[SPACE_BIAS],
        vector_grads[FEED_GAIN],
        vector_grads[FEED_SHIFT],
        grad_expand,
        vector_grads[EXPAND_BIAS:].reshape(-1),
        grad_reduce,
        vector_grads[REDUCE_BIAS],
    )


def solution(mesh):
    clip, st = mesh.shape["clip"], mesh.shape["st"]
    finer = Mesh(mesh.devices.reshape(clip // 2, 2, st // 2, 2), ("z", "x", "y", "core"))
    token = P(("z", "x"), ("y", "core"), None, None)
    vec = P(("z", "x", "y", "core"))
    mat = P(("z", "x", "y", "core"), None)
    in_specs = (
        token, vec, vec, mat, mat, vec, mat, vec, vec, vec, mat, mat, vec, vec, vec, mat, vec, mat, vec, token,
    )
    out_specs = (
        token, token, vec, vec, mat, mat, vec, mat, vec, vec, vec, mat, mat, vec, vec, vec, mat, vec, mat, vec,
    )
    return jax.shard_map(body, mesh=finer, in_specs=in_specs, out_specs=out_specs, check_vma=False)
```

```python
import functools

import jax
import jax.numpy as jnp
from jax import lax
from jax.experimental import pallas as pl
from jax.experimental.pallas import tpu as pltpu
from jax.sharding import Mesh
from jax.sharding import PartitionSpec as P

HEADS = 12
HEAD_DIM = 64
LANES = 128
EPSILON = 1e-06
SCALE = 0.125
ROOT_HALF = 0.7071067811865476
DENSITY = 0.3989422804014327
LOW = jnp.bfloat16
HIGH = jnp.float32
TIME_BLOCK = 112
VMEM_BYTES = 32 * 1024 * 1024

TIME_GAIN, TIME_SHIFT, MERGE_BIAS, MIXER_BIAS = 0, 1, 2, 3
SPACE_GAIN, SPACE_SHIFT, SPACE_BIAS = 4, 5, 6
FEED_GAIN, FEED_SHIFT, REDUCE_BIAS, EXPAND_BIAS = 7, 8, 9, 10
VECTORS = 14
ROWS_OF_VECTORS = 16


def dot(left, right):
    return jnp.dot(left, right, preferred_element_type=HIGH)


def dot_nt(left, right):
    return lax.dot_general(left, right, (((1,), (1,)), ((), ())), preferred_element_type=HIGH)


def dot_tn(left, right):
    return lax.dot_general(left, right, (((0,), (0,)), ((), ())), preferred_element_type=HIGH)


def norm(values, gain, shift):
    centred = values - jnp.mean(values, -1, keepdims=True)
    inverse = lax.rsqrt(jnp.mean(centred * centred, -1, keepdims=True) + EPSILON)
    normed = centred * inverse
    return normed * gain + shift, normed, inverse


def norm_back(upstream, normed, inverse, gain):
    scaled = upstream * gain
    return inverse * (
        scaled
        - jnp.mean(scaled, -1, keepdims=True)
        - normed * jnp.mean(scaled * normed, -1, keepdims=True)
    )


def column_sum(values):
    return jnp.sum(values, 0, keepdims=True)


class Mover:
    def __init__(self, sems):
        self.sems, self.used = sems, 0

    def start(self, source, target):
        copy = pltpu.make_async_copy(source, target, self.sems.at[self.used])
        self.used += 1
        copy.start()
        return copy


def finished(copies):
    for copy in copies:
        copy.wait()


def stacked(pair):
    lane = lax.broadcasted_iota(jnp.int32, (1, LANES), 1)
    first = jnp.where(lane < HEAD_DIM, 1.0, 0.0).astype(LOW)
    second = jnp.where(lane < HEAD_DIM, 0.0, 1.0).astype(LOW)
    return jnp.concatenate([pair * first, pair * second], 0)


def joined(both):
    rows = both.shape[0] // 2
    lane = lax.broadcasted_iota(jnp.int32, (rows, LANES), 1)
    return jnp.where(lane < HEAD_DIM, both[:rows], both[rows:])


def shares_of(queries, key_rows, valid):
    scores = jnp.where(valid, dot_nt(queries, key_rows) * SCALE, -1e30)
    raised = jnp.exp(scores - jnp.max(scores, -1, keepdims=True))
    return raised * (1.0 / jnp.sum(raised, -1, keepdims=True))


def pair_forward(packed_ref, mixed_ref, rows, pair, width, valid):
    at = [pl.ds(pl.multiple_of(pair * LANES + part * width, LANES), LANES) for part in range(3)]
    queries = stacked(packed_ref[rows, at[0]])
    shares = shares_of(queries, packed_ref[rows, at[1]], valid)
    mixed = dot(shares.astype(LOW), packed_ref[rows, at[2]])
    mixed_ref[rows, at[0]] = joined(mixed).astype(LOW)


def pair_backward(packed_ref, up_ref, grad_ref, rows, pair, width, valid):
    at = [pl.ds(pl.multiple_of(pair * LANES + part * width, LANES), LANES) for part in range(3)]
    queries = stacked(packed_ref[rows, at[0]])
    key_rows = packed_ref[rows, at[1]]
    upstream = stacked(up_ref[rows, at[0]])
    shares = shares_of(queries, key_rows, valid)
    grad_shares = dot_nt(upstream, packed_ref[rows, at[2]])
    grad_scores = (
        shares * (grad_shares - jnp.sum(grad_shares * shares, -1, keepdims=True))
    ).astype(LOW)
    grad_ref[rows, at[0]] = (joined(dot(grad_scores, key_rows)) * SCALE).astype(LOW)
    grad_ref[rows, at[1]] = (dot_tn(grad_scores, queries) * SCALE).astype(LOW)
    grad_ref[rows, at[2]] = dot_tn(shares.astype(LOW), upstream).astype(LOW)


def time_valid(block, frames):
    row = lax.broadcasted_iota(jnp.int32, (2 * block, block), 0)
    col = lax.broadcasted_iota(jnp.int32, (2 * block, block), 1)
    return (row % block) // frames == col // frames


def space_valid(rows, pad, places):
    col = lax.broadcasted_iota(jnp.int32, (2 * rows, rows), 1)
    return col % pad < places


def vector(vec_ref, row):
    return vec_ref[row : row + 1, :]


def to_places(tokens_ref, tiles_ref):
    frames, places, width = tokens_ref.shape
    for frame in range(frames):
        rows = tokens_ref[frame].astype(HIGH)
        for tile in range(width // LANES):
            at = slice(tile * LANES, (tile + 1) * LANES)
            tiles_ref[tile, pl.ds(frame, places, stride=frames), :] = rows[:, at]
    return jnp.concatenate([tiles_ref[tile] for tile in range(width // LANES)], 1)


def from_places(values, tiles_ref, tokens_ref):
    frames, places, width = tokens_ref.shape
    for tile in range(width // LANES):
        tiles_ref[tile] = values[:, tile * LANES : (tile + 1) * LANES]
    for frame in range(frames):
        for tile in range(width // LANES):
            at = slice(tile * LANES, (tile + 1) * LANES)
            rows = tiles_ref[tile, pl.ds(frame, places, stride=frames), :]
            tokens_ref[frame, :, at] = rows.astype(LOW)


def to_frames(tokens_ref, held_ref):
    quarters, frames, places, _ = tokens_ref.shape
    for frame in range(frames):
        for quarter in range(quarters):
            start = (frame * quarters + quarter) * places
            held_ref[start : start + places, :] = tokens_ref[quarter, frame].astype(held_ref.dtype)


def from_frames(held_ref, tokens_ref):
    quarters, frames, places, _ = tokens_ref.shape
    for frame in range(frames):
        for quarter in range(quarters):
            start = (frame * quarters + quarter) * places
            tokens_ref[quarter, frame] = held_ref[start : start + places, :].astype(LOW)


def weight_copies(place_ref, pieces, weight_ref, mover):
    if len(pieces) == 1:
        return [mover.start(pieces[0], weight_ref)]
    core, x, y = place_ref[0], place_ref[1], place_ref[2]
    quarter = pieces[0].shape[-1]
    copies = []
    for number, piece in enumerate(pieces):
        whose, side, far = number // 4, number // 2 % 2, number % 2
        half = core if whose == 0 else 1 - core
        start = pl.multiple_of(half * (2 * quarter) + side * quarter, LANES)
        for near in range(2):
            far_y, far_x = (far, near) if side == 0 else (near, far)
            at_x = 1 - x if far_x else x
            at_y = 1 - y if far_y else y
            target = weight_ref.at[:, at_x * 2 + at_y, :, pl.ds(start, quarter)]
            copies.append(mover.start(piece.at[near], target))
    return copies


def columns_of(weight_ref, at):
    if len(weight_ref.shape) == 2:
        return weight_ref[:, at]
    value = weight_ref[:, :, :, at]
    return value.reshape(-1, value.shape[-1])


def put(core, half, keep_ref, send_ref, at, value):
    @pl.when(core == half)
    def _():
        keep_ref[:, at] = value

    @pl.when(core != half)
    def _():
        send_ref[:, at] = value


def time_forward_kernel(place_ref, tokens_ref, *refs):
    *pieces, branch_ref, vec_ref = refs[:-11]
    *kept, tiles_ref, entry_ref, packed_ref, mixed_ref, middle_ref, weight_ref, sems = refs[-11:]
    frames, _, width = tokens_ref.shape
    rows = entry_ref.shape[0]
    mover = Mover(sems)
    copies = weight_copies(place_ref, pieces, weight_ref, mover)
    tokens = to_places(tokens_ref, tiles_ref)
    finished(copies)
    vec_at = slice(5 * width, 5 * width + LANES)
    vec_ref[...] = jnp.transpose(columns_of(weight_ref, vec_at).astype(HIGH))[:ROWS_OF_VECTORS]
    entry, _, _ = norm(tokens, vector(vec_ref, TIME_GAIN), vector(vec_ref, TIME_SHIFT))
    entry_ref[...] = entry.astype(LOW)
    stores = [mover.start(entry_ref, kept[0])]
    for part in range(3):
        at = slice(part * width, (part + 1) * width)
        packed_ref[:, at] = dot(entry_ref[...], columns_of(weight_ref, at)).astype(LOW)
    stores.append(mover.start(packed_ref, kept[1]))
    valid = time_valid(TIME_BLOCK, frames)

    def step(pair, carry):
        for start in range(0, rows, TIME_BLOCK):
            pair_forward(packed_ref, mixed_ref, slice(start, start + TIME_BLOCK), pair, width, valid)
        return carry

    lax.fori_loop(0, HEADS // 2, step, 0)
    stores.append(mover.start(mixed_ref, kept[2]))
    merge = columns_of(weight_ref, slice(3 * width, 4 * width))
    middle_ref[...] = (dot(mixed_ref[...], merge) + vector(vec_ref, MERGE_BIAS)).astype(LOW)
    stores.append(mover.start(middle_ref, kept[3]))
    mixer = columns_of(weight_ref, slice(4 * width, 5 * width))
    branch = dot(middle_ref[...], mixer) + vector(vec_ref, MIXER_BIAS)
    from_places(branch, tiles_ref, branch_ref)
    finished(stores)


def space_forward_kernel(all_places, place_ref, clips_ref, branch_ref, vec_ref, *refs):
    *pieces, after_space_ref = refs[:-11]
    *kept, held_ref, after_time_ref, entry_ref, packed_ref, mixed_ref, weight_ref, sems = refs[-11:]
    quarters, frames, pad, width = clips_ref.shape
    rows = held_ref.shape[0]
    mover = Mover(sems)
    copies = weight_copies(place_ref, pieces, weight_ref, mover)
    to_frames(clips_ref, after_time_ref)
    to_frames(branch_ref, held_ref)
    after_time = after_time_ref[...] + held_ref[...]
    after_time_ref[...] = after_time
    stores = [mover.start(after_time_ref, kept[0])]
    entry, _, _ = norm(after_time, vector(vec_ref, SPACE_GAIN), vector(vec_ref, SPACE_SHIFT))
    entry_ref[...] = entry.astype(LOW)
    stores.append(mover.start(entry_ref, kept[1]))
    finished(copies)
    for part in range(3):
        at = slice(part * width, (part + 1) * width)
        packed_ref[:, at] = dot(entry_ref[...], columns_of(weight_ref, at)).astype(LOW)
    stores.append(mover.start(packed_ref, kept[2]))
    each = rows // frames
    valid = space_valid(each, pad, all_places // quarters)

    def step(pair, carry):
        for start in range(0, rows, each):
            pair_forward(packed_ref, mixed_ref, slice(start, start + each), pair, width, valid)
        return carry

    lax.fori_loop(0, HEADS // 2, step, 0)
    stores.append(mover.start(mixed_ref, kept[3]))
    merge = columns_of(weight_ref, slice(3 * width, 4 * width))
    after_space_ref[...] = (
        after_time_ref[...] + dot(mixed_ref[...], merge) + vector(vec_ref, SPACE_BIAS)
    )
    finished(stores)


def feed_kernel(
    place_ref, after_space_ref, upstream_ref, vec_ref, weight_ref,
    space_sum_ref, grad_vec_ref, result_ref, grad_ref,
    held_ref, up_ref, entry_ref, out_ref, back_ref, results_ref, weights_ref, grads_ref, sems,
):
    width = after_space_ref.shape[-1]
    half = weight_ref.shape[1] // 2
    blocks = half // width
    mover = Mover(sems)

    def columns(side, block):
        return pl.ds(side * half + block * width, width)

    def load(block):
        return [
            mover.start(weight_ref.at[:, columns(side, block)], weights_ref.at[block, side]) for side in range(2)
        ]

    loads = [load(block) for block in range(blocks)]
    to_frames(upstream_ref, held_ref)
    up_ref[...] = held_ref[...].astype(LOW)
    gain, shift = vector(vec_ref, FEED_GAIN), vector(vec_ref, FEED_SHIFT)
    entry, _, _ = norm(after_space_ref[...], gain, shift)
    entry_ref[...] = entry.astype(LOW)
    grad_vec_ref[...] = jnp.zeros_like(grad_vec_ref)
    stores = []
    for block in range(blocks):
        finished(loads[block])
        expand, reduce = weights_ref[block, 0], weights_ref[block, 1]
        hidden = dot(entry_ref[...], expand) + vector(vec_ref, EXPAND_BIAS + block)
        normal = 0.5 * (1.0 + lax.erf(hidden * ROOT_HALF))
        active = (hidden * normal).astype(LOW)
        out = dot(active, reduce)
        slope = normal + hidden * DENSITY * jnp.exp(-0.5 * hidden * hidden)
        hidden_grad = (dot_nt(up_ref[...], reduce) * slope).astype(LOW)
        back = dot_nt(hidden_grad, expand)
        if block:
            out_ref[...] += out
            back_ref[...] += back
        else:
            out_ref[...] = after_space_ref[...] + vector(vec_ref, REDUCE_BIAS) + out
            back_ref[...] = back
        grad_vec_ref[3 + block : 4 + block, :] = column_sum(hidden_grad.astype(HIGH))
        if block > 1:
            finished(stores[2 * block - 4 : 2 * block - 2])
        grads_ref[block % 2, 0] = dot_tn(entry_ref[...], hidden_grad).astype(LOW)
        grads_ref[block % 2, 1] = dot_tn(active, up_ref[...]).astype(LOW)
        for side in range(2):
            stores.append(mover.start(grads_ref.at[block % 2, side], grad_ref.at[:, columns(side, block)]))
    from_frames(out_ref, results_ref)
    stores.append(mover.start(results_ref, result_ref))
    _, normed, inverse = norm(after_space_ref[...], gain, shift)
    upstream = back_ref[...]
    grad_vec_ref[0:1, :] = column_sum(upstream * normed)
    grad_vec_ref[1:2, :] = column_sum(upstream)
    grad_vec_ref[2:3, :] = column_sum(held_ref[...])
    space_sum_ref[...] = held_ref[...] + norm_back(upstream, normed, inverse, gain)
    finished(stores[2 * blocks - 4 :])


def space_backward_kernel(all_places, place_ref, space_sum_ref, vec_ref, *refs):
    *kept, time_round_ref, keep_ref, send_ref, grad_vec_ref, time_sum_ref = refs[:-10]
    kept, pieces = kept[:4], kept[4:]
    *held, sum_ref, round_ref, up_ref, grad_ref, weight_ref, sems = refs[-10:]
    after_time_ref, entry_ref, packed_ref, mixed_ref = held
    rows, width = space_sum_ref.shape
    quarters, frames, pad, _ = time_round_ref.shape
    core = place_ref[0]
    half = keep_ref.shape[1]
    mover = Mover(sems)
    mixed_copy = mover.start(kept[3], mixed_ref)
    copies = weight_copies(place_ref, pieces, weight_ref, mover)
    packed_copy = mover.start(kept[2], packed_ref)
    others = [mover.start(kept[1], entry_ref), mover.start(kept[0], after_time_ref)]
    round_ref[...] = space_sum_ref[...].astype(LOW)
    mixed_copy.wait()
    put(core, 1, keep_ref, send_ref, slice(half - width, half), dot_tn(mixed_ref[...], round_ref[...]).astype(LOW))
    finished(copies)
    up_ref[...] = dot_nt(round_ref[...], columns_of(weight_ref, slice(3 * width, 4 * width))).astype(LOW)
    each = rows // frames
    valid = space_valid(each, pad, all_places // quarters)
    packed_copy.wait()

    def step(pair, carry):
        for start in range(0, rows, each):
            pair_backward(packed_ref, up_ref, grad_ref, slice(start, start + each), pair, width, valid)
        return carry

    lax.fori_loop(0, HEADS // 2, step, 0)
    finished(others)
    back = dot_nt(grad_ref[:, 0:width], columns_of(weight_ref, slice(0, width)))
    for part in range(1, 3):
        at = slice(part * width, (part + 1) * width)
        back += dot_nt(grad_ref[:, at], columns_of(weight_ref, at))
    gain = vector(vec_ref, SPACE_GAIN)
    _, normed, inverse = norm(after_time_ref[...], gain, vector(vec_ref, SPACE_SHIFT))
    sum_ref[...] = space_sum_ref[...] + norm_back(back, normed, inverse, gain)
    store = mover.start(sum_ref, time_sum_ref)
    from_frames(sum_ref, time_round_ref)
    grad_vec_ref[...] = jnp.zeros_like(grad_vec_ref)
    grad_vec_ref[0:1, :] = column_sum(back * normed)
    grad_vec_ref[1:2, :] = column_sum(back)
    grad_vec_ref[2:3, :] = column_sum(round_ref[...].astype(HIGH))
    for part in range(3):
        at = slice(part * width, (part + 1) * width)
        value = dot_tn(entry_ref[...], grad_ref[:, at]).astype(LOW)
        start = part * width % half
        put(core, part * width // half, keep_ref, send_ref, slice(start, start + width), value)
    store.wait()


def time_backward_kernel(place_ref, time_round_ref, vec_ref, space_vec_ref, feed_vec_ref, *refs):
    *kept, inward_ref, keep_ref, send_ref = refs[:-12]
    kept, pieces = kept[:5], kept[5:]
    *held, tiles_ref, round_ref, up_ref, grad_ref, vectors_ref, weight_ref, sems = refs[-12:]
    tokens_ref, entry_ref, packed_ref, mixed_ref, middle_ref = held
    frames, _, width = time_round_ref.shape
    rows = entry_ref.shape[0]
    core = place_ref[0]
    half = keep_ref.shape[1]
    mover = Mover(sems)
    middle_copy = mover.start(kept[4], middle_ref)
    copies = weight_copies(place_ref, pieces, weight_ref, mover)
    mixed_copy, packed_copy = mover.start(kept[3], mixed_ref), mover.start(kept[2], packed_ref)
    others = [mover.start(kept[1], entry_ref), mover.start(kept[0], tokens_ref)]
    rounded = to_places(time_round_ref, tiles_ref)
    round_ref[...] = rounded.astype(LOW)
    vectors_ref[...] = jnp.zeros_like(vectors_ref)
    vectors_ref[MIXER_BIAS : MIXER_BIAS + 1, :] = column_sum(rounded)
    tail = 3 * width - half
    at = slice(tail + width, tail + 2 * width)
    middle_copy.wait()
    put(core, 1, keep_ref, send_ref, at, dot_tn(middle_ref[...], round_ref[...]).astype(LOW))
    finished(copies)
    up_ref[...] = dot_nt(round_ref[...], columns_of(weight_ref, slice(4 * width, 5 * width))).astype(LOW)
    vectors_ref[MERGE_BIAS : MERGE_BIAS + 1, :] = column_sum(up_ref[...].astype(HIGH))
    at = slice(tail, tail + width)
    mixed_copy.wait()
    put(core, 1, keep_ref, send_ref, at, dot_tn(mixed_ref[...], up_ref[...]).astype(LOW))
    up_ref[...] = dot_nt(up_ref[...], columns_of(weight_ref, slice(3 * width, 4 * width))).astype(LOW)
    valid = time_valid(TIME_BLOCK, frames)
    packed_copy.wait()

    def step(pair, carry):
        for start in range(0, rows, TIME_BLOCK):
            pair_backward(packed_ref, up_ref, grad_ref, slice(start, start + TIME_BLOCK), pair, width, valid)
        return carry

    lax.fori_loop(0, HEADS // 2, step, 0)
    finished(others)
    for start, stop in ((0, half), (half, 3 * width)):
        value = dot_tn(entry_ref[...], grad_ref[:, start:stop]).astype(LOW)
        put(core, start // half, keep_ref, send_ref, slice(0, stop - start), value)
    back = dot_nt(grad_ref[:, 0:width], columns_of(weight_ref, slice(0, width)))
    for part in range(1, 3):
        at = slice(part * width, (part + 1) * width)
        back += dot_nt(grad_ref[:, at], columns_of(weight_ref, at))
    tokens = to_places(tokens_ref, tiles_ref)
    gain = vector(vec_ref, TIME_GAIN)
    _, normed, inverse = norm(tokens, gain, vector(vec_ref, TIME_SHIFT))
    vectors_ref[TIME_GAIN : TIME_GAIN + 1, :] = column_sum(back * normed)
    vectors_ref[TIME_SHIFT : TIME_SHIFT + 1, :] = column_sum(back)
    for start, stop, source in ((SPACE_GAIN, FEED_GAIN, space_vec_ref), (FEED_GAIN, VECTORS, feed_vec_ref)):
        for row in range(start, stop):
            vectors_ref[row : row + 1, :] = source[row - start : row - start + 1, :]
    columns = jnp.transpose(vectors_ref[...]).astype(LOW)
    put(core, 1, keep_ref, send_ref, slice(half - 2 * LANES, half - LANES), columns)
    put(core, 1, keep_ref, send_ref, slice(half - LANES, half), jnp.zeros_like(columns))
    from_places(norm_back(back, normed, inverse, gain), tiles_ref, inward_ref)


def first_route_kernel(place_ref, *refs):
    *pairs, left_send, left_keep, right_send, right_keep = refs
    x, y = place_ref[1], place_ref[2]
    begin = 0
    for keep_ref, got_ref in zip(pairs[::2], pairs[1::2]):
        quarter = keep_ref.shape[-1] // 2
        left, right = slice(0, quarter), slice(quarter, 2 * quarter)
        to = slice(begin, begin + quarter)
        begin += quarter

        def total(at_x, at_y, columns):
            return added(keep_ref[0, at_x, at_y, :, columns], got_ref[0, at_x, at_y, :, columns])

        for other in range(2):
            left_send[0, other, :, to] = total(other, 1 - y, left)
            right_send[0, other, :, to] = total(1 - x, other, right)
            left_keep[0, other, :, to] = total(other, y, left)
            right_keep[0, other, :, to] = total(x, other, right)


def second_route_kernel(place_ref, *refs):
    *fours, left_send, left_keep, right_send, right_keep = refs
    x, y = place_ref[1], place_ref[2]
    begin = 0
    for at in range(0, len(fours), 4):
        left_ref, left_got, right_ref, right_got = fours[at : at + 4]
        to = slice(begin, begin + left_ref.shape[-1])
        begin = to.stop
        left_send[0, :, to] = added(left_ref[0, 1 - x], left_got[0, 1 - x])
        right_send[0, :, to] = added(right_ref[0, 1 - y], right_got[0, 1 - y])
        left_keep[0, :, to] = added(left_ref[0, x], left_got[0, x])
        right_keep[0, :, to] = added(right_ref[0, y], right_got[0, y])


def third_route_kernel(place_ref, left_ref, left_got, right_ref, right_got, *sends):
    quarter = left_ref.shape[-1]
    count = left_ref.shape[0]
    for distance, send in enumerate(sends):
        at = lax.rem(place_ref[3] + distance, count) if len(sends) > 1 else 0
        rows = at if len(sends) > 1 else slice(None)
        send[..., 0:quarter] = added(left_ref[rows], left_got[rows], send.dtype)
        send[..., quarter : 2 * quarter] = added(right_ref[rows], right_got[rows], send.dtype)


def last_kernel(place_ref, *refs):
    *parts, mine_ref, other_ref = refs
    total = sum(part[...].astype(HIGH) for part in parts)
    rows = mine_ref.shape[0]
    near, far = total[:rows], total[rows:]
    mine_ref[...] = jnp.where(place_ref[0] == 0, near, far)
    other_ref[...] = jnp.where(place_ref[0] == 0, far, near)


def owned_kernel(halves, spans, place_ref, mine_ref, other_ref, *refs):
    core = place_ref[0]
    half = sum(halves)
    outs, table_ref = refs[:-1], refs[-1]
    begin, wholes = 0, []
    for each in halves:
        quarters = [slice(at, at + each // 2) for at in (begin, half // 2 + begin)]
        begin += each // 2
        low = [jnp.where(core == 0, mine_ref[:, at], other_ref[:, at]) for at in quarters]
        high = [jnp.where(core == 0, other_ref[:, at], mine_ref[:, at]) for at in quarters]
        wholes.append(jnp.concatenate(low + high, 1))
    for (matrix, start, stop), out_ref in zip(spans, outs):
        value = wholes[matrix][:, start:stop]
        if out_ref.shape == value.shape:
            out_ref[...] = value
        else:
            table_ref[...] = jnp.zeros_like(table_ref)
            table_ref[0 : value.shape[0], :] = value
            out_ref[...] = jnp.transpose(table_ref[...])[: out_ref.shape[0], : out_ref.shape[1]]


def arranged_kernel(place_ref, *refs):
    *blocks, left_ref, right_ref = refs
    count, _, quarter = left_ref.shape
    for distance, block in enumerate(blocks):
        at = lax.rem(place_ref[3] + distance, count)
        left_ref[at] = block[:, 0:quarter]
        right_ref[at] = block[:, quarter : 2 * quarter]


def prepare_kernel(place_ref, vectors_ref, *refs):
    *sources, time_mine, time_send, space_mine, space_send = refs[:-7]
    *held, table_ref, sems = refs[-7:]
    heads_ref, merge_ref, mixer_ref, space_heads_ref, space_merge_ref = held
    mover = Mover(sems)
    copies = [mover.start(source, target) for source, target in zip(sources, held)]
    width = merge_ref.shape[1]
    rows, half = time_mine.shape
    table_ref[...] = jnp.zeros_like(table_ref)
    table_ref[0 : vectors_ref.shape[0], 0:rows] = vectors_ref[...].astype(HIGH)
    columns = jnp.transpose(table_ref[...])[0:rows].astype(LOW)
    finished(copies)

    def fill(low, high, space_low, space_high):
        low[...] = heads_ref[:, 0:half]
        rest = 3 * width - half
        high[:, 0:rest] = heads_ref[:, half:]
        high[:, rest : rest + width] = merge_ref[...]
        high[:, rest + width : rest + 2 * width] = mixer_ref[...]
        high[:, half - 2 * LANES : half - LANES] = columns
        high[:, half - LANES :] = jnp.zeros_like(columns)
        space_half = space_low.shape[1]
        space_low[...] = space_heads_ref[:, 0:space_half]
        space_high[:, 0 : 3 * width - space_half] = space_heads_ref[:, space_half:]
        space_high[:, 3 * width - space_half :] = space_merge_ref[...]

    @pl.when(place_ref[0] == 0)
    def _():
        fill(time_mine, time_send, space_mine, space_send)

    @pl.when(place_ref[0] != 0)
    def _():
        fill(time_send, time_mine, space_send, space_mine)


def in_hbm(value):
    return pltpu.with_memory_space_constraint(value, pltpu.HBM)


def call(kernel, outs, kept, scratch, flops, name):
    def run(place, blocks, streamed, weights):
        args = (place, *blocks, *streamed)
        every = outs + kept
        moved = sum(a.size * a.dtype.itemsize for a in args)
        moved += sum(s.size * s.dtype.itemsize for s in every)
        in_vmem, in_place = pl.BlockSpec(memory_space=pltpu.VMEM), pl.BlockSpec(memory_space=pltpu.HBM)
        return pl.pallas_call(
            kernel,
            out_shape=outs + tuple(out if out.size > 4000000 else pltpu.HBM(out.shape, out.dtype) for out in kept),
            in_specs=[pl.BlockSpec(memory_space=pltpu.SMEM)]
            + [in_vmem] * len(blocks)
            + [in_place] * len(streamed),
            out_specs=(in_vmem,) * len(outs) + (in_place,) * len(kept),
            scratch_shapes=scratch + weights + [pltpu.SemaphoreType.DMA((32,))],
            compiler_params=pltpu.CompilerParams(vmem_limit_bytes=VMEM_BYTES),
            cost_estimate=pl.CostEstimate(flops=flops, bytes_accessed=moved, transcendentals=0),
            name=name,
        )(place, *blocks, *(in_hbm(value) for value in streamed))

    return run


def weight_scratch(pieces):
    if len(pieces) == 1:
        return pltpu.VMEM(pieces[0].shape, LOW)
    _, count, rows, quarter = pieces[0].shape
    return pltpu.VMEM((count, 4, rows, 4 * quarter), LOW)


def route(kernel, outs, name, place, blocks, whole=False, scratch=()):
    def spec(dims):
        if whole:
            return pl.BlockSpec(memory_space=pltpu.VMEM)
        return pl.BlockSpec((1,) + tuple(dims[1:]), lambda step: (step,) + (0,) * (len(dims) - 1))

    return pl.pallas_call(
        kernel,
        grid=() if whole else (blocks[0].shape[0],),
        out_shape=outs,
        in_specs=[pl.BlockSpec(memory_space=pltpu.SMEM)] + [spec(b.shape) for b in blocks],
        out_specs=tuple(spec(o.shape) for o in outs),
        scratch_shapes=scratch,
        compiler_params=pltpu.CompilerParams(vmem_limit_bytes=VMEM_BYTES),
        name=name,
    )(place, *blocks)


def shape(dims, dtype=LOW):
    return jax.ShapeDtypeStruct(dims, dtype)


SWAP = ((0, 1), (1, 0))


def swapped(value, axis):
    return lax.ppermute(value, axis, SWAP)


def added(left, right, dtype=LOW):
    return (left.astype(HIGH) + right.astype(HIGH)).astype(dtype)


def picked(value, index, axis):
    return lax.dynamic_index_in_dim(value, index, axis, keepdims=False)


def tied(value):
    return lax.optimization_barrier(value)


def synced(groups, *others):
    states, others = tied(([group.state for group in groups], others))
    for group, state in zip(groups, states):
        group.state = state
    return others if len(others) != 1 else others[0]


def shifted(value, distance):
    count = lax.axis_size("z")
    return lax.ppermute(value, "z", [(k, (k - distance) % count) for k in range(count)])


FEW = 4


class Sum:
    def __init__(self, place, keep, send, name):
        self.place, self.name = place, name
        self.count = lax.axis_size("z")
        self.rows = keep.shape[0] // (self.count * 4)
        self.halves = (keep.shape[1],)
        self.state = (keep, swapped(send, "core"))

    def joined(self, other):
        self.halves += other.halves
        self.state += other.state

    def first(self):
        part = shape((self.count, 2, self.rows, sum(self.halves) // 2))
        left, left_keep, right, right_keep = route(
            first_route_kernel, (part,) * 4, self.name + "_first", self.place,
            [value.reshape(self.count, 2, 2, self.rows, -1) for value in self.state],
        )
        self.state = (left_keep, swapped(left, "y"), right_keep, swapped(right, "x"))

    def second(self):
        self.half = sum(self.halves)
        part = shape((self.count, self.rows, self.half // 2))
        left, left_keep, right, right_keep = route(
            second_route_kernel, (part,) * 4, self.name + "_second", self.place, self.state
        )
        self.state = (left_keep, swapped(left, "x"), right_keep, swapped(right, "y"))

    def third(self):
        one = (self.rows, self.half)
        if self.count > FEW:
            outs = (shape((self.count, *one)),)
        else:
            outs = (shape(one, HIGH),) + (shape(one),) * (self.count - 1)
        mine, *sends = route(third_route_kernel, outs, self.name + "_third", self.place, self.state, True)
        if sends:
            self.state = (mine, *(shifted(send, -1 - k) for k, send in enumerate(sends)))
        else:
            arrived = lax.all_to_all(mine, "z", split_axis=0, concat_axis=0, tiled=True)
            self.state = (arrived.astype(HIGH).sum(0),)

    def last(self):
        part = shape((self.rows // 2, self.half), HIGH)
        mine, other = route(last_kernel, (part, part), self.name + "_last", self.place, self.state, True)
        self.state = (mine, swapped(other, "core"))

    def owned(self, spans):
        rows = self.rows // 2
        outs = tuple(
            shape((ROWS_OF_VECTORS, rows) if stop is None else (rows, stop - start), HIGH)
            for _, start, stop in spans
        )
        spans = tuple((which, start, start + LANES if stop is None else stop) for which, start, stop in spans)
        kernel = functools.partial(owned_kernel, self.halves, spans)
        table = [pltpu.VMEM((LANES, LANES), HIGH)]
        return route(kernel, outs, self.name + "_owned", self.place, self.state, True, table)


class Spread:
    def __init__(self, place, chip):
        self.place = place
        self.state = chip
        self.rows, self.half = chip.shape

    def first(self):
        count = lax.axis_size("z")
        if count > FEW:
            column = jnp.broadcast_to(self.state[None], (count, self.rows, self.half))
            self.state = lax.all_to_all(column, "z", split_axis=0, concat_axis=0, tiled=True)
        else:
            self.state = (self.state, *(shifted(self.state, k) for k in range(1, count)))

    def second(self):
        if isinstance(self.state, tuple):
            part = shape((len(self.state), self.rows, self.half // 2))
            left, right = route(arranged_kernel, (part, part), "arranged", self.place, self.state, True)
        else:
            left, right = self.state[..., : self.half // 2], self.state[..., self.half // 2 :]
        self.state = (left, swapped(left, "x"), right, swapped(right, "y"))

    def third(self):
        left, right = jnp.stack(self.state[:2]), jnp.stack(self.state[2:])
        own = (left, swapped(left, "y"), right, swapped(right, "x"))
        self.state = own + (swapped(left, "core"), swapped(right, "core"))

    def fourth(self):
        left, left_got, right, right_got, left_far, right_far = self.state
        far = (left_far, swapped(left_got, "core"), right_far, swapped(right_got, "core"))
        self.state = (left, left_got, right, right_got) + far

    def pieces(self):
        if self.rows % 16 == 0:
            return self.state
        core, x, y = lax.axis_index("core"), lax.axis_index("x"), lax.axis_index("y")

        def placed(near, far, side):
            piece = jnp.stack([near, far], side)
            piece = jnp.where(y == 0, piece, piece[::-1])
            return jnp.where(x == 0, piece, piece[:, ::-1])

        own, far = (
            jnp.concatenate(
                [placed(*self.state[k : k + 2], 0), placed(*self.state[k + 2 : k + 4], 1)], -1
            )
            for k in (0, 4)
        )
        whole = jnp.where(core == 0, jnp.concatenate([own, far], -1), jnp.concatenate([far, own], -1))
        return (whole.transpose(2, 1, 0, 3, 4).reshape(-1, 2 * self.half),)


def regrouped(tokens):
    return lax.all_to_all(tokens, ("y", "core"), split_axis=0, concat_axis=0, tiled=True)


def in_quarters(tokens, quarters, pad):
    _, frames, places, width = tokens.shape
    tokens = tokens.reshape(frames, quarters, places // quarters, width).swapaxes(0, 1)
    return jnp.pad(tokens, ((0, 0), (0, 0), (0, pad - places // quarters), (0, 0)))


def body(
    clips, time_gain, time_shift, time_heads, time_merge, merge_bias, time_mixer, mixer_bias,
    space_gain, space_shift, space_heads, space_merge, space_bias,
    feed_gain, feed_shift, feed_expand, expand_bias, feed_reduce, reduce_bias, cotangent,
):
    everyone = ("z", "x", "y", "core")
    _, near, all_places, width = clips.shape
    quarters = lax.axis_size("y") * lax.axis_size("core")
    frames, places = near * quarters, all_places // quarters
    pad = -(-places // 8) * 8
    rows = frames * pad
    hidden = feed_expand.shape[1]
    blocks = hidden // width
    share = feed_expand.shape[0]
    count = width // share
    core = lax.axis_index("core")
    place = jnp.stack([core, *(lax.axis_index(axis) for axis in ("x", "y", "z"))]).astype(jnp.int32)

    tall, tokens = (rows, width), (frames, pad, width)
    tiles = (width // LANES, rows, LANES)
    token_flops = 2 * rows * width * width
    vec_shape = shape((ROWS_OF_VECTORS, width), HIGH)
    space_half = 2 * width

    clips_in = in_quarters(clips, quarters, pad)
    by_place = regrouped(clips_in).reshape(tokens)
    vectors = jnp.concatenate(
        [
            jnp.stack(
                [
                    time_gain, time_shift, merge_bias, mixer_bias, space_gain, space_shift, space_bias,
                    feed_gain, feed_shift, reduce_bias,
                ]
            ),
            expand_bias.reshape(blocks, share),
        ],
        0,
    )
    time_half = 5 * width // 2 + LANES
    time_part, space_part = shape((share, time_half)), shape((share, space_half))
    sources = (time_heads, time_merge, time_mixer, space_heads, space_merge)
    time_mine, time_send, space_mine, space_send = call(
        prepare_kernel,
        (time_part, time_part, space_part, space_part),
        (),
        [pltpu.VMEM(source.shape, LOW) for source in sources] + [pltpu.VMEM((LANES, LANES), HIGH)],
        0,
        "prepare",
    )(place, (vectors,), sources, [])

    def spread(mine, send):
        got = swapped(send, "core")
        chip = jnp.where(core == 0, jnp.concatenate([mine, got], 0), jnp.concatenate([got, mine], 0))
        return Spread(place, chip)

    time = spread(time_mine, time_send)
    feed_expand, feed_reduce, cotangent = synced([time], feed_expand, feed_reduce, cotangent)
    time.first()
    space = spread(space_mine, space_send)
    expand = feed_expand.reshape(share, count, blocks, share).swapaxes(1, 2).reshape(share, hidden)
    feed_pack = jnp.concatenate([expand, *feed_reduce.reshape(blocks, share, width)], 1)
    feed_pack, by_place = synced([time, space], feed_pack, by_place)
    feed = lax.all_gather(feed_pack, everyone, axis=0, tiled=True)
    time.second()
    space.first()
    upstream_in = in_quarters(cotangent, quarters, pad)
    upstream_in = synced([time, space], upstream_in)
    time.third()
    synced([time])
    time.fourth()
    space.second()
    synced([time, space])
    space.third()
    low, high = pltpu.VMEM(tall, LOW), pltpu.VMEM(tall, HIGH)
    wide = pltpu.VMEM((rows, 3 * width), LOW)
    branch, vec, *time_kept = call(
        time_forward_kernel,
        (shape(tokens), vec_shape),
        (shape(tall), shape(wide.shape), shape(tall), shape(tall)),
        [pltpu.VMEM(tiles, HIGH), low, wide, low, low],
        6 * token_flops,
        "time_forward",
    )(place, (by_place,), time.pieces(), [weight_scratch(time.pieces())])
    branch = synced([space], branch)
    by_frame = regrouped(branch.reshape(clips_in.shape))
    space.fourth()
    after_space, *space_kept = call(
        functools.partial(space_forward_kernel, all_places),
        (shape(tall, HIGH),),
        (shape(tall, HIGH), shape(tall), shape(wide.shape), shape(tall)),
        [high, high, low, wide, low],
        6 * token_flops,
        "space_forward",
    )(place, (clips_in, by_frame, vec), space.pieces(), [weight_scratch(space.pieces())])
    space_sum, feed_vec, result, feed_grad = call(
        feed_kernel,
        (shape(tall, HIGH), vec_shape),
        (shape(clips_in.shape), jax.ShapeDtypeStruct((width, 2 * hidden), LOW)),
        [high, low, low, high, high, pltpu.VMEM(clips_in.shape, LOW)],
        24 * token_flops,
        "feed",
    )(
        place, (after_space, upstream_in, vec), (feed,),
        [pltpu.VMEM((blocks, 2, width, width), LOW), pltpu.VMEM((2, 2, width, width), LOW)],
    )
    feed_owned = lax.psum_scatter(feed_grad, everyone, scatter_dimension=0, tiled=True)
    time_round, space_keep, space_send, space_vec, time_sum = call(
        functools.partial(space_backward_kernel, all_places),
        (shape(clips_in.shape), shape((width, space_half)), shape((width, space_half)), vec_shape),
        (shape(tall, HIGH),),
        [high, low, wide, low, high, low, low, wide],
        12 * token_flops,
        "space_backward",
    )(place, (space_sum, vec), (*space_kept, *space.pieces()), [weight_scratch(space.pieces())])
    space_sums = Sum(place, space_keep, space_send, "space")
    time_round = regrouped(time_round)
    space_sums.first()
    inward, time_keep, time_send = call(
        time_backward_kernel,
        (shape(tokens), shape((width, time_half)), shape((width, time_half))),
        (),
        [
            pltpu.VMEM(tokens, LOW), low, wide, low, low,
            pltpu.VMEM(tiles, HIGH), low, low, wide, pltpu.VMEM((LANES, width), HIGH),
        ],
        14 * token_flops,
        "time_backward",
    )(
        place, (time_round.reshape(tokens), vec, space_vec, feed_vec),
        (by_place, *time_kept, *time.pieces()), [weight_scratch(time.pieces())],
    )
    inward, time_keep, time_send = synced([space_sums], inward, time_keep, time_send)
    time_sums = Sum(place, time_keep, time_send, "time")
    entry_round = regrouped(inward.reshape(clips_in.shape))
    space_sums.second()
    synced([time_sums])
    time_sums.first()
    synced([time_sums, space_sums])
    time_sums.second()
    space_sums.third()
    entry_round = synced([time_sums], entry_round)
    time_sums.third()
    time_sum = time_sum.reshape(near, quarters, pad, width)
    grad_clips = (time_sum + entry_round.swapaxes(0, 1).astype(HIGH)).astype(LOW)
    grad_clips = grad_clips[:, :, :places].reshape(clips.shape)
    layer_output = result[:, :, :places].swapaxes(0, 1).reshape(clips.shape)
    layer_output, grad_clips = synced([time_sums, space_sums], layer_output, grad_clips)
    space_sums.last()
    time_sums.last()
    grad_space_heads, grad_space_merge = space_sums.owned([(0, 0, 3 * width), (0, 3 * width, 4 * width)])
    grad_time_heads, grad_time_merge, grad_time_mixer, vector_grads = time_sums.owned(
        [(0, 0, 3 * width), (0, 3 * width, 4 * width), (0, 4 * width, 5 * width), (0, 5 * width, None)]
    )
    vector_grads = vector_grads[:VECTORS]
    feed_owned = feed_owned.astype(HIGH)
    grad_expand = feed_owned[:, :hidden].reshape(share, blocks, count, share).swapaxes(1, 2).reshape(share, hidden)
    grad_reduce = jnp.concatenate(
        [feed_owned[:, hidden + k * width : hidden + (k + 1) * width] for k in range(blocks)], 0
    )
    return (
        layer_output,
        grad_clips,
        vector_grads[TIME_GAIN],
        vector_grads[TIME_SHIFT],
        grad_time_heads,
        grad_time_merge,
        vector_grads[MERGE_BIAS],
        grad_time_mixer,
        vector_grads[MIXER_BIAS],
        vector_grads[SPACE_GAIN],
        vector_grads[SPACE_SHIFT],
        grad_space_heads,
        grad_space_merge,
        vector_grads[SPACE_BIAS],
        vector_grads[FEED_GAIN],
        vector_grads[FEED_SHIFT],
        grad_expand,
        vector_grads[EXPAND_BIAS:].reshape(-1),
        grad_reduce,
        vector_grads[REDUCE_BIAS],
    )


def solution(mesh):
    clip, st = mesh.shape["clip"], mesh.shape["st"]
    finer = Mesh(mesh.devices.reshape(clip // 2, 2, st // 2, 2), ("z", "x", "y", "core"))
    token = P(("z", "x"), ("y", "core"), None, None)
    vec = P(("z", "x", "y", "core"))
    mat = P(("z", "x", "y", "core"), None)
    in_specs = (
        token, vec, vec, mat, mat, vec, mat, vec, vec, vec, mat, mat, vec, vec, vec, mat, vec, mat, vec, token,
    )
    out_specs = (
        token, token, vec, vec, mat, mat, vec, mat, vec, vec, vec, mat, mat, vec, vec, vec, mat, vec, mat, vec,
    )
    return jax.shard_map(body, mesh=finer, in_specs=in_specs, out_specs=out_specs, check_vma=False)
```

```python
import functools

import jax
import jax.numpy as jnp
from jax import lax
from jax.experimental import pallas as pl
from jax.experimental.pallas import tpu as pltpu
from jax.sharding import Mesh
from jax.sharding import PartitionSpec as P

HEADS = 12
HEAD_DIM = 64
LANES = 128
EPSILON = 1e-06
SCALE = 0.125
ROOT_HALF = 0.7071067811865476
DENSITY = 0.3989422804014327
LOW = jnp.bfloat16
HIGH = jnp.float32
TIME_BLOCK = 112
VMEM_BYTES = 28 * 1024 * 1024

TIME_GAIN, TIME_SHIFT, MERGE_BIAS, MIXER_BIAS = 0, 1, 2, 3
SPACE_GAIN, SPACE_SHIFT, SPACE_BIAS = 4, 5, 6
FEED_GAIN, FEED_SHIFT, REDUCE_BIAS, EXPAND_BIAS = 7, 8, 9, 10
VECTORS = 14
ROWS_OF_VECTORS = 16


def dot(left, right):
    return jnp.dot(left, right, preferred_element_type=HIGH)


def dot_nt(left, right):
    return lax.dot_general(left, right, (((1,), (1,)), ((), ())), preferred_element_type=HIGH)


def dot_tn(left, right):
    return lax.dot_general(left, right, (((0,), (0,)), ((), ())), preferred_element_type=HIGH)


def norm(values, gain, shift):
    centred = values - jnp.mean(values, -1, keepdims=True)
    inverse = lax.rsqrt(jnp.mean(centred * centred, -1, keepdims=True) + EPSILON)
    normed = centred * inverse
    return normed * gain + shift, normed, inverse


def norm_back(upstream, normed, inverse, gain):
    scaled = upstream * gain
    return inverse * (
        scaled
        - jnp.mean(scaled, -1, keepdims=True)
        - normed * jnp.mean(scaled * normed, -1, keepdims=True)
    )


def column_sum(values):
    return jnp.sum(values, 0, keepdims=True)


class Mover:
    def __init__(self, sems):
        self.sems, self.used = sems, 0

    def start(self, source, target):
        copy = pltpu.make_async_copy(source, target, self.sems.at[self.used])
        self.used += 1
        copy.start()
        return copy

    def start_rows(self, source, target, parts=7):
        return [self.start(source, target)]


def finished(copies):
    for copy in copies:
        copy.wait()


def stacked(pair, scale=1.0):
    lane = lax.broadcasted_iota(jnp.int32, (1, LANES), 1)
    first = jnp.where(lane < HEAD_DIM, scale, 0.0).astype(LOW)
    second = jnp.where(lane < HEAD_DIM, 0.0, scale).astype(LOW)
    return jnp.concatenate([pair * first, pair * second], 0)


def joined(both):
    rows = both.shape[0] // 2
    lane = lax.broadcasted_iota(jnp.int32, (rows, LANES), 1)
    return jnp.where(lane < HEAD_DIM, both[:rows], both[rows:])


def shares_of(queries, key_rows, valid):
    scores = jnp.where(valid, dot_nt(queries, key_rows), -1e30)
    raised = jnp.exp(scores - jnp.max(scores, -1, keepdims=True))
    return raised * (1.0 / jnp.sum(raised, -1, keepdims=True))


def pair_forward(packed_ref, mixed_ref, rows, pair, width, valid):
    at = [slice(pair * LANES + part * width, (pair + 1) * LANES + part * width) for part in range(3)]
    queries = stacked(packed_ref[rows, at[0]], SCALE)
    shares = shares_of(queries, packed_ref[rows, at[1]], valid)
    mixed = dot(shares.astype(LOW), packed_ref[rows, at[2]])
    mixed_ref[rows, at[0]] = joined(mixed).astype(LOW)


def pair_backward(packed_ref, up_ref, grad_ref, rows, pair, width, valid):
    at = [slice(pair * LANES + part * width, (pair + 1) * LANES + part * width) for part in range(3)]
    queries = stacked(packed_ref[rows, at[0]], SCALE)
    key_rows = packed_ref[rows, at[1]]
    upstream = stacked(up_ref[rows, at[0]])
    scores = jnp.where(valid, dot_nt(key_rows, queries), -1e30)
    raised = jnp.exp(scores - jnp.max(scores, 0, keepdims=True))
    shares = raised * (1.0 / jnp.sum(raised, 0, keepdims=True))
    grad_shares = dot_nt(packed_ref[rows, at[2]], upstream)
    grad_scores = (
        shares * (grad_shares - jnp.sum(grad_shares * shares, 0, keepdims=True))
    ).astype(LOW)
    grad_ref[rows, at[0]] = (joined(dot_tn(grad_scores, key_rows)) * SCALE).astype(LOW)
    grad_ref[rows, at[1]] = dot(grad_scores, queries).astype(LOW)
    grad_ref[rows, at[2]] = dot(shares.astype(LOW), upstream).astype(LOW)


def time_valid(block, frames, turned=False):
    dims = (block, 2 * block) if turned else (2 * block, block)
    row = lax.broadcasted_iota(jnp.int32, dims, 0)
    col = lax.broadcasted_iota(jnp.int32, dims, 1)
    return (row % block) // frames == (col % block) // frames


def space_valid(rows, pad, places, turned=False):
    dims = (rows, 2 * rows) if turned else (2 * rows, rows)
    return lax.broadcasted_iota(jnp.int32, dims, 0 if turned else 1) % pad < places


def vector(vec_ref, row):
    return vec_ref[row : row + 1, :]


def to_places(tokens_ref, tiles_ref):
    frames, places, width = tokens_ref.shape
    for frame in range(frames):
        rows = tokens_ref[frame].astype(HIGH)
        for tile in range(width // LANES):
            at = slice(tile * LANES, (tile + 1) * LANES)
            tiles_ref[tile, pl.ds(frame, places, stride=frames), :] = rows[:, at]
    return jnp.concatenate([tiles_ref[tile] for tile in range(width // LANES)], 1)


def from_places(values, tiles_ref, tokens_ref):
    frames, places, width = tokens_ref.shape
    for tile in range(width // LANES):
        tiles_ref[tile] = values[:, tile * LANES : (tile + 1) * LANES]
    for frame in range(frames):
        for tile in range(width // LANES):
            at = slice(tile * LANES, (tile + 1) * LANES)
            rows = tiles_ref[tile, pl.ds(frame, places, stride=frames), :]
            tokens_ref[frame, :, at] = rows.astype(LOW)


def to_frames(tokens_ref, held_ref):
    quarters, frames, places, _ = tokens_ref.shape
    for frame in range(frames):
        for quarter in range(quarters):
            start = (frame * quarters + quarter) * places
            held_ref[start : start + places, :] = tokens_ref[quarter, frame].astype(held_ref.dtype)


def from_frames(held_ref, tokens_ref):
    quarters, frames, places, _ = tokens_ref.shape
    for frame in range(frames):
        for quarter in range(quarters):
            start = (frame * quarters + quarter) * places
            tokens_ref[quarter, frame] = held_ref[start : start + places, :].astype(LOW)


def weight_copies(place_ref, pieces, weight_ref, mover):
    if len(pieces) == 1:
        return [mover.start(pieces[0], weight_ref)]
    core, x, y = place_ref[0], place_ref[1], place_ref[2]
    quarter = pieces[0].shape[-1]
    copies = []
    for number, piece in enumerate(pieces):
        whose, side, far = number // 4, number // 2 % 2, number % 2
        half = core if whose == 0 else 1 - core
        start = pl.multiple_of(half * (2 * quarter) + side * quarter, LANES)
        for near in range(2):
            far_y, far_x = (far, near) if side == 0 else (near, far)
            at_x = 1 - x if far_x else x
            at_y = 1 - y if far_y else y
            target = weight_ref.at[:, at_x * 2 + at_y, :, pl.ds(start, quarter)]
            copies.append(mover.start(piece.at[near], target))
    return copies


def columns_of(weight_ref, at):
    if len(weight_ref.shape) == 2:
        return weight_ref[:, at]
    value = weight_ref[:, :, :, at]
    return value.reshape(-1, value.shape[-1])


def put(core, half, keep_ref, send_ref, at, value):
    @pl.when(core == half)
    def _():
        keep_ref[:, at] = value

    @pl.when(core != half)
    def _():
        send_ref[:, at] = value


def time_forward_kernel(place_ref, tokens_ref, *refs):
    *pieces, branch_ref, vec_ref = refs[:-11]
    *kept, tiles_ref, entry_ref, packed_ref, mixed_ref, middle_ref, weight_ref, sems = refs[-11:]
    frames, _, width = tokens_ref.shape
    rows = entry_ref.shape[0]
    mover = Mover(sems)
    copies = weight_copies(place_ref, pieces, weight_ref, mover)
    tokens = to_places(tokens_ref, tiles_ref)
    finished(copies)
    vec_at = slice(5 * width, 5 * width + LANES)
    vec_ref[...] = jnp.transpose(columns_of(weight_ref, vec_at).astype(HIGH))[:ROWS_OF_VECTORS]
    entry, _, _ = norm(tokens, vector(vec_ref, TIME_GAIN), vector(vec_ref, TIME_SHIFT))
    entry_ref[...] = entry.astype(LOW)
    stores = mover.start_rows(entry_ref, kept[0])
    for part in range(3):
        at = slice(part * width, (part + 1) * width)
        packed_ref[:, at] = dot(entry_ref[...], columns_of(weight_ref, at)).astype(LOW)
    stores += mover.start_rows(packed_ref, kept[1])
    valid = time_valid(TIME_BLOCK, frames)

    for pair in range(HEADS // 2):
        for start in range(0, rows, TIME_BLOCK):
            pair_forward(packed_ref, mixed_ref, slice(start, start + TIME_BLOCK), pair, width, valid)
    stores += mover.start_rows(mixed_ref, kept[2])
    merge = columns_of(weight_ref, slice(3 * width, 4 * width))
    middle_ref[...] = (dot(mixed_ref[...], merge) + vector(vec_ref, MERGE_BIAS)).astype(LOW)
    stores += mover.start_rows(middle_ref, kept[3])
    mixer = columns_of(weight_ref, slice(4 * width, 5 * width))
    branch = dot(middle_ref[...], mixer) + vector(vec_ref, MIXER_BIAS)
    from_places(branch, tiles_ref, branch_ref)
    finished(stores)


def space_forward_kernel(all_places, place_ref, clips_ref, branch_ref, vec_ref, *refs):
    *pieces, after_space_ref = refs[:-11]
    *kept, held_ref, after_time_ref, entry_ref, packed_ref, mixed_ref, weight_ref, sems = refs[-11:]
    quarters, frames, pad, width = clips_ref.shape
    rows = held_ref.shape[0]
    mover = Mover(sems)
    copies = weight_copies(place_ref, pieces, weight_ref, mover)
    to_frames(clips_ref, after_time_ref)
    to_frames(branch_ref, held_ref)
    after_time = after_time_ref[...] + held_ref[...]
    after_time_ref[...] = after_time
    stores = mover.start_rows(after_time_ref, kept[0])
    entry, _, _ = norm(after_time, vector(vec_ref, SPACE_GAIN), vector(vec_ref, SPACE_SHIFT))
    entry_ref[...] = entry.astype(LOW)
    stores += mover.start_rows(entry_ref, kept[1])
    finished(copies)
    for part in range(3):
        at = slice(part * width, (part + 1) * width)
        packed_ref[:, at] = dot(entry_ref[...], columns_of(weight_ref, at)).astype(LOW)
    stores += mover.start_rows(packed_ref, kept[2])
    each = rows // frames
    valid = space_valid(each, pad, all_places // quarters)

    for pair in range(HEADS // 2):
        for start in range(0, rows, each):
            pair_forward(packed_ref, mixed_ref, slice(start, start + each), pair, width, valid)
    stores += mover.start_rows(mixed_ref, kept[3])
    merge = columns_of(weight_ref, slice(3 * width, 4 * width))
    after_space_ref[...] = (
        after_time_ref[...] + dot(mixed_ref[...], merge) + vector(vec_ref, SPACE_BIAS)
    )
    finished(stores)


def feed_kernel(
    place_ref, after_space_ref, upstream_ref, vec_ref, weight_ref,
    space_sum_ref, grad_vec_ref, keep_ref, send_ref, result_ref, grad_ref,
    held_ref, up_ref, entry_ref, out_ref, back_ref, results_ref, weights_ref, grads_ref, sems,
):
    width = after_space_ref.shape[-1]
    half = weight_ref.shape[1] // 2
    blocks = half // width
    mover = Mover(sems)

    def columns(side, block, whole=half):
        return pl.ds(side * whole + block * width, width)

    def load(block):
        return [
            copy
            for side in range(2)
            for copy in mover.start_rows(weight_ref.at[:, columns(side, block)], weights_ref.at[block, side], 4)
        ]

    loads = [load(block) for block in range(blocks)]
    to_frames(upstream_ref, held_ref)
    up_ref[...] = held_ref[...].astype(LOW)
    gain, shift = vector(vec_ref, FEED_GAIN), vector(vec_ref, FEED_SHIFT)
    entry, _, _ = norm(after_space_ref[...], gain, shift)
    entry_ref[...] = entry.astype(LOW)
    grad_vec_ref[...] = jnp.zeros_like(grad_vec_ref)
    stores = []
    for block in range(blocks):
        finished(loads[block])
        expand, reduce = weights_ref[block, 0], weights_ref[block, 1]
        hidden = dot(entry_ref[...], expand) + vector(vec_ref, EXPAND_BIAS + block)
        normal = 0.5 * (1.0 + lax.erf(hidden * ROOT_HALF))
        active = (hidden * normal).astype(LOW)
        out = dot(active, reduce)
        slope = normal + hidden * DENSITY * jnp.exp(-0.5 * hidden * hidden)
        hidden_grad = (dot_nt(up_ref[...], reduce) * slope).astype(LOW)
        back = dot_nt(hidden_grad, expand)
        if block:
            out_ref[...] += out
            back_ref[...] += back
        else:
            out_ref[...] = after_space_ref[...] + vector(vec_ref, REDUCE_BIAS) + out
            back_ref[...] = back
        grad_vec_ref[3 + block : 4 + block, :] = column_sum(hidden_grad.astype(HIGH))
        expand_grad = dot_tn(entry_ref[...], hidden_grad).astype(LOW)
        reduce_grad = dot_tn(active, up_ref[...]).astype(LOW)
        if block == blocks - 1:
            put(place_ref[0], 0, keep_ref, send_ref, slice(0, width), expand_grad)
            put(place_ref[0], 1, keep_ref, send_ref, slice(0, width), reduce_grad)
            continue
        if block > 1:
            finished(stores[2 * block - 4 : 2 * block - 2])
        grads_ref[block % 2, 0] = expand_grad
        grads_ref[block % 2, 1] = reduce_grad
        for side in range(2):
            target = grad_ref.at[:, columns(side, block, half - width)]
            stores.append(mover.start(grads_ref.at[block % 2, side], target))
    from_frames(out_ref, results_ref)
    stores.append(mover.start(results_ref, result_ref))
    _, normed, inverse = norm(after_space_ref[...], gain, shift)
    upstream = back_ref[...]
    grad_vec_ref[0:1, :] = column_sum(upstream * normed)
    grad_vec_ref[1:2, :] = column_sum(upstream)
    grad_vec_ref[2:3, :] = column_sum(held_ref[...])
    space_sum_ref[...] = held_ref[...] + norm_back(upstream, normed, inverse, gain)
    finished(stores[2 * blocks - 6 :])


def space_backward_kernel(all_places, place_ref, space_sum_ref, vec_ref, *refs):
    *kept, time_round_ref, keep_ref, send_ref, grad_vec_ref, time_sum_ref = refs[:-10]
    kept, pieces = kept[:4], kept[4:]
    *held, sum_ref, round_ref, up_ref, grad_ref, weight_ref, sems = refs[-10:]
    after_time_ref, entry_ref, packed_ref, mixed_ref = held
    rows, width = space_sum_ref.shape
    quarters, frames, pad, _ = time_round_ref.shape
    core = place_ref[0]
    half = keep_ref.shape[1]
    mover = Mover(sems)
    mixed_copies = mover.start_rows(kept[3], mixed_ref)
    copies = weight_copies(place_ref, pieces, weight_ref, mover)
    packed_copies = mover.start_rows(kept[2], packed_ref)
    others = mover.start_rows(kept[1], entry_ref) + mover.start_rows(kept[0], after_time_ref)
    round_ref[...] = space_sum_ref[...].astype(LOW)
    finished(mixed_copies)
    put(core, 1, keep_ref, send_ref, slice(half - width, half), dot_tn(mixed_ref[...], round_ref[...]).astype(LOW))
    finished(copies)
    up_ref[...] = dot_nt(round_ref[...], columns_of(weight_ref, slice(3 * width, 4 * width))).astype(LOW)
    each = rows // frames
    valid = space_valid(each, pad, all_places // quarters, True)
    finished(packed_copies)

    for pair in range(HEADS // 2):
        for start in range(0, rows, each):
            pair_backward(packed_ref, up_ref, grad_ref, slice(start, start + each), pair, width, valid)
    finished(others)
    back = dot_nt(grad_ref[:, 0:width], columns_of(weight_ref, slice(0, width)))
    for part in range(1, 3):
        at = slice(part * width, (part + 1) * width)
        back += dot_nt(grad_ref[:, at], columns_of(weight_ref, at))
    gain = vector(vec_ref, SPACE_GAIN)
    _, normed, inverse = norm(after_time_ref[...], gain, vector(vec_ref, SPACE_SHIFT))
    sum_ref[...] = space_sum_ref[...] + norm_back(back, normed, inverse, gain)
    stores = mover.start_rows(sum_ref, time_sum_ref)
    from_frames(sum_ref, time_round_ref)
    grad_vec_ref[...] = jnp.zeros_like(grad_vec_ref)
    grad_vec_ref[0:1, :] = column_sum(back * normed)
    grad_vec_ref[1:2, :] = column_sum(back)
    grad_vec_ref[2:3, :] = column_sum(round_ref[...].astype(HIGH))
    for part in range(3):
        at = slice(part * width, (part + 1) * width)
        value = dot_tn(entry_ref[...], grad_ref[:, at]).astype(LOW)
        start = part * width % half
        put(core, part * width // half, keep_ref, send_ref, slice(start, start + width), value)
    finished(stores)


def time_backward_kernel(place_ref, time_round_ref, vec_ref, space_vec_ref, feed_vec_ref, *refs):
    *kept, inward_ref, keep_ref, send_ref = refs[:-12]
    kept, pieces = kept[:5], kept[5:]
    *held, tiles_ref, round_ref, up_ref, grad_ref, vectors_ref, weight_ref, sems = refs[-12:]
    tokens_ref, entry_ref, packed_ref, mixed_ref, middle_ref = held
    frames, _, width = time_round_ref.shape
    rows = entry_ref.shape[0]
    core = place_ref[0]
    half = keep_ref.shape[1]
    mover = Mover(sems)
    middle_copies = mover.start_rows(kept[4], middle_ref)
    copies = weight_copies(place_ref, pieces, weight_ref, mover)
    mixed_copies, packed_copies = mover.start_rows(kept[3], mixed_ref), mover.start_rows(kept[2], packed_ref)
    others = mover.start_rows(kept[1], entry_ref) + mover.start_rows(kept[0], tokens_ref, 8)
    rounded = to_places(time_round_ref, tiles_ref)
    round_ref[...] = rounded.astype(LOW)
    vectors_ref[...] = jnp.zeros_like(vectors_ref)
    vectors_ref[MIXER_BIAS : MIXER_BIAS + 1, :] = column_sum(rounded)
    tail = 3 * width - half
    at = slice(tail + width, tail + 2 * width)
    finished(middle_copies)
    put(core, 1, keep_ref, send_ref, at, dot_tn(middle_ref[...], round_ref[...]).astype(LOW))
    finished(copies)
    up_ref[...] = dot_nt(round_ref[...], columns_of(weight_ref, slice(4 * width, 5 * width))).astype(LOW)
    vectors_ref[MERGE_BIAS : MERGE_BIAS + 1, :] = column_sum(up_ref[...].astype(HIGH))
    at = slice(tail, tail + width)
    finished(mixed_copies)
    put(core, 1, keep_ref, send_ref, at, dot_tn(mixed_ref[...], up_ref[...]).astype(LOW))
    up_ref[...] = dot_nt(up_ref[...], columns_of(weight_ref, slice(3 * width, 4 * width))).astype(LOW)
    valid = time_valid(TIME_BLOCK, frames, True)
    finished(packed_copies)

    for pair in range(HEADS // 2):
        for start in range(0, rows, TIME_BLOCK):
            pair_backward(packed_ref, up_ref, grad_ref, slice(start, start + TIME_BLOCK), pair, width, valid)
    finished(others)
    for start, stop in ((0, half), (half, 3 * width)):
        value = dot_tn(entry_ref[...], grad_ref[:, start:stop]).astype(LOW)
        put(core, start // half, keep_ref, send_ref, slice(0, stop - start), value)
    back = dot_nt(grad_ref[:, 0:width], columns_of(weight_ref, slice(0, width)))
    for part in range(1, 3):
        at = slice(part * width, (part + 1) * width)
        back += dot_nt(grad_ref[:, at], columns_of(weight_ref, at))
    tokens = to_places(tokens_ref, tiles_ref)
    gain = vector(vec_ref, TIME_GAIN)
    _, normed, inverse = norm(tokens, gain, vector(vec_ref, TIME_SHIFT))
    vectors_ref[TIME_GAIN : TIME_GAIN + 1, :] = column_sum(back * normed)
    vectors_ref[TIME_SHIFT : TIME_SHIFT + 1, :] = column_sum(back)
    for start, stop, source in ((SPACE_GAIN, FEED_GAIN, space_vec_ref), (FEED_GAIN, VECTORS, feed_vec_ref)):
        for row in range(start, stop):
            vectors_ref[row : row + 1, :] = source[row - start : row - start + 1, :]
    columns = jnp.transpose(vectors_ref[...]).astype(LOW)
    put(core, 1, keep_ref, send_ref, slice(half - 2 * LANES, half - LANES), columns)
    put(core, 1, keep_ref, send_ref, slice(half - LANES, half), jnp.zeros_like(columns))
    from_places(norm_back(back, normed, inverse, gain), tiles_ref, inward_ref)


def first_route_kernel(place_ref, *refs):
    *pairs, left_send, left_keep, right_send, right_keep = refs
    x, y = place_ref[1], place_ref[2]
    begin = 0
    for keep_ref, got_ref in zip(pairs[::2], pairs[1::2]):
        quarter = keep_ref.shape[-1] // 2
        left, right = slice(0, quarter), slice(quarter, 2 * quarter)
        to = slice(begin, begin + quarter)
        begin += quarter

        def total(at_x, at_y, columns):
            return added(keep_ref[0, at_x, at_y, :, columns], got_ref[0, at_x, at_y, :, columns])

        for other in range(2):
            left_send[0, other, :, to] = total(other, 1 - y, left)
            right_send[0, other, :, to] = total(1 - x, other, right)
            left_keep[0, other, :, to] = total(other, y, left)
            right_keep[0, other, :, to] = total(x, other, right)


def second_route_kernel(place_ref, *refs):
    *fours, left_send, left_keep, right_send, right_keep = refs
    x, y = place_ref[1], place_ref[2]
    begin = 0
    for at in range(0, len(fours), 4):
        left_ref, left_got, right_ref, right_got = fours[at : at + 4]
        to = slice(begin, begin + left_ref.shape[-1])
        begin = to.stop
        left_send[0, :, to] = added(left_ref[0, 1 - x], left_got[0, 1 - x])
        right_send[0, :, to] = added(right_ref[0, 1 - y], right_got[0, 1 - y])
        left_keep[0, :, to] = added(left_ref[0, x], left_got[0, x])
        right_keep[0, :, to] = added(right_ref[0, y], right_got[0, y])


def third_route_kernel(place_ref, left_ref, left_got, right_ref, right_got, *sends):
    quarter = left_ref.shape[-1]
    count = left_ref.shape[0]
    for distance, send in enumerate(sends):
        at = lax.rem(place_ref[3] + distance, count) if len(sends) > 1 else 0
        rows = at if len(sends) > 1 else slice(None)
        send[..., 0:quarter] = added(left_ref[rows], left_got[rows], send.dtype)
        send[..., quarter : 2 * quarter] = added(right_ref[rows], right_got[rows], send.dtype)


def last_kernel(place_ref, *refs):
    *parts, mine_ref, other_ref = refs
    total = sum(part[...].astype(HIGH) for part in parts)
    rows = mine_ref.shape[0]
    near, far = total[:rows], total[rows:]
    mine_ref[...] = jnp.where(place_ref[0] == 0, near, far)
    other_ref[...] = jnp.where(place_ref[0] == 0, far, near)


def owned_kernel(halves, spans, place_ref, mine_ref, other_ref, *refs):
    core = place_ref[0]
    half = sum(halves)
    outs, table_ref = refs[:-1], refs[-1]
    begin, wholes = 0, []
    for each in halves:
        quarters = [slice(at, at + each // 2) for at in (begin, half // 2 + begin)]
        begin += each // 2
        low = [jnp.where(core == 0, mine_ref[:, at], other_ref[:, at]) for at in quarters]
        high = [jnp.where(core == 0, other_ref[:, at], mine_ref[:, at]) for at in quarters]
        wholes.append(jnp.concatenate(low + high, 1))
    for (matrix, start, stop), out_ref in zip(spans, outs):
        value = wholes[matrix][:, start:stop]
        if out_ref.shape == value.shape:
            out_ref[...] = value
        else:
            table_ref[...] = jnp.zeros_like(table_ref)
            table_ref[0 : value.shape[0], :] = value
            out_ref[...] = jnp.transpose(table_ref[...])[: out_ref.shape[0], : out_ref.shape[1]]


def feed_owned_kernel(place_ref, owned_ref, last_expand_ref, last_reduce_ref, expand_ref, reduce_ref, table_ref, turned_ref):
    rows, hidden = expand_ref.shape
    width = reduce_ref.shape[1]
    blocks, count = hidden // width, width // rows
    before = hidden - width
    for block in range(blocks - 1):
        at = slice(before + block * width, before + (block + 1) * width)
        reduce_ref[block * rows : (block + 1) * rows, :] = owned_ref[:, at].astype(HIGH)
    reduce_ref[(blocks - 1) * rows :, :] = last_reduce_ref[...]
    table_ref[...] = jnp.zeros_like(table_ref)
    table_ref[0:rows, 0:before] = owned_ref[:, 0:before].astype(HIGH)
    table_ref[0:rows, before:] = last_expand_ref[...]
    turned = jnp.transpose(table_ref[...])
    for block in range(blocks):
        for owner in range(count):
            to = (owner * blocks + block) * rows
            at = block * width + owner * rows
            turned_ref[to : to + rows, :] = turned[at : at + rows]
    expand_ref[...] = jnp.transpose(turned_ref[...])[0:rows]


def arranged_kernel(place_ref, *refs):
    *blocks, left_ref, right_ref = refs
    count, _, quarter = left_ref.shape
    for distance, block in enumerate(blocks):
        at = lax.rem(place_ref[3] + distance, count)
        left_ref[at] = block[:, 0:quarter]
        right_ref[at] = block[:, quarter : 2 * quarter]


def prepare_kernel(place_ref, vectors_ref, *refs):
    *sources, time_mine, time_send, space_mine, space_send = refs[:-7]
    *held, table_ref, sems = refs[-7:]
    heads_ref, merge_ref, mixer_ref, space_heads_ref, space_merge_ref = held
    mover = Mover(sems)
    copies = [mover.start(source, target) for source, target in zip(sources, held)]
    width = merge_ref.shape[1]
    rows, half = time_mine.shape
    table_ref[...] = jnp.zeros_like(table_ref)
    table_ref[0 : vectors_ref.shape[0], 0:rows] = vectors_ref[...].astype(HIGH)
    columns = jnp.transpose(table_ref[...])[0:rows].astype(LOW)
    finished(copies)

    def fill(low, high, space_low, space_high):
        low[...] = heads_ref[:, 0:half]
        rest = 3 * width - half
        high[:, 0:rest] = heads_ref[:, half:]
        high[:, rest : rest + width] = merge_ref[...]
        high[:, rest + width : rest + 2 * width] = mixer_ref[...]
        high[:, half - 2 * LANES : half - LANES] = columns
        high[:, half - LANES :] = jnp.zeros_like(columns)
        space_half = space_low.shape[1]
        space_low[...] = space_heads_ref[:, 0:space_half]
        space_high[:, 0 : 3 * width - space_half] = space_heads_ref[:, space_half:]
        space_high[:, 3 * width - space_half :] = space_merge_ref[...]

    @pl.when(place_ref[0] == 0)
    def _():
        fill(time_mine, time_send, space_mine, space_send)

    @pl.when(place_ref[0] != 0)
    def _():
        fill(time_send, time_mine, space_send, space_mine)


def in_hbm(value):
    return pltpu.with_memory_space_constraint(value, pltpu.HBM)


def call(kernel, outs, kept, scratch, flops, name):
    def run(place, blocks, streamed, weights):
        args = (place, *blocks, *streamed)
        every = outs + kept
        moved = sum(a.size * a.dtype.itemsize for a in args)
        moved += sum(s.size * s.dtype.itemsize for s in every)
        in_vmem, in_place = pl.BlockSpec(memory_space=pltpu.VMEM), pl.BlockSpec(memory_space=pltpu.HBM)
        return pl.pallas_call(
            kernel,
            out_shape=outs + tuple(out if out.size > 3000000 else pltpu.HBM(out.shape, out.dtype) for out in kept),
            in_specs=[pl.BlockSpec(memory_space=pltpu.SMEM)]
            + [in_vmem] * len(blocks)
            + [in_place] * len(streamed),
            out_specs=(in_vmem,) * len(outs) + (in_place,) * len(kept),
            scratch_shapes=scratch + weights + [pltpu.SemaphoreType.DMA((96,))],
            compiler_params=pltpu.CompilerParams(vmem_limit_bytes=VMEM_BYTES),
            cost_estimate=pl.CostEstimate(flops=flops, bytes_accessed=moved, transcendentals=0),
            name=name,
        )(place, *blocks, *(in_hbm(value) for value in streamed))

    return run


def weight_scratch(pieces):
    if len(pieces) == 1:
        return pltpu.VMEM(pieces[0].shape, LOW)
    _, count, rows, quarter = pieces[0].shape
    return pltpu.VMEM((count, 4, rows, 4 * quarter), LOW)


def route(kernel, outs, name, place, blocks, whole=False, scratch=()):
    def spec(dims):
        if whole:
            return pl.BlockSpec(memory_space=pltpu.VMEM)
        return pl.BlockSpec((1,) + tuple(dims[1:]), lambda step: (step,) + (0,) * (len(dims) - 1))

    return pl.pallas_call(
        kernel,
        grid=() if whole else (blocks[0].shape[0],),
        out_shape=outs,
        in_specs=[pl.BlockSpec(memory_space=pltpu.SMEM)] + [spec(b.shape) for b in blocks],
        out_specs=tuple(spec(o.shape) for o in outs),
        scratch_shapes=scratch,
        compiler_params=pltpu.CompilerParams(vmem_limit_bytes=VMEM_BYTES),
        name=name,
    )(place, *blocks)


def shape(dims, dtype=LOW):
    return jax.ShapeDtypeStruct(dims, dtype)


SWAP = ((0, 1), (1, 0))


def swapped(value, axis):
    return lax.ppermute(value, axis, SWAP)


def added(left, right, dtype=LOW):
    return (left.astype(HIGH) + right.astype(HIGH)).astype(dtype)


def picked(value, index, axis):
    return lax.dynamic_index_in_dim(value, index, axis, keepdims=False)


def tied(value):
    return lax.optimization_barrier(value)


def synced(groups, *others):
    states, others = tied(([group.state for group in groups], others))
    for group, state in zip(groups, states):
        group.state = state
    return others if len(others) != 1 else others[0]


def shifted(value, distance):
    count = lax.axis_size("z")
    return lax.ppermute(value, "z", [(k, (k - distance) % count) for k in range(count)])


FEW = 4


class Sum:
    def __init__(self, place, keep, send, name):
        self.place, self.name = place, name
        self.count = lax.axis_size("z")
        self.rows = keep.shape[0] // (self.count * 4)
        self.halves = (keep.shape[1],)
        self.state = (keep, swapped(send, "core"))

    def joined(self, other):
        self.halves += other.halves
        self.state += other.state

    def first(self):
        part = shape((self.count, 2, self.rows, sum(self.halves) // 2))
        left, left_keep, right, right_keep = route(
            first_route_kernel, (part,) * 4, self.name + "_first", self.place,
            [value.reshape(self.count, 2, 2, self.rows, -1) for value in self.state],
        )
        self.state = (left_keep, left, right_keep, right)

    def first_sent(self):
        left_keep, left, right_keep, right = self.state
        self.state = (left_keep, swapped(left, "y"), right_keep, swapped(right, "x"))

    def second(self):
        self.half = sum(self.halves)
        part = shape((self.count, self.rows, self.half // 2))
        left, left_keep, right, right_keep = route(
            second_route_kernel, (part,) * 4, self.name + "_second", self.place, self.state
        )
        self.state = (left_keep, left, right_keep, right)

    def second_sent(self):
        left_keep, left, right_keep, right = self.state
        self.state = (left_keep, swapped(left, "x"), right_keep, swapped(right, "y"))

    def third(self):
        one = (self.rows, self.half)
        if self.count > FEW:
            outs = (shape((self.count, *one)),)
        else:
            outs = (shape(one, HIGH),) + (shape(one),) * (self.count - 1)
        self.state = tuple(route(third_route_kernel, outs, self.name + "_third", self.place, self.state, True))

    def third_sent(self):
        mine, *sends = self.state
        if sends:
            self.state = (mine, *(shifted(send, -1 - k) for k, send in enumerate(sends)))
        else:
            arrived = lax.all_to_all(mine, "z", split_axis=0, concat_axis=0, tiled=True)
            self.state = (arrived.astype(HIGH).sum(0),)

    def last(self):
        part = shape((self.rows // 2, self.half), HIGH)
        mine, other = route(last_kernel, (part, part), self.name + "_last", self.place, self.state, True)
        self.state = (mine, swapped(other, "core"))

    def owned(self, spans):
        rows = self.rows // 2
        outs = tuple(
            shape((ROWS_OF_VECTORS, rows) if stop is None else (rows, stop - start), HIGH)
            for _, start, stop in spans
        )
        spans = tuple((which, start, start + LANES if stop is None else stop) for which, start, stop in spans)
        kernel = functools.partial(owned_kernel, self.halves, spans)
        table = [pltpu.VMEM((LANES, LANES), HIGH)]
        return route(kernel, outs, self.name + "_owned", self.place, self.state, True, table)


class Spread:
    def __init__(self, place, chip):
        self.place = place
        self.state = chip
        self.rows, self.half = chip.shape

    def first(self):
        count = lax.axis_size("z")
        if count > FEW:
            column = jnp.broadcast_to(self.state[None], (count, self.rows, self.half))
            self.state = lax.all_to_all(column, "z", split_axis=0, concat_axis=0, tiled=True)
        else:
            self.state = (self.state, *(shifted(self.state, k) for k in range(1, count)))

    def second(self):
        if isinstance(self.state, tuple):
            part = shape((len(self.state), self.rows, self.half // 2))
            left, right = route(arranged_kernel, (part, part), "arranged", self.place, self.state, True)
        else:
            left, right = self.state[..., : self.half // 2], self.state[..., self.half // 2 :]
        self.state = (left, swapped(left, "x"), right, swapped(right, "y"))

    def third(self):
        left, right = jnp.stack(self.state[:2]), jnp.stack(self.state[2:])
        own = (left, swapped(left, "y"), right, swapped(right, "x"))
        self.state = own + (swapped(left, "core"), swapped(right, "core"))

    def fourth(self):
        left, left_got, right, right_got, left_far, right_far = self.state
        far = (left_far, swapped(left_got, "core"), right_far, swapped(right_got, "core"))
        self.state = (left, left_got, right, right_got) + far

    def pieces(self):
        if self.rows % 16 == 0:
            return self.state
        core, x, y = lax.axis_index("core"), lax.axis_index("x"), lax.axis_index("y")

        def placed(near, far, side):
            piece = jnp.stack([near, far], side)
            piece = jnp.where(y == 0, piece, piece[::-1])
            return jnp.where(x == 0, piece, piece[:, ::-1])

        own, far = (
            jnp.concatenate(
                [placed(*self.state[k : k + 2], 0), placed(*self.state[k + 2 : k + 4], 1)], -1
            )
            for k in (0, 4)
        )
        whole = jnp.where(core == 0, jnp.concatenate([own, far], -1), jnp.concatenate([far, own], -1))
        return (whole.transpose(2, 1, 0, 3, 4).reshape(-1, 2 * self.half),)


def regrouped(tokens):
    return lax.all_to_all(tokens, ("y", "core"), split_axis=0, concat_axis=0, tiled=True)


def in_quarters(tokens, quarters, pad):
    _, frames, places, width = tokens.shape
    tokens = tokens.reshape(frames, quarters, places // quarters, width).swapaxes(0, 1)
    return jnp.pad(tokens, ((0, 0), (0, 0), (0, pad - places // quarters), (0, 0)))


def body(
    clips, time_gain, time_shift, time_heads, time_merge, merge_bias, time_mixer, mixer_bias,
    space_gain, space_shift, space_heads, space_merge, space_bias,
    feed_gain, feed_shift, feed_expand, expand_bias, feed_reduce, reduce_bias, cotangent,
):
    everyone = ("z", "x", "y", "core")
    _, near, all_places, width = clips.shape
    quarters = lax.axis_size("y") * lax.axis_size("core")
    frames, places = near * quarters, all_places // quarters
    pad = -(-places // 8) * 8
    rows = frames * pad
    hidden = feed_expand.shape[1]
    blocks = hidden // width
    share = feed_expand.shape[0]
    count = width // share
    core = lax.axis_index("core")
    place = jnp.stack([core, *(lax.axis_index(axis) for axis in ("x", "y", "z"))]).astype(jnp.int32)

    tall, tokens = (rows, width), (frames, pad, width)
    tiles = (width // LANES, rows, LANES)
    token_flops = 2 * rows * width * width
    vec_shape = shape((ROWS_OF_VECTORS, width), HIGH)
    space_half = 2 * width

    clips_in = in_quarters(clips, quarters, pad)
    by_place = regrouped(clips_in).reshape(tokens)
    vectors = jnp.concatenate(
        [
            jnp.stack(
                [
                    time_gain, time_shift, merge_bias, mixer_bias, space_gain, space_shift, space_bias,
                    feed_gain, feed_shift, reduce_bias,
                ]
            ),
            expand_bias.reshape(blocks, share),
        ],
        0,
    )
    time_half = 5 * width // 2 + LANES
    time_part, space_part = shape((share, time_half)), shape((share, space_half))
    sources = (time_heads, time_merge, time_mixer, space_heads, space_merge)
    time_mine, time_send, space_mine, space_send = call(
        prepare_kernel,
        (time_part, time_part, space_part, space_part),
        (),
        [pltpu.VMEM(source.shape, LOW) for source in sources] + [pltpu.VMEM((LANES, LANES), HIGH)],
        0,
        "prepare",
    )(place, (vectors,), sources, [])

    def spread(mine, send):
        got = swapped(send, "core")
        chip = jnp.where(core == 0, jnp.concatenate([mine, got], 0), jnp.concatenate([got, mine], 0))
        return Spread(place, chip)

    time = spread(time_mine, time_send)
    feed_expand, feed_reduce, cotangent = synced([time], feed_expand, feed_reduce, cotangent)
    time.first()
    space = spread(space_mine, space_send)
    expand = feed_expand.reshape(share, count, blocks, share).swapaxes(1, 2).reshape(share, hidden)
    feed_pack = jnp.concatenate([expand, *feed_reduce.reshape(blocks, share, width)], 1)
    feed_pack, by_place = synced([time, space], feed_pack, by_place)
    feed = lax.all_gather(feed_pack, everyone, axis=0, tiled=True)
    time.second()
    space.first()
    upstream_in = in_quarters(cotangent, quarters, pad)
    upstream_in = synced([time, space], upstream_in)
    time.third()
    synced([time])
    time.fourth()
    space.second()
    synced([time, space])
    space.third()
    low, high = pltpu.VMEM(tall, LOW), pltpu.VMEM(tall, HIGH)
    wide = pltpu.VMEM((rows, 3 * width), LOW)
    branch, vec, *time_kept = call(
        time_forward_kernel,
        (shape(tokens), vec_shape),
        (shape(tall), shape(wide.shape), shape(tall), shape(tall)),
        [pltpu.VMEM(tiles, HIGH), low, wide, low, low],
        6 * token_flops,
        "time_forward",
    )(place, (by_place,), time.pieces(), [weight_scratch(time.pieces())])
    branch = synced([space], branch)
    by_frame = regrouped(branch.reshape(clips_in.shape))
    space.fourth()
    after_space, *space_kept = call(
        functools.partial(space_forward_kernel, all_places),
        (shape(tall, HIGH),),
        (shape(tall, HIGH), shape(tall), shape(wide.shape), shape(tall)),
        [high, high, low, wide, low],
        6 * token_flops,
        "space_forward",
    )(place, (clips_in, by_frame, vec), space.pieces(), [weight_scratch(space.pieces())])
    space_sum, feed_vec, last_keep, last_send, result, feed_grad = call(
        feed_kernel,
        (shape(tall, HIGH), vec_shape, shape((width, width)), shape((width, width))),
        (shape(clips_in.shape), shape((width, 2 * (hidden - width)))),
        [high, low, low, high, high, pltpu.VMEM(clips_in.shape, LOW)],
        24 * token_flops,
        "feed",
    )(
        place, (after_space, upstream_in, vec), (feed,),
        [pltpu.VMEM((blocks, 2, width, width), LOW), pltpu.VMEM((2, 2, width, width), LOW)],
    )
    feed_owned = lax.psum_scatter(feed_grad, everyone, scatter_dimension=0, tiled=True)
    last_sums = Sum(place, last_keep, last_send, "last")
    time_round, space_keep, space_send, space_vec, time_sum = call(
        functools.partial(space_backward_kernel, all_places),
        (shape(clips_in.shape), shape((width, space_half)), shape((width, space_half)), vec_shape),
        (shape(tall, HIGH),),
        [high, low, wide, low, high, low, low, wide],
        12 * token_flops,
        "space_backward",
    )(place, (space_sum, vec), (*space_kept, *space.pieces()), [weight_scratch(space.pieces())])
    space_sums = Sum(place, space_keep, space_send, "space")
    time_round = regrouped(time_round)
    space_sums.joined(last_sums)
    space_sums.first()
    space_sums.first_sent()
    inward, time_keep, time_send = call(
        time_backward_kernel,
        (shape(tokens), shape((width, time_half)), shape((width, time_half))),
        (),
        [
            pltpu.VMEM(tokens, LOW), low, wide, low, low,
            pltpu.VMEM(tiles, HIGH), low, low, wide, pltpu.VMEM((LANES, width), HIGH),
        ],
        14 * token_flops,
        "time_backward",
    )(
        place, (time_round.reshape(tokens), vec, space_vec, feed_vec),
        (by_place, *time_kept, *time.pieces()), [weight_scratch(time.pieces())],
    )
    inward, time_keep, time_send = synced([space_sums], inward, time_keep, time_send)
    time_sums = Sum(place, time_keep, time_send, "time")
    space_sums.second()
    space_sums.second_sent()
    time_sums.first()
    synced([time_sums, space_sums])
    time_sums.first_sent()
    space_sums.third()
    space_sums.third_sent()
    time_sums.second()
    synced([time_sums, space_sums])
    time_sums.second_sent()
    inward = synced([time_sums], inward)
    time_sums.third()
    time_sums.third_sent()
    entry_round = regrouped(inward.reshape(clips_in.shape))
    time_sum = time_sum.reshape(near, quarters, pad, width)
    grad_clips = (time_sum + entry_round.swapaxes(0, 1).astype(HIGH)).astype(LOW)
    grad_clips = grad_clips[:, :, :places].reshape(clips.shape)
    layer_output = result[:, :, :places].swapaxes(0, 1).reshape(clips.shape)
    layer_output, grad_clips = synced([time_sums, space_sums], layer_output, grad_clips)
    space_sums.last()
    time_sums.last()
    grad_space_heads, grad_space_merge, last_expand, last_reduce = space_sums.owned(
        [(0, 0, 3 * width), (0, 3 * width, 4 * width), (1, 0, width), (1, width, 2 * width)]
    )
    grad_time_heads, grad_time_merge, grad_time_mixer, vector_grads = time_sums.owned(
        [(0, 0, 3 * width), (0, 3 * width, 4 * width), (0, 4 * width, 5 * width), (0, 5 * width, None)]
    )
    vector_grads = vector_grads[:VECTORS]
    if share % 8 == 0:
        grad_expand, grad_reduce = route(
            feed_owned_kernel, (shape((share, hidden), HIGH), shape((blocks * share, width), HIGH)), "feed_owned",
            place, (feed_owned, last_expand, last_reduce), True, [pltpu.VMEM((LANES, hidden), HIGH), pltpu.VMEM((hidden, LANES), HIGH)],
        )
    else:
        feed_owned = feed_owned.astype(HIGH)
        before = hidden - width
        grad_expand = jnp.concatenate([feed_owned[:, :before], last_expand], 1)
        grad_expand = grad_expand.reshape(share, blocks, count, share).swapaxes(1, 2).reshape(share, hidden)
        grad_reduce = [feed_owned[:, before + k * width : before + (k + 1) * width] for k in range(blocks - 1)]
        grad_reduce = jnp.concatenate([*grad_reduce, last_reduce], 0)
    return (
        layer_output,
        grad_clips,
        vector_grads[TIME_GAIN],
        vector_grads[TIME_SHIFT],
        grad_time_heads,
        grad_time_merge,
        vector_grads[MERGE_BIAS],
        grad_time_mixer,
        vector_grads[MIXER_BIAS],
        vector_grads[SPACE_GAIN],
        vector_grads[SPACE_SHIFT],
        grad_space_heads,
        grad_space_merge,
        vector_grads[SPACE_BIAS],
        vector_grads[FEED_GAIN],
        vector_grads[FEED_SHIFT],
        grad_expand,
        vector_grads[EXPAND_BIAS:].reshape(-1),
        grad_reduce,
        vector_grads[REDUCE_BIAS],
    )


def solution(mesh):
    clip, st = mesh.shape["clip"], mesh.shape["st"]
    finer = Mesh(mesh.devices.reshape(clip // 2, 2, st // 2, 2), ("z", "x", "y", "core"))
    token = P(("z", "x"), ("y", "core"), None, None)
    vec = P(("z", "x", "y", "core"))
    mat = P(("z", "x", "y", "core"), None)
    in_specs = (
        token, vec, vec, mat, mat, vec, mat, vec, vec, vec, mat, mat, vec, vec, vec, mat, vec, mat, vec, token,
    )
    out_specs = (
        token, token, vec, vec, mat, mat, vec, mat, vec, vec, vec, mat, mat, vec, vec, vec, mat, vec, mat, vec,
    )
    return jax.shard_map(body, mesh=finer, in_specs=in_specs, out_specs=out_specs, check_vma=False)
```

```python
import functools

import jax
import jax.numpy as jnp
from jax import lax
from jax.experimental import pallas as pl
from jax.experimental.pallas import tpu as pltpu
from jax.sharding import Mesh
from jax.sharding import PartitionSpec as P

HEADS = 12
HEAD_DIM = 64
LANES = 128
EPSILON = 1e-06
SCALE = 0.125
ROOT_HALF = 0.7071067811865476
DENSITY = 0.3989422804014327
LOW = jnp.bfloat16
HIGH = jnp.float32
TIME_BLOCK = 112
VMEM_BYTES = 28 * 1024 * 1024

TIME_GAIN, TIME_SHIFT, MERGE_BIAS, MIXER_BIAS = 0, 1, 2, 3
SPACE_GAIN, SPACE_SHIFT, SPACE_BIAS = 4, 5, 6
FEED_GAIN, FEED_SHIFT, REDUCE_BIAS, EXPAND_BIAS = 7, 8, 9, 10
VECTORS = 14
ROWS_OF_VECTORS = 16


def dot(left, right):
    return jnp.dot(left, right, preferred_element_type=HIGH)


def dot_nt(left, right):
    return lax.dot_general(left, right, (((1,), (1,)), ((), ())), preferred_element_type=HIGH)


def dot_tn(left, right):
    return lax.dot_general(left, right, (((0,), (0,)), ((), ())), preferred_element_type=HIGH)


def norm(values, gain, shift):
    centred = values - jnp.mean(values, -1, keepdims=True)
    inverse = lax.rsqrt(jnp.mean(centred * centred, -1, keepdims=True) + EPSILON)
    normed = centred * inverse
    return normed * gain + shift, normed, inverse


def norm_back(upstream, normed, inverse, gain):
    scaled = upstream * gain
    return inverse * (
        scaled
        - jnp.mean(scaled, -1, keepdims=True)
        - normed * jnp.mean(scaled * normed, -1, keepdims=True)
    )


def column_sum(values):
    return jnp.sum(values, 0, keepdims=True)


class Mover:
    def __init__(self, sems):
        self.sems, self.used = sems, 0

    def start(self, source, target):
        copy = pltpu.make_async_copy(source, target, self.sems.at[self.used])
        self.used += 1
        copy.start()
        return copy

    def start_rows(self, source, target, parts=7):
        return [self.start(source, target)]


def finished(copies):
    for copy in copies:
        copy.wait()


def stacked(pair, scale=1.0):
    lane = lax.broadcasted_iota(jnp.int32, (1, LANES), 1)
    first = jnp.where(lane < HEAD_DIM, scale, 0.0).astype(LOW)
    second = jnp.where(lane < HEAD_DIM, 0.0, scale).astype(LOW)
    return jnp.concatenate([pair * first, pair * second], 0)


def joined(both):
    rows = both.shape[0] // 2
    lane = lax.broadcasted_iota(jnp.int32, (rows, LANES), 1)
    return jnp.where(lane < HEAD_DIM, both[:rows], both[rows:])


def shares_of(queries, key_rows, valid):
    scores = jnp.where(valid, dot_nt(queries, key_rows), -1e30)
    raised = jnp.exp(scores - jnp.max(scores, -1, keepdims=True))
    return raised * (1.0 / jnp.sum(raised, -1, keepdims=True))


def pair_forward(packed_ref, mixed_ref, rows, pair, width, valid):
    at = [slice(pair * LANES + part * width, (pair + 1) * LANES + part * width) for part in range(3)]
    queries = stacked(packed_ref[rows, at[0]], SCALE)
    shares = shares_of(queries, packed_ref[rows, at[1]], valid)
    mixed = dot(shares.astype(LOW), packed_ref[rows, at[2]])
    mixed_ref[rows, at[0]] = joined(mixed).astype(LOW)


def pair_backward(packed_ref, up_ref, grad_ref, rows, pair, width, valid):
    at = [slice(pair * LANES + part * width, (pair + 1) * LANES + part * width) for part in range(3)]
    queries = stacked(packed_ref[rows, at[0]], SCALE)
    key_rows = packed_ref[rows, at[1]]
    upstream = stacked(up_ref[rows, at[0]])
    scores = jnp.where(valid, dot_nt(key_rows, queries), -1e30)
    raised = jnp.exp(scores - jnp.max(scores, 0, keepdims=True))
    shares = raised * (1.0 / jnp.sum(raised, 0, keepdims=True))
    grad_shares = dot_nt(packed_ref[rows, at[2]], upstream)
    grad_scores = (
        shares * (grad_shares - jnp.sum(grad_shares * shares, 0, keepdims=True))
    ).astype(LOW)
    grad_ref[rows, at[0]] = (joined(dot_tn(grad_scores, key_rows)) * SCALE).astype(LOW)
    grad_ref[rows, at[1]] = dot(grad_scores, queries).astype(LOW)
    grad_ref[rows, at[2]] = dot(shares.astype(LOW), upstream).astype(LOW)


def time_valid(block, frames, turned=False):
    dims = (block, 2 * block) if turned else (2 * block, block)
    row = lax.broadcasted_iota(jnp.int32, dims, 0)
    col = lax.broadcasted_iota(jnp.int32, dims, 1)
    return (row % block) // frames == (col % block) // frames


def space_valid(rows, pad, places, turned=False):
    dims = (rows, 2 * rows) if turned else (2 * rows, rows)
    return lax.broadcasted_iota(jnp.int32, dims, 0 if turned else 1) % pad < places


def vector(vec_ref, row):
    return vec_ref[row : row + 1, :]


def to_places(tokens_ref, tiles_ref):
    frames, places, width = tokens_ref.shape
    for frame in range(frames):
        rows = tokens_ref[frame].astype(HIGH)
        for tile in range(width // LANES):
            at = slice(tile * LANES, (tile + 1) * LANES)
            tiles_ref[tile, pl.ds(frame, places, stride=frames), :] = rows[:, at]
    return jnp.concatenate([tiles_ref[tile] for tile in range(width // LANES)], 1)


def from_places(values, tiles_ref, tokens_ref):
    frames, places, width = tokens_ref.shape
    for tile in range(width // LANES):
        tiles_ref[tile] = values[:, tile * LANES : (tile + 1) * LANES]
    for frame in range(frames):
        for tile in range(width // LANES):
            at = slice(tile * LANES, (tile + 1) * LANES)
            rows = tiles_ref[tile, pl.ds(frame, places, stride=frames), :]
            tokens_ref[frame, :, at] = rows.astype(LOW)


def to_frames(tokens_ref, held_ref):
    quarters, frames, places, _ = tokens_ref.shape
    for frame in range(frames):
        for quarter in range(quarters):
            start = (frame * quarters + quarter) * places
            held_ref[start : start + places, :] = tokens_ref[quarter, frame].astype(held_ref.dtype)


def from_frames(held_ref, tokens_ref):
    quarters, frames, places, _ = tokens_ref.shape
    for frame in range(frames):
        for quarter in range(quarters):
            start = (frame * quarters + quarter) * places
            tokens_ref[quarter, frame] = held_ref[start : start + places, :].astype(LOW)


def weight_copies(place_ref, pieces, weight_ref, mover):
    if len(pieces) == 1:
        return [mover.start(pieces[0], weight_ref)]
    core, x, y = place_ref[0], place_ref[1], place_ref[2]
    quarter = pieces[0].shape[-1]
    copies = []
    for number, piece in enumerate(pieces):
        whose, side, far = number // 4, number // 2 % 2, number % 2
        half = core if whose == 0 else 1 - core
        start = pl.multiple_of(half * (2 * quarter) + side * quarter, LANES)
        for near in range(2):
            far_y, far_x = (far, near) if side == 0 else (near, far)
            at_x = 1 - x if far_x else x
            at_y = 1 - y if far_y else y
            target = weight_ref.at[:, at_x * 2 + at_y, :, pl.ds(start, quarter)]
            copies.append(mover.start(piece.at[near], target))
    return copies


def columns_of(weight_ref, at):
    if len(weight_ref.shape) == 2:
        return weight_ref[:, at]
    value = weight_ref[:, :, :, at]
    return value.reshape(-1, value.shape[-1])


def put(core, half, keep_ref, send_ref, at, value):
    @pl.when(core == half)
    def _():
        keep_ref[:, at] = value

    @pl.when(core != half)
    def _():
        send_ref[:, at] = value


def time_forward_kernel(place_ref, tokens_ref, *refs):
    *pieces, branch_ref = refs[:-13]
    *kept, tiles_ref, entry_ref, packed_ref, mixed_ref, middle_ref, vec_ref, weight_ref, sems = refs[-13:]
    frames, _, width = tokens_ref.shape
    rows = entry_ref.shape[0]
    mover = Mover(sems)
    copies = weight_copies(place_ref, pieces, weight_ref, mover)
    tokens = to_places(tokens_ref, tiles_ref)
    finished(copies)
    vec_at = slice(5 * width, 5 * width + LANES)
    vec_ref[...] = jnp.transpose(columns_of(weight_ref, vec_at).astype(HIGH))[:ROWS_OF_VECTORS]
    entry, _, _ = norm(tokens, vector(vec_ref, TIME_GAIN), vector(vec_ref, TIME_SHIFT))
    entry_ref[...] = entry.astype(LOW)
    stores = mover.start_rows(entry_ref, kept[0]) + [mover.start(vec_ref, kept[4])]
    for part in range(3):
        at = slice(part * width, (part + 1) * width)
        packed_ref[:, at] = dot(entry_ref[...], columns_of(weight_ref, at)).astype(LOW)
    stores += mover.start_rows(packed_ref, kept[1])
    valid = time_valid(TIME_BLOCK, frames)

    for pair in range(HEADS // 2):
        for start in range(0, rows, TIME_BLOCK):
            pair_forward(packed_ref, mixed_ref, slice(start, start + TIME_BLOCK), pair, width, valid)
    stores += mover.start_rows(mixed_ref, kept[2])
    merge = columns_of(weight_ref, slice(3 * width, 4 * width))
    middle_ref[...] = (dot(mixed_ref[...], merge) + vector(vec_ref, MERGE_BIAS)).astype(LOW)
    stores += mover.start_rows(middle_ref, kept[3])
    mixer = columns_of(weight_ref, slice(4 * width, 5 * width))
    branch = dot(middle_ref[...], mixer) + vector(vec_ref, MIXER_BIAS)
    from_places(branch, tiles_ref, branch_ref)
    finished(stores)


def space_forward_kernel(all_places, place_ref, clips_ref, branch_ref, vec_in, *refs):
    pieces = refs[:-13]
    *kept, held_ref, after_time_ref, entry_ref, packed_ref, mixed_ref, vec_ref, weight_ref, sems = refs[-13:]
    quarters, frames, pad, width = clips_ref.shape
    rows = held_ref.shape[0]
    mover = Mover(sems)
    vec_copy = mover.start(vec_in, vec_ref)
    copies = weight_copies(place_ref, pieces, weight_ref, mover)
    to_frames(clips_ref, after_time_ref)
    to_frames(branch_ref, held_ref)
    after_time = after_time_ref[...] + held_ref[...]
    after_time_ref[...] = after_time
    stores = mover.start_rows(after_time_ref, kept[0])
    vec_copy.wait()
    entry, _, _ = norm(after_time, vector(vec_ref, SPACE_GAIN), vector(vec_ref, SPACE_SHIFT))
    entry_ref[...] = entry.astype(LOW)
    stores += mover.start_rows(entry_ref, kept[1])
    finished(copies)
    for part in range(3):
        at = slice(part * width, (part + 1) * width)
        packed_ref[:, at] = dot(entry_ref[...], columns_of(weight_ref, at)).astype(LOW)
    stores += mover.start_rows(packed_ref, kept[2])
    each = rows // frames
    valid = space_valid(each, pad, all_places // quarters)

    for pair in range(HEADS // 2):
        for start in range(0, rows, each):
            pair_forward(packed_ref, mixed_ref, slice(start, start + each), pair, width, valid)
    stores += mover.start_rows(mixed_ref, kept[3])
    merge = columns_of(weight_ref, slice(3 * width, 4 * width))
    held_ref[...] = after_time_ref[...] + dot(mixed_ref[...], merge) + vector(vec_ref, SPACE_BIAS)
    stores += mover.start_rows(held_ref, kept[4])
    finished(stores)


def feed_kernel(
    place_ref, upstream_ref, after_space_in, vec_in, weight_ref,
    keep_ref, send_ref, result_ref, space_sum_ref, vec_out, grad_ref,
    held_ref, up_ref, entry_ref, out_ref, back_ref, results_ref, after_space_ref, vec_ref, grad_vec_ref,
    weights_ref, grads_ref, sems,
):
    width = after_space_ref.shape[-1]
    half = weight_ref.shape[1] // 2
    blocks = half // width
    mover = Mover(sems)
    first = [mover.start(vec_in, vec_ref), mover.start(after_space_in, after_space_ref)]

    def columns(side, block, whole=half):
        return pl.ds(side * whole + block * width, width)

    def load(block):
        return [
            copy
            for side in range(2)
            for copy in mover.start_rows(weight_ref.at[:, columns(side, block)], weights_ref.at[block, side], 4)
        ]

    loads = [load(block) for block in range(blocks)]
    to_frames(upstream_ref, held_ref)
    up_ref[...] = held_ref[...].astype(LOW)
    finished(first)
    gain, shift = vector(vec_ref, FEED_GAIN), vector(vec_ref, FEED_SHIFT)
    entry, _, _ = norm(after_space_ref[...], gain, shift)
    entry_ref[...] = entry.astype(LOW)
    grad_vec_ref[...] = jnp.zeros_like(grad_vec_ref)
    stores = []
    for block in range(blocks):
        finished(loads[block])
        expand, reduce = weights_ref[block, 0], weights_ref[block, 1]
        hidden = dot(entry_ref[...], expand) + vector(vec_ref, EXPAND_BIAS + block)
        normal = 0.5 * (1.0 + lax.erf(hidden * ROOT_HALF))
        active = (hidden * normal).astype(LOW)
        out = dot(active, reduce)
        slope = normal + hidden * DENSITY * jnp.exp(-0.5 * hidden * hidden)
        hidden_grad = (dot_nt(up_ref[...], reduce) * slope).astype(LOW)
        back = dot_nt(hidden_grad, expand)
        if block:
            out_ref[...] += out
            back_ref[...] += back
        else:
            out_ref[...] = after_space_ref[...] + vector(vec_ref, REDUCE_BIAS) + out
            back_ref[...] = back
        grad_vec_ref[3 + block : 4 + block, :] = column_sum(hidden_grad.astype(HIGH))
        expand_grad = dot_tn(entry_ref[...], hidden_grad).astype(LOW)
        reduce_grad = dot_tn(active, up_ref[...]).astype(LOW)
        if block == blocks - 1:
            put(place_ref[0], 0, keep_ref, send_ref, slice(0, width), expand_grad)
            put(place_ref[0], 1, keep_ref, send_ref, slice(0, width), reduce_grad)
            continue
        if block > 1:
            finished(stores[2 * block - 4 : 2 * block - 2])
        grads_ref[block % 2, 0] = expand_grad
        grads_ref[block % 2, 1] = reduce_grad
        for side in range(2):
            target = grad_ref.at[:, columns(side, block, half - width)]
            stores.append(mover.start(grads_ref.at[block % 2, side], target))
    from_frames(out_ref, results_ref)
    stores.append(mover.start(results_ref, result_ref))
    _, normed, inverse = norm(after_space_ref[...], gain, shift)
    upstream = back_ref[...]
    grad_vec_ref[0:1, :] = column_sum(upstream * normed)
    grad_vec_ref[1:2, :] = column_sum(upstream)
    grad_vec_ref[2:3, :] = column_sum(held_ref[...])
    back_ref[...] = held_ref[...] + norm_back(upstream, normed, inverse, gain)
    stores += [mover.start(back_ref, space_sum_ref), mover.start(grad_vec_ref, vec_out)]
    finished(stores[2 * blocks - 6 :])


def space_backward_kernel(all_places, place_ref, space_sum_in, vec_in, *refs):
    *kept, time_round_ref, keep_ref, send_ref, time_sum_ref, vec_out = refs[:-13]
    kept, pieces = kept[:4], kept[4:]
    *held, sum_ref, round_ref, up_ref, grad_ref, space_sum_ref, vec_ref, grad_vec_ref, weight_ref, sems = refs[-13:]
    after_time_ref, entry_ref, packed_ref, mixed_ref = held
    rows, width = space_sum_ref.shape
    quarters, frames, pad, _ = time_round_ref.shape
    core = place_ref[0]
    half = keep_ref.shape[1]
    mover = Mover(sems)
    first = [mover.start(space_sum_in, space_sum_ref), mover.start(vec_in, vec_ref)]
    mixed_copies = mover.start_rows(kept[3], mixed_ref)
    copies = weight_copies(place_ref, pieces, weight_ref, mover)
    packed_copies = mover.start_rows(kept[2], packed_ref)
    others = mover.start_rows(kept[1], entry_ref) + mover.start_rows(kept[0], after_time_ref)
    finished(first)
    round_ref[...] = space_sum_ref[...].astype(LOW)
    finished(mixed_copies)
    put(core, 1, keep_ref, send_ref, slice(half - width, half), dot_tn(mixed_ref[...], round_ref[...]).astype(LOW))
    finished(copies)
    up_ref[...] = dot_nt(round_ref[...], columns_of(weight_ref, slice(3 * width, 4 * width))).astype(LOW)
    each = rows // frames
    valid = space_valid(each, pad, all_places // quarters, True)
    finished(packed_copies)

    for pair in range(HEADS // 2):
        for start in range(0, rows, each):
            pair_backward(packed_ref, up_ref, grad_ref, slice(start, start + each), pair, width, valid)
    finished(others)
    back = dot_nt(grad_ref[:, 0:width], columns_of(weight_ref, slice(0, width)))
    for part in range(1, 3):
        at = slice(part * width, (part + 1) * width)
        back += dot_nt(grad_ref[:, at], columns_of(weight_ref, at))
    gain = vector(vec_ref, SPACE_GAIN)
    _, normed, inverse = norm(after_time_ref[...], gain, vector(vec_ref, SPACE_SHIFT))
    sum_ref[...] = space_sum_ref[...] + norm_back(back, normed, inverse, gain)
    stores = mover.start_rows(sum_ref, time_sum_ref)
    from_frames(sum_ref, time_round_ref)
    grad_vec_ref[...] = jnp.zeros_like(grad_vec_ref)
    grad_vec_ref[0:1, :] = column_sum(back * normed)
    grad_vec_ref[1:2, :] = column_sum(back)
    grad_vec_ref[2:3, :] = column_sum(round_ref[...].astype(HIGH))
    stores.append(mover.start(grad_vec_ref, vec_out))
    for part in range(3):
        at = slice(part * width, (part + 1) * width)
        value = dot_tn(entry_ref[...], grad_ref[:, at]).astype(LOW)
        start = part * width % half
        put(core, part * width // half, keep_ref, send_ref, slice(start, start + width), value)
    finished(stores)


def time_backward_kernel(place_ref, time_round_ref, vec_in, space_vec_in, feed_vec_in, *refs):
    *kept, inward_ref, keep_ref, send_ref = refs[:-15]
    kept, pieces = kept[:5], kept[5:]
    *held, tiles_ref, round_ref, up_ref, grad_ref, vectors_ref, vec_ref, space_vec_ref, feed_vec_ref, weight_ref, sems = refs[-15:]
    tokens_ref, entry_ref, packed_ref, mixed_ref, middle_ref = held
    frames, _, width = time_round_ref.shape
    rows = entry_ref.shape[0]
    core = place_ref[0]
    half = keep_ref.shape[1]
    mover = Mover(sems)
    middle_copies = mover.start_rows(kept[4], middle_ref)
    copies = weight_copies(place_ref, pieces, weight_ref, mover)
    mixed_copies, packed_copies = mover.start_rows(kept[3], mixed_ref), mover.start_rows(kept[2], packed_ref)
    others = mover.start_rows(kept[1], entry_ref) + mover.start_rows(kept[0], tokens_ref, 8)
    for source, target in ((vec_in, vec_ref), (space_vec_in, space_vec_ref), (feed_vec_in, feed_vec_ref)):
        others.append(mover.start(source, target))
    rounded = to_places(time_round_ref, tiles_ref)
    round_ref[...] = rounded.astype(LOW)
    vectors_ref[...] = jnp.zeros_like(vectors_ref)
    vectors_ref[MIXER_BIAS : MIXER_BIAS + 1, :] = column_sum(rounded)
    tail = 3 * width - half
    at = slice(tail + width, tail + 2 * width)
    finished(middle_copies)
    put(core, 1, keep_ref, send_ref, at, dot_tn(middle_ref[...], round_ref[...]).astype(LOW))
    finished(copies)
    up_ref[...] = dot_nt(round_ref[...], columns_of(weight_ref, slice(4 * width, 5 * width))).astype(LOW)
    vectors_ref[MERGE_BIAS : MERGE_BIAS + 1, :] = column_sum(up_ref[...].astype(HIGH))
    at = slice(tail, tail + width)
    finished(mixed_copies)
    put(core, 1, keep_ref, send_ref, at, dot_tn(mixed_ref[...], up_ref[...]).astype(LOW))
    up_ref[...] = dot_nt(up_ref[...], columns_of(weight_ref, slice(3 * width, 4 * width))).astype(LOW)
    valid = time_valid(TIME_BLOCK, frames, True)
    finished(packed_copies)

    for pair in range(HEADS // 2):
        for start in range(0, rows, TIME_BLOCK):
            pair_backward(packed_ref, up_ref, grad_ref, slice(start, start + TIME_BLOCK), pair, width, valid)
    finished(others)
    for start, stop in ((0, half), (half, 3 * width)):
        value = dot_tn(entry_ref[...], grad_ref[:, start:stop]).astype(LOW)
        put(core, start // half, keep_ref, send_ref, slice(0, stop - start), value)
    back = dot_nt(grad_ref[:, 0:width], columns_of(weight_ref, slice(0, width)))
    for part in range(1, 3):
        at = slice(part * width, (part + 1) * width)
        back += dot_nt(grad_ref[:, at], columns_of(weight_ref, at))
    tokens = to_places(tokens_ref, tiles_ref)
    gain = vector(vec_ref, TIME_GAIN)
    _, normed, inverse = norm(tokens, gain, vector(vec_ref, TIME_SHIFT))
    vectors_ref[TIME_GAIN : TIME_GAIN + 1, :] = column_sum(back * normed)
    vectors_ref[TIME_SHIFT : TIME_SHIFT + 1, :] = column_sum(back)
    for start, stop, source in ((SPACE_GAIN, FEED_GAIN, space_vec_ref), (FEED_GAIN, VECTORS, feed_vec_ref)):
        for row in range(start, stop):
            vectors_ref[row : row + 1, :] = source[row - start : row - start + 1, :]
    columns = jnp.transpose(vectors_ref[...]).astype(LOW)
    put(core, 1, keep_ref, send_ref, slice(half - 2 * LANES, half - LANES), columns)
    put(core, 1, keep_ref, send_ref, slice(half - LANES, half), jnp.zeros_like(columns))
    from_places(norm_back(back, normed, inverse, gain), tiles_ref, inward_ref)


def first_route_kernel(place_ref, *refs):
    *pairs, left_send, left_keep, right_send, right_keep = refs
    x, y = place_ref[1], place_ref[2]
    begin = 0
    for keep_ref, got_ref in zip(pairs[::2], pairs[1::2]):
        quarter = keep_ref.shape[-1] // 2
        left, right = slice(0, quarter), slice(quarter, 2 * quarter)
        to = slice(begin, begin + quarter)
        begin += quarter

        def total(at_x, at_y, columns):
            return added(keep_ref[0, at_x, at_y, :, columns], got_ref[0, at_x, at_y, :, columns])

        for other in range(2):
            left_send[0, other, :, to] = total(other, 1 - y, left)
            right_send[0, other, :, to] = total(1 - x, other, right)
            left_keep[0, other, :, to] = total(other, y, left)
            right_keep[0, other, :, to] = total(x, other, right)


def second_route_kernel(place_ref, *refs):
    *fours, left_send, left_keep, right_send, right_keep = refs
    x, y = place_ref[1], place_ref[2]
    begin = 0
    for at in range(0, len(fours), 4):
        left_ref, left_got, right_ref, right_got = fours[at : at + 4]
        to = slice(begin, begin + left_ref.shape[-1])
        begin = to.stop
        left_send[0, :, to] = added(left_ref[0, 1 - x], left_got[0, 1 - x])
        right_send[0, :, to] = added(right_ref[0, 1 - y], right_got[0, 1 - y])
        left_keep[0, :, to] = added(left_ref[0, x], left_got[0, x])
        right_keep[0, :, to] = added(right_ref[0, y], right_got[0, y])


def third_route_kernel(place_ref, left_ref, left_got, right_ref, right_got, *sends):
    quarter = left_ref.shape[-1]
    count = left_ref.shape[0]
    for distance, send in enumerate(sends):
        at = lax.rem(place_ref[3] + distance, count) if len(sends) > 1 else 0
        rows = at if len(sends) > 1 else slice(None)
        send[..., 0:quarter] = added(left_ref[rows], left_got[rows], send.dtype)
        send[..., quarter : 2 * quarter] = added(right_ref[rows], right_got[rows], send.dtype)


def last_kernel(place_ref, *refs):
    *parts, mine_ref, other_ref = refs
    total = sum(part[...].astype(HIGH) for part in parts)
    rows = mine_ref.shape[0]
    near, far = total[:rows], total[rows:]
    mine_ref[...] = jnp.where(place_ref[0] == 0, near, far)
    other_ref[...] = jnp.where(place_ref[0] == 0, far, near)


def owned_kernel(halves, spans, place_ref, mine_ref, other_ref, *refs):
    core = place_ref[0]
    half = sum(halves)
    outs, table_ref = refs[:-1], refs[-1]
    begin, wholes = 0, []
    for each in halves:
        quarters = [slice(at, at + each // 2) for at in (begin, half // 2 + begin)]
        begin += each // 2
        low = [jnp.where(core == 0, mine_ref[:, at], other_ref[:, at]) for at in quarters]
        high = [jnp.where(core == 0, other_ref[:, at], mine_ref[:, at]) for at in quarters]
        wholes.append(jnp.concatenate(low + high, 1))
    for (matrix, start, stop), out_ref in zip(spans, outs):
        value = wholes[matrix][:, start:stop]
        if out_ref.shape == value.shape:
            out_ref[...] = value
        else:
            table_ref[...] = jnp.zeros_like(table_ref)
            table_ref[0 : value.shape[0], :] = value
            out_ref[...] = jnp.transpose(table_ref[...])[: out_ref.shape[0], : out_ref.shape[1]]


def feed_owned_kernel(place_ref, owned_ref, last_expand_ref, last_reduce_ref, expand_ref, reduce_ref, table_ref, turned_ref):
    rows, hidden = expand_ref.shape
    width = reduce_ref.shape[1]
    blocks, count = hidden // width, width // rows
    before = hidden - width
    for block in range(blocks - 1):
        at = slice(before + block * width, before + (block + 1) * width)
        reduce_ref[block * rows : (block + 1) * rows, :] = owned_ref[:, at].astype(HIGH)
    reduce_ref[(blocks - 1) * rows :, :] = last_reduce_ref[...]
    table_ref[...] = jnp.zeros_like(table_ref)
    table_ref[0:rows, 0:before] = owned_ref[:, 0:before].astype(HIGH)
    table_ref[0:rows, before:] = last_expand_ref[...]
    turned = jnp.transpose(table_ref[...])
    for block in range(blocks):
        for owner in range(count):
            to = (owner * blocks + block) * rows
            at = block * width + owner * rows
            turned_ref[to : to + rows, :] = turned[at : at + rows]
    expand_ref[...] = jnp.transpose(turned_ref[...])[0:rows]


def arranged_kernel(place_ref, *refs):
    *blocks, left_ref, right_ref = refs
    count, _, quarter = left_ref.shape
    for distance, block in enumerate(blocks):
        at = lax.rem(place_ref[3] + distance, count)
        left_ref[at] = block[:, 0:quarter]
        right_ref[at] = block[:, quarter : 2 * quarter]


def prepare_kernel(place_ref, vectors_ref, *refs):
    *sources, time_mine, time_send, space_mine, space_send = refs[:-7]
    *held, table_ref, sems = refs[-7:]
    heads_ref, merge_ref, mixer_ref, space_heads_ref, space_merge_ref = held
    mover = Mover(sems)
    copies = [mover.start(source, target) for source, target in zip(sources, held)]
    width = merge_ref.shape[1]
    rows, half = time_mine.shape
    table_ref[...] = jnp.zeros_like(table_ref)
    table_ref[0 : vectors_ref.shape[0], 0:rows] = vectors_ref[...].astype(HIGH)
    columns = jnp.transpose(table_ref[...])[0:rows].astype(LOW)
    finished(copies)

    def fill(low, high, space_low, space_high):
        low[...] = heads_ref[:, 0:half]
        rest = 3 * width - half
        high[:, 0:rest] = heads_ref[:, half:]
        high[:, rest : rest + width] = merge_ref[...]
        high[:, rest + width : rest + 2 * width] = mixer_ref[...]
        high[:, half - 2 * LANES : half - LANES] = columns
        high[:, half - LANES :] = jnp.zeros_like(columns)
        space_half = space_low.shape[1]
        space_low[...] = space_heads_ref[:, 0:space_half]
        space_high[:, 0 : 3 * width - space_half] = space_heads_ref[:, space_half:]
        space_high[:, 3 * width - space_half :] = space_merge_ref[...]

    @pl.when(place_ref[0] == 0)
    def _():
        fill(time_mine, time_send, space_mine, space_send)

    @pl.when(place_ref[0] != 0)
    def _():
        fill(time_send, time_mine, space_send, space_mine)


def in_hbm(value):
    return pltpu.with_memory_space_constraint(value, pltpu.HBM)


def call(kernel, outs, kept, scratch, flops, name):
    def run(place, blocks, streamed, weights):
        args = (place, *blocks, *streamed)
        every = outs + kept
        moved = sum(a.size * a.dtype.itemsize for a in args)
        moved += sum(s.size * s.dtype.itemsize for s in every)
        in_vmem, in_place = pl.BlockSpec(memory_space=pltpu.VMEM), pl.BlockSpec(memory_space=pltpu.HBM)
        return pl.pallas_call(
            kernel,
            out_shape=outs + tuple(out if out.size > 3000000 else pltpu.HBM(out.shape, out.dtype) for out in kept),
            in_specs=[pl.BlockSpec(memory_space=pltpu.SMEM)]
            + [in_vmem] * len(blocks)
            + [in_place] * len(streamed),
            out_specs=(in_vmem,) * len(outs) + (in_place,) * len(kept),
            scratch_shapes=scratch + weights + [pltpu.SemaphoreType.DMA((96,))],
            compiler_params=pltpu.CompilerParams(vmem_limit_bytes=VMEM_BYTES),
            cost_estimate=pl.CostEstimate(flops=flops, bytes_accessed=moved, transcendentals=0),
            name=name,
        )(place, *blocks, *(in_hbm(value) for value in streamed))

    return run


def weight_scratch(pieces):
    if len(pieces) == 1:
        return pltpu.VMEM(pieces[0].shape, LOW)
    _, count, rows, quarter = pieces[0].shape
    return pltpu.VMEM((count, 4, rows, 4 * quarter), LOW)


def route(kernel, outs, name, place, blocks, whole=False, scratch=()):
    def spec(dims):
        if whole:
            return pl.BlockSpec(memory_space=pltpu.VMEM)
        return pl.BlockSpec((1,) + tuple(dims[1:]), lambda step: (step,) + (0,) * (len(dims) - 1))

    return pl.pallas_call(
        kernel,
        grid=() if whole else (blocks[0].shape[0],),
        out_shape=outs,
        in_specs=[pl.BlockSpec(memory_space=pltpu.SMEM)] + [spec(b.shape) for b in blocks],
        out_specs=tuple(spec(o.shape) for o in outs),
        scratch_shapes=scratch,
        compiler_params=pltpu.CompilerParams(vmem_limit_bytes=VMEM_BYTES),
        name=name,
    )(place, *blocks)


def shape(dims, dtype=LOW):
    return jax.ShapeDtypeStruct(dims, dtype)


SWAP = ((0, 1), (1, 0))


def swapped(value, axis):
    return lax.ppermute(value, axis, SWAP)


def added(left, right, dtype=LOW):
    return (left.astype(HIGH) + right.astype(HIGH)).astype(dtype)


def picked(value, index, axis):
    return lax.dynamic_index_in_dim(value, index, axis, keepdims=False)


def tied(value):
    return lax.optimization_barrier(value)


def synced(groups, *others):
    states, others = tied(([group.state for group in groups], others))
    for group, state in zip(groups, states):
        group.state = state
    return others if len(others) != 1 else others[0]


def shifted(value, distance):
    count = lax.axis_size("z")
    return lax.ppermute(value, "z", [(k, (k - distance) % count) for k in range(count)])


FEW = 4


class Sum:
    def __init__(self, place, keep, send, name):
        self.place, self.name = place, name
        self.count = lax.axis_size("z")
        self.rows = keep.shape[0] // (self.count * 4)
        self.halves = (keep.shape[1],)
        self.state = (keep, swapped(send, "core"))

    def joined(self, other):
        self.halves += other.halves
        self.state += other.state

    def first(self, kept_in=jax.ShapeDtypeStruct):
        part = shape((self.count, 2, self.rows, sum(self.halves) // 2))
        kept = kept_in(part.shape, part.dtype)
        left, left_keep, right, right_keep = route(
            first_route_kernel, (part, kept, part, kept), self.name + "_first", self.place,
            [value.reshape(self.count, 2, 2, self.rows, -1) for value in self.state],
        )
        self.state = (left_keep, left, right_keep, right)

    def first_sent(self):
        left_keep, left, right_keep, right = self.state
        self.state = (left_keep, swapped(left, "y"), right_keep, swapped(right, "x"))

    def second(self):
        self.half = sum(self.halves)
        part = shape((self.count, self.rows, self.half // 2))
        left, left_keep, right, right_keep = route(
            second_route_kernel, (part,) * 4, self.name + "_second", self.place, self.state
        )
        self.state = (left_keep, left, right_keep, right)

    def second_sent(self):
        left_keep, left, right_keep, right = self.state
        self.state = (left_keep, swapped(left, "x"), right_keep, swapped(right, "y"))

    def third(self):
        one = (self.rows, self.half)
        if self.count > FEW:
            outs = (shape((self.count, *one)),)
        else:
            outs = (shape(one, HIGH),) + (shape(one),) * (self.count - 1)
        self.state = tuple(route(third_route_kernel, outs, self.name + "_third", self.place, self.state, True))

    def third_sent(self):
        mine, *sends = self.state
        if sends:
            self.state = (mine, *(shifted(send, -1 - k) for k, send in enumerate(sends)))
        else:
            arrived = lax.all_to_all(mine, "z", split_axis=0, concat_axis=0, tiled=True)
            self.state = (arrived.astype(HIGH).sum(0),)

    def last(self):
        part = shape((self.rows // 2, self.half), HIGH)
        mine, other = route(last_kernel, (part, part), self.name + "_last", self.place, self.state, True)
        self.state = (mine, swapped(other, "core"))

    def owned(self, spans):
        rows = self.rows // 2
        outs = tuple(
            shape((ROWS_OF_VECTORS, rows) if stop is None else (rows, stop - start), HIGH)
            for _, start, stop in spans
        )
        spans = tuple((which, start, start + LANES if stop is None else stop) for which, start, stop in spans)
        kernel = functools.partial(owned_kernel, self.halves, spans)
        table = [pltpu.VMEM((LANES, LANES), HIGH)]
        return route(kernel, outs, self.name + "_owned", self.place, self.state, True, table)


class Spread:
    def __init__(self, place, chip):
        self.place = place
        self.state = chip
        self.rows, self.half = chip.shape

    def first(self):
        count = lax.axis_size("z")
        if count > FEW:
            column = jnp.broadcast_to(self.state[None], (count, self.rows, self.half))
            self.state = lax.all_to_all(column, "z", split_axis=0, concat_axis=0, tiled=True)
        else:
            self.state = (self.state, *(shifted(self.state, k) for k in range(1, count)))

    def second(self):
        if isinstance(self.state, tuple):
            part = shape((len(self.state), self.rows, self.half // 2))
            left, right = route(arranged_kernel, (part, part), "arranged", self.place, self.state, True)
        else:
            left, right = self.state[..., : self.half // 2], self.state[..., self.half // 2 :]
        self.state = (left, swapped(left, "x"), right, swapped(right, "y"))

    def third(self):
        left, right = jnp.stack(self.state[:2]), jnp.stack(self.state[2:])
        own = (left, swapped(left, "y"), right, swapped(right, "x"))
        self.state = own + (swapped(left, "core"), swapped(right, "core"))

    def fourth(self):
        left, left_got, right, right_got, left_far, right_far = self.state
        far = (left_far, swapped(left_got, "core"), right_far, swapped(right_got, "core"))
        self.state = (left, left_got, right, right_got) + far

    def pieces(self):
        if self.rows % 16 == 0:
            return self.state
        core, x, y = lax.axis_index("core"), lax.axis_index("x"), lax.axis_index("y")

        def placed(near, far, side):
            piece = jnp.stack([near, far], side)
            piece = jnp.where(y == 0, piece, piece[::-1])
            return jnp.where(x == 0, piece, piece[:, ::-1])

        own, far = (
            jnp.concatenate(
                [placed(*self.state[k : k + 2], 0), placed(*self.state[k + 2 : k + 4], 1)], -1
            )
            for k in (0, 4)
        )
        whole = jnp.where(core == 0, jnp.concatenate([own, far], -1), jnp.concatenate([far, own], -1))
        return (whole.transpose(2, 1, 0, 3, 4).reshape(-1, 2 * self.half),)


def regrouped(tokens):
    return lax.all_to_all(tokens, ("y", "core"), split_axis=0, concat_axis=0, tiled=True)


def in_quarters(tokens, quarters, pad):
    _, frames, places, width = tokens.shape
    tokens = tokens.reshape(frames, quarters, places // quarters, width).swapaxes(0, 1)
    return jnp.pad(tokens, ((0, 0), (0, 0), (0, pad - places // quarters), (0, 0)))


def body(
    clips, time_gain, time_shift, time_heads, time_merge, merge_bias, time_mixer, mixer_bias,
    space_gain, space_shift, space_heads, space_merge, space_bias,
    feed_gain, feed_shift, feed_expand, expand_bias, feed_reduce, reduce_bias, cotangent,
):
    everyone = ("z", "x", "y", "core")
    _, near, all_places, width = clips.shape
    quarters = lax.axis_size("y") * lax.axis_size("core")
    frames, places = near * quarters, all_places // quarters
    pad = -(-places // 8) * 8
    rows = frames * pad
    hidden = feed_expand.shape[1]
    blocks = hidden // width
    share = feed_expand.shape[0]
    count = width // share
    core = lax.axis_index("core")
    place = jnp.stack([core, *(lax.axis_index(axis) for axis in ("x", "y", "z"))]).astype(jnp.int32)

    tall, tokens = (rows, width), (frames, pad, width)
    tiles = (width // LANES, rows, LANES)
    token_flops = 2 * rows * width * width
    vec_shape = shape((ROWS_OF_VECTORS, width), HIGH)
    space_half = 2 * width

    clips_in = in_quarters(clips, quarters, pad)
    by_place = regrouped(clips_in).reshape(tokens)
    vectors = jnp.concatenate(
        [
            jnp.stack(
                [
                    time_gain, time_shift, merge_bias, mixer_bias, space_gain, space_shift, space_bias,
                    feed_gain, feed_shift, reduce_bias,
                ]
            ),
            expand_bias.reshape(blocks, share),
        ],
        0,
    )
    time_half = 5 * width // 2 + LANES
    time_part, space_part = shape((share, time_half)), shape((share, space_half))
    sources = (time_heads, time_merge, time_mixer, space_heads, space_merge)
    time_mine, time_send, space_mine, space_send = call(
        prepare_kernel,
        (time_part, time_part, space_part, space_part),
        (),
        [pltpu.VMEM(source.shape, LOW) for source in sources] + [pltpu.VMEM((LANES, LANES), HIGH)],
        0,
        "prepare",
    )(place, (vectors,), sources, [])

    def spread(mine, send):
        got = swapped(send, "core")
        chip = jnp.where(core == 0, jnp.concatenate([mine, got], 0), jnp.concatenate([got, mine], 0))
        return Spread(place, chip)

    time = spread(time_mine, time_send)
    feed_expand, feed_reduce, cotangent = synced([time], feed_expand, feed_reduce, cotangent)
    time.first()
    space = spread(space_mine, space_send)
    expand = feed_expand.reshape(share, count, blocks, share).swapaxes(1, 2).reshape(share, hidden)
    feed_pack = jnp.concatenate([expand, *feed_reduce.reshape(blocks, share, width)], 1)
    feed_pack, by_place = synced([time, space], feed_pack, by_place)
    feed = lax.all_gather(feed_pack, everyone, axis=0, tiled=True)
    time.second()
    space.first()
    upstream_in = in_quarters(cotangent, quarters, pad)
    upstream_in = synced([time, space], upstream_in)
    time.third()
    synced([time])
    time.fourth()
    space.second()
    synced([time, space])
    space.third()
    low, high = pltpu.VMEM(tall, LOW), pltpu.VMEM(tall, HIGH)
    wide = pltpu.VMEM((rows, 3 * width), LOW)
    vec_block = pltpu.VMEM(vec_shape.shape, HIGH)
    branch, *time_kept, vec = call(
        time_forward_kernel,
        (shape(tokens),),
        (shape(tall), shape(wide.shape), shape(tall), shape(tall), vec_shape),
        [pltpu.VMEM(tiles, HIGH), low, wide, low, low, vec_block],
        6 * token_flops,
        "time_forward",
    )(place, (by_place,), time.pieces(), [weight_scratch(time.pieces())])
    branch = synced([space], branch)
    by_frame = regrouped(branch.reshape(clips_in.shape))
    space.fourth()
    *space_kept, after_space = call(
        functools.partial(space_forward_kernel, all_places),
        (),
        (shape(tall, HIGH), shape(tall), shape(wide.shape), shape(tall), shape(tall, HIGH)),
        [high, high, low, wide, low, vec_block],
        6 * token_flops,
        "space_forward",
    )(place, (clips_in, by_frame), (vec, *space.pieces()), [weight_scratch(space.pieces())])
    last_keep, last_send, result, space_sum, feed_vec, feed_grad = call(
        feed_kernel,
        (shape((width, width)), shape((width, width))),
        (shape(clips_in.shape), shape(tall, HIGH), vec_shape, shape((width, 2 * (hidden - width)))),
        [high, low, low, high, high, pltpu.VMEM(clips_in.shape, LOW), high, vec_block, vec_block],
        24 * token_flops,
        "feed",
    )(
        place, (upstream_in,), (after_space, vec, feed),
        [pltpu.VMEM((blocks, 2, width, width), LOW), pltpu.VMEM((2, 2, width, width), LOW)],
    )
    feed_owned = lax.psum_scatter(feed_grad, everyone, scatter_dimension=0, tiled=True)
    last_sums = Sum(place, last_keep, last_send, "last")
    time_round, space_keep, space_send, time_sum, space_vec = call(
        functools.partial(space_backward_kernel, all_places),
        (shape(clips_in.shape), shape((width, space_half)), shape((width, space_half))),
        (shape(tall, HIGH), vec_shape),
        [high, low, wide, low, high, low, low, wide, high, vec_block, vec_block],
        12 * token_flops,
        "space_backward",
    )(place, (), (space_sum, vec, *space_kept, *space.pieces()), [weight_scratch(space.pieces())])
    space_sums = Sum(place, space_keep, space_send, "space")
    time_round = regrouped(time_round)
    space_sums.joined(last_sums)
    space_sums.first(pltpu.HBM)
    space_sums.first_sent()
    inward, time_keep, time_send = call(
        time_backward_kernel,
        (shape(tokens), shape((width, time_half)), shape((width, time_half))),
        (),
        [
            pltpu.VMEM(tokens, LOW), low, wide, low, low,
            pltpu.VMEM(tiles, HIGH), low, low, wide, pltpu.VMEM((LANES, width), HIGH),
            vec_block, vec_block, vec_block,
        ],
        14 * token_flops,
        "time_backward",
    )(
        place, (time_round.reshape(tokens),),
        (vec, space_vec, feed_vec, by_place, *time_kept, *time.pieces()), [weight_scratch(time.pieces())],
    )
    inward, time_keep, time_send = synced([space_sums], inward, time_keep, time_send)
    time_sums = Sum(place, time_keep, time_send, "time")
    space_sums.second()
    space_sums.second_sent()
    time_sums.first()
    synced([time_sums, space_sums])
    time_sums.first_sent()
    space_sums.third()
    space_sums.third_sent()
    time_sums.second()
    synced([time_sums, space_sums])
    time_sums.second_sent()
    inward = synced([time_sums], inward)
    time_sums.third()
    result = synced([time_sums, space_sums], result)
    time_sums.third_sent()
    entry_round = regrouped(inward.reshape(clips_in.shape))
    time_sum = time_sum.reshape(near, quarters, pad, width)
    grad_clips = (time_sum + entry_round.swapaxes(0, 1).astype(HIGH)).astype(LOW)
    grad_clips = grad_clips[:, :, :places].reshape(clips.shape)
    layer_output = result[:, :, :places].swapaxes(0, 1).reshape(clips.shape)
    space_sums.last()
    space_grads = space_sums.owned(
        [(0, 0, 3 * width), (0, 3 * width, 4 * width), (1, 0, width), (1, width, 2 * width)]
    )
    layer_output, grad_clips, *space_grads = synced([time_sums], layer_output, grad_clips, *space_grads)
    grad_space_heads, grad_space_merge, last_expand, last_reduce = space_grads
    time_sums.last()
    grad_time_heads, grad_time_merge, grad_time_mixer, vector_grads = time_sums.owned(
        [(0, 0, 3 * width), (0, 3 * width, 4 * width), (0, 4 * width, 5 * width), (0, 5 * width, None)]
    )
    vector_grads = vector_grads[:VECTORS]
    if share % 8 == 0:
        grad_expand, grad_reduce = route(
            feed_owned_kernel, (shape((share, hidden), HIGH), shape((blocks * share, width), HIGH)), "feed_owned",
            place, (feed_owned, last_expand, last_reduce), True, [pltpu.VMEM((LANES, hidden), HIGH), pltpu.VMEM((hidden, LANES), HIGH)],
        )
    else:
        feed_owned = feed_owned.astype(HIGH)
        before = hidden - width
        grad_expand = jnp.concatenate([feed_owned[:, :before], last_expand], 1)
        grad_expand = grad_expand.reshape(share, blocks, count, share).swapaxes(1, 2).reshape(share, hidden)
        grad_reduce = [feed_owned[:, before + k * width : before + (k + 1) * width] for k in range(blocks - 1)]
        grad_reduce = jnp.concatenate([*grad_reduce, last_reduce], 0)
    return (
        layer_output,
        grad_clips,
        vector_grads[TIME_GAIN],
        vector_grads[TIME_SHIFT],
        grad_time_heads,
        grad_time_merge,
        vector_grads[MERGE_BIAS],
        grad_time_mixer,
        vector_grads[MIXER_BIAS],
        vector_grads[SPACE_GAIN],
        vector_grads[SPACE_SHIFT],
        grad_space_heads,
        grad_space_merge,
        vector_grads[SPACE_BIAS],
        vector_grads[FEED_GAIN],
        vector_grads[FEED_SHIFT],
        grad_expand,
        vector_grads[EXPAND_BIAS:].reshape(-1),
        grad_reduce,
        vector_grads[REDUCE_BIAS],
    )


def solution(mesh):
    clip, st = mesh.shape["clip"], mesh.shape["st"]
    finer = Mesh(mesh.devices.reshape(clip // 2, 2, st // 2, 2), ("z", "x", "y", "core"))
    token = P(("z", "x"), ("y", "core"), None, None)
    vec = P(("z", "x", "y", "core"))
    mat = P(("z", "x", "y", "core"), None)
    in_specs = (
        token, vec, vec, mat, mat, vec, mat, vec, vec, vec, mat, mat, vec, vec, vec, mat, vec, mat, vec, token,
    )
    out_specs = (
        token, token, vec, vec, mat, mat, vec, mat, vec, vec, vec, mat, mat, vec, vec, vec, mat, vec, mat, vec,
    )
    return jax.shard_map(body, mesh=finer, in_specs=in_specs, out_specs=out_specs, check_vma=False)
```

```python
import functools

import jax
import jax.numpy as jnp
from jax import lax
from jax.experimental import pallas as pl
from jax.experimental.pallas import tpu as pltpu
from jax.sharding import Mesh
from jax.sharding import PartitionSpec as P

HEADS = 12
HEAD_DIM = 64
LANES = 128
EPSILON = 1e-06
SCALE = 0.125
ROOT_HALF = 0.7071067811865476
DENSITY = 0.3989422804014327
LOW = jnp.bfloat16
HIGH = jnp.float32
TIME_BLOCK = 112
VMEM_BYTES = 28 * 1024 * 1024

TIME_GAIN, TIME_SHIFT, MERGE_BIAS, MIXER_BIAS = 0, 1, 2, 3
SPACE_GAIN, SPACE_SHIFT, SPACE_BIAS = 4, 5, 6
FEED_GAIN, FEED_SHIFT, REDUCE_BIAS, EXPAND_BIAS = 7, 8, 9, 10
VECTORS = 14
ROWS_OF_VECTORS = 16


def dot(left, right):
    return jnp.dot(left, right, preferred_element_type=HIGH)


def dot_nt(left, right):
    return lax.dot_general(left, right, (((1,), (1,)), ((), ())), preferred_element_type=HIGH)


def dot_tn(left, right):
    return lax.dot_general(left, right, (((0,), (0,)), ((), ())), preferred_element_type=HIGH)


def norm(values, gain, shift):
    centred = values - jnp.mean(values, -1, keepdims=True)
    inverse = lax.rsqrt(jnp.mean(centred * centred, -1, keepdims=True) + EPSILON)
    normed = centred * inverse
    return normed * gain + shift, normed, inverse


def norm_back(upstream, normed, inverse, gain):
    scaled = upstream * gain
    return inverse * (
        scaled
        - jnp.mean(scaled, -1, keepdims=True)
        - normed * jnp.mean(scaled * normed, -1, keepdims=True)
    )


def column_sum(values):
    return jnp.sum(values, 0, keepdims=True)


class Mover:
    def __init__(self, sems):
        self.sems, self.used = sems, 0

    def start(self, source, target):
        copy = pltpu.make_async_copy(source, target, self.sems.at[self.used])
        self.used += 1
        copy.start()
        return copy

    def start_rows(self, source, target, parts=7):
        return [self.start(source, target)]


def finished(copies):
    for copy in copies:
        copy.wait()


def stacked(pair, scale=1.0):
    lane = lax.broadcasted_iota(jnp.int32, (1, LANES), 1)
    first = jnp.where(lane < HEAD_DIM, scale, 0.0).astype(LOW)
    second = jnp.where(lane < HEAD_DIM, 0.0, scale).astype(LOW)
    return jnp.concatenate([pair * first, pair * second], 0)


def joined(both):
    rows = both.shape[0] // 2
    lane = lax.broadcasted_iota(jnp.int32, (rows, LANES), 1)
    return jnp.where(lane < HEAD_DIM, both[:rows], both[rows:])


def shares_of(queries, key_rows, valid):
    scores = jnp.where(valid, dot_nt(queries, key_rows), -1e30)
    raised = jnp.exp(scores - jnp.max(scores, -1, keepdims=True))
    return raised * (1.0 / jnp.sum(raised, -1, keepdims=True))


def pair_forward(packed_ref, mixed_ref, rows, pair, width, valid):
    at = [slice(pair * LANES + part * width, (pair + 1) * LANES + part * width) for part in range(3)]
    queries = stacked(packed_ref[rows, at[0]], SCALE)
    shares = shares_of(queries, packed_ref[rows, at[1]], valid)
    mixed = dot(shares.astype(LOW), packed_ref[rows, at[2]])
    mixed_ref[rows, at[0]] = joined(mixed).astype(LOW)


def pair_backward(packed_ref, up_ref, grad_ref, rows, pair, width, valid):
    at = [slice(pair * LANES + part * width, (pair + 1) * LANES + part * width) for part in range(3)]
    queries = stacked(packed_ref[rows, at[0]], SCALE)
    key_rows = packed_ref[rows, at[1]]
    upstream = stacked(up_ref[rows, at[0]])
    scores = jnp.where(valid, dot_nt(key_rows, queries), -1e30)
    raised = jnp.exp(scores - jnp.max(scores, 0, keepdims=True))
    shares = raised * (1.0 / jnp.sum(raised, 0, keepdims=True))
    grad_shares = dot_nt(packed_ref[rows, at[2]], upstream)
    grad_scores = (
        shares * (grad_shares - jnp.sum(grad_shares * shares, 0, keepdims=True))
    ).astype(LOW)
    grad_ref[rows, at[0]] = (joined(dot_tn(grad_scores, key_rows)) * SCALE).astype(LOW)
    grad_ref[rows, at[1]] = dot(grad_scores, queries).astype(LOW)
    grad_ref[rows, at[2]] = dot(shares.astype(LOW), upstream).astype(LOW)


def time_valid(block, frames, turned=False):
    dims = (block, 2 * block) if turned else (2 * block, block)
    row = lax.broadcasted_iota(jnp.int32, dims, 0)
    col = lax.broadcasted_iota(jnp.int32, dims, 1)
    return (row % block) // frames == (col % block) // frames


def space_valid(rows, pad, places, turned=False):
    dims = (rows, 2 * rows) if turned else (2 * rows, rows)
    return lax.broadcasted_iota(jnp.int32, dims, 0 if turned else 1) % pad < places


def vector(vec_ref, row):
    return vec_ref[row : row + 1, :]


def to_places(tokens_ref, tiles_ref):
    frames, places, width = tokens_ref.shape
    for frame in range(frames):
        rows = tokens_ref[frame].astype(HIGH)
        for tile in range(width // LANES):
            at = slice(tile * LANES, (tile + 1) * LANES)
            tiles_ref[tile, pl.ds(frame, places, stride=frames), :] = rows[:, at]
    return jnp.concatenate([tiles_ref[tile] for tile in range(width // LANES)], 1)


def from_places(values, tiles_ref, tokens_ref):
    frames, places, width = tokens_ref.shape
    for tile in range(width // LANES):
        tiles_ref[tile] = values[:, tile * LANES : (tile + 1) * LANES]
    for frame in range(frames):
        for tile in range(width // LANES):
            at = slice(tile * LANES, (tile + 1) * LANES)
            rows = tiles_ref[tile, pl.ds(frame, places, stride=frames), :]
            tokens_ref[frame, :, at] = rows.astype(LOW)


def to_frames(tokens_ref, held_ref):
    quarters, frames, places, _ = tokens_ref.shape
    for frame in range(frames):
        for quarter in range(quarters):
            start = (frame * quarters + quarter) * places
            held_ref[start : start + places, :] = tokens_ref[quarter, frame].astype(held_ref.dtype)


def from_frames(held_ref, tokens_ref):
    quarters, frames, places, _ = tokens_ref.shape
    for frame in range(frames):
        for quarter in range(quarters):
            start = (frame * quarters + quarter) * places
            tokens_ref[quarter, frame] = held_ref[start : start + places, :].astype(LOW)


def weight_copies(place_ref, pieces, weight_ref, mover):
    if len(pieces) == 1:
        return [mover.start(pieces[0], weight_ref)]
    core, x, y = place_ref[0], place_ref[1], place_ref[2]
    quarter = pieces[0].shape[-1]
    copies = []
    for number, piece in enumerate(pieces):
        whose, side, far = number // 4, number // 2 % 2, number % 2
        half = core if whose == 0 else 1 - core
        start = pl.multiple_of(half * (2 * quarter) + side * quarter, LANES)
        for near in range(2):
            far_y, far_x = (far, near) if side == 0 else (near, far)
            at_x = 1 - x if far_x else x
            at_y = 1 - y if far_y else y
            target = weight_ref.at[:, at_x * 2 + at_y, :, pl.ds(start, quarter)]
            copies.append(mover.start(piece.at[near], target))
    return copies


def columns_of(weight_ref, at):
    if len(weight_ref.shape) == 2:
        return weight_ref[:, at]
    value = weight_ref[:, :, :, at]
    return value.reshape(-1, value.shape[-1])


def put(core, half, keep_ref, send_ref, at, value):
    @pl.when(core == half)
    def _():
        keep_ref[:, at] = value

    @pl.when(core != half)
    def _():
        send_ref[:, at] = value


def time_forward_kernel(place_ref, tokens_ref, *refs):
    *pieces, branch_ref = refs[:-13]
    *kept, tiles_ref, entry_ref, packed_ref, mixed_ref, middle_ref, vec_ref, weight_ref, sems = refs[-13:]
    frames, _, width = tokens_ref.shape
    rows = entry_ref.shape[0]
    mover = Mover(sems)
    copies = weight_copies(place_ref, pieces, weight_ref, mover)
    tokens = to_places(tokens_ref, tiles_ref)
    finished(copies)
    vec_at = slice(5 * width, 5 * width + LANES)
    vec_ref[...] = jnp.transpose(columns_of(weight_ref, vec_at).astype(HIGH))[:ROWS_OF_VECTORS]
    entry, _, _ = norm(tokens, vector(vec_ref, TIME_GAIN), vector(vec_ref, TIME_SHIFT))
    entry_ref[...] = entry.astype(LOW)
    stores = mover.start_rows(entry_ref, kept[0]) + [mover.start(vec_ref, kept[4])]
    for part in range(3):
        at = slice(part * width, (part + 1) * width)
        packed_ref[:, at] = dot(entry_ref[...], columns_of(weight_ref, at)).astype(LOW)
    stores += mover.start_rows(packed_ref, kept[1])
    valid = time_valid(TIME_BLOCK, frames)

    for pair in range(HEADS // 2):
        for start in range(0, rows, TIME_BLOCK):
            pair_forward(packed_ref, mixed_ref, slice(start, start + TIME_BLOCK), pair, width, valid)
    stores += mover.start_rows(mixed_ref, kept[2])
    merge = columns_of(weight_ref, slice(3 * width, 4 * width))
    middle_ref[...] = (dot(mixed_ref[...], merge) + vector(vec_ref, MERGE_BIAS)).astype(LOW)
    stores += mover.start_rows(middle_ref, kept[3])
    mixer = columns_of(weight_ref, slice(4 * width, 5 * width))
    branch = dot(middle_ref[...], mixer) + vector(vec_ref, MIXER_BIAS)
    from_places(branch, tiles_ref, branch_ref)
    finished(stores)


def space_forward_kernel(all_places, place_ref, clips_ref, branch_ref, vec_in, *refs):
    pieces = refs[:-13]
    *kept, held_ref, after_time_ref, entry_ref, packed_ref, mixed_ref, vec_ref, weight_ref, sems = refs[-13:]
    quarters, frames, pad, width = clips_ref.shape
    rows = held_ref.shape[0]
    mover = Mover(sems)
    vec_copy = mover.start(vec_in, vec_ref)
    copies = weight_copies(place_ref, pieces, weight_ref, mover)
    to_frames(clips_ref, after_time_ref)
    to_frames(branch_ref, held_ref)
    after_time = after_time_ref[...] + held_ref[...]
    after_time_ref[...] = after_time
    stores = mover.start_rows(after_time_ref, kept[0])
    vec_copy.wait()
    entry, _, _ = norm(after_time, vector(vec_ref, SPACE_GAIN), vector(vec_ref, SPACE_SHIFT))
    entry_ref[...] = entry.astype(LOW)
    stores += mover.start_rows(entry_ref, kept[1])
    finished(copies)
    for part in range(3):
        at = slice(part * width, (part + 1) * width)
        packed_ref[:, at] = dot(entry_ref[...], columns_of(weight_ref, at)).astype(LOW)
    stores += mover.start_rows(packed_ref, kept[2])
    each = rows // frames
    valid = space_valid(each, pad, all_places // quarters)

    for pair in range(HEADS // 2):
        for start in range(0, rows, each):
            pair_forward(packed_ref, mixed_ref, slice(start, start + each), pair, width, valid)
    stores += mover.start_rows(mixed_ref, kept[3])
    merge = columns_of(weight_ref, slice(3 * width, 4 * width))
    held_ref[...] = after_time_ref[...] + dot(mixed_ref[...], merge) + vector(vec_ref, SPACE_BIAS)
    stores += mover.start_rows(held_ref, kept[4])
    finished(stores)


def feed_kernel(
    place_ref, upstream_ref, after_space_in, vec_in, weight_ref,
    keep_ref, send_ref, result_ref, space_sum_ref, vec_out, grad_ref,
    held_ref, up_ref, entry_ref, out_ref, back_ref, results_ref, after_space_ref, vec_ref, grad_vec_ref,
    weights_ref, grads_ref, sems,
):
    width = after_space_ref.shape[-1]
    half = weight_ref.shape[1] // 2
    blocks = half // width
    mover = Mover(sems)
    first = [mover.start(vec_in, vec_ref), mover.start(after_space_in, after_space_ref)]

    def columns(side, block, whole=half):
        return pl.ds(side * whole + block * width, width)

    def load(block):
        return [
            copy
            for side in range(2)
            for copy in mover.start_rows(weight_ref.at[:, columns(side, block)], weights_ref.at[block, side], 4)
        ]

    loads = [load(block) for block in range(blocks)]
    to_frames(upstream_ref, held_ref)
    up_ref[...] = held_ref[...].astype(LOW)
    finished(first)
    gain, shift = vector(vec_ref, FEED_GAIN), vector(vec_ref, FEED_SHIFT)
    entry, _, _ = norm(after_space_ref[...], gain, shift)
    entry_ref[...] = entry.astype(LOW)
    grad_vec_ref[...] = jnp.zeros_like(grad_vec_ref)
    stores = []
    for block in range(blocks):
        finished(loads[block])
        expand, reduce = weights_ref[block, 0], weights_ref[block, 1]
        hidden = dot(entry_ref[...], expand) + vector(vec_ref, EXPAND_BIAS + block)
        normal = 0.5 * (1.0 + lax.erf(hidden * ROOT_HALF))
        active = (hidden * normal).astype(LOW)
        out = dot(active, reduce)
        slope = normal + hidden * DENSITY * jnp.exp(-0.5 * hidden * hidden)
        hidden_grad = (dot_nt(up_ref[...], reduce) * slope).astype(LOW)
        back = dot_nt(hidden_grad, expand)
        if block:
            out_ref[...] += out
            back_ref[...] += back
        else:
            out_ref[...] = after_space_ref[...] + vector(vec_ref, REDUCE_BIAS) + out
            back_ref[...] = back
        grad_vec_ref[3 + block : 4 + block, :] = column_sum(hidden_grad.astype(HIGH))
        expand_grad = dot_tn(entry_ref[...], hidden_grad).astype(LOW)
        reduce_grad = dot_tn(active, up_ref[...]).astype(LOW)
        if block == blocks - 1:
            put(place_ref[0], 0, keep_ref, send_ref, slice(0, width), expand_grad)
            put(place_ref[0], 1, keep_ref, send_ref, slice(0, width), reduce_grad)
            continue
        if block > 1:
            finished(stores[2 * block - 4 : 2 * block - 2])
        grads_ref[block % 2, 0] = expand_grad
        grads_ref[block % 2, 1] = reduce_grad
        for side in range(2):
            target = grad_ref.at[:, columns(side, block, half - width)]
            stores.append(mover.start(grads_ref.at[block % 2, side], target))
    from_frames(out_ref, results_ref)
    stores.append(mover.start(results_ref, result_ref))
    _, normed, inverse = norm(after_space_ref[...], gain, shift)
    upstream = back_ref[...]
    grad_vec_ref[0:1, :] = column_sum(upstream * normed)
    grad_vec_ref[1:2, :] = column_sum(upstream)
    grad_vec_ref[2:3, :] = column_sum(held_ref[...])
    back_ref[...] = held_ref[...] + norm_back(upstream, normed, inverse, gain)
    stores += [mover.start(back_ref, space_sum_ref), mover.start(grad_vec_ref, vec_out)]
    finished(stores[2 * blocks - 6 :])


def space_backward_kernel(all_places, place_ref, space_sum_in, vec_in, *refs):
    *kept, time_round_ref, keep_ref, send_ref, time_sum_ref, vec_out = refs[:-13]
    kept, pieces = kept[:4], kept[4:]
    *held, sum_ref, round_ref, up_ref, grad_ref, space_sum_ref, vec_ref, grad_vec_ref, weight_ref, sems = refs[-13:]
    after_time_ref, entry_ref, packed_ref, mixed_ref = held
    rows, width = space_sum_ref.shape
    quarters, frames, pad, _ = time_round_ref.shape
    core = place_ref[0]
    half = keep_ref.shape[1]
    mover = Mover(sems)
    first = [mover.start(space_sum_in, space_sum_ref), mover.start(vec_in, vec_ref)]
    mixed_copies = mover.start_rows(kept[3], mixed_ref)
    copies = weight_copies(place_ref, pieces, weight_ref, mover)
    packed_copies = mover.start_rows(kept[2], packed_ref)
    others = mover.start_rows(kept[1], entry_ref) + mover.start_rows(kept[0], after_time_ref)
    finished(first)
    round_ref[...] = space_sum_ref[...].astype(LOW)
    finished(mixed_copies)
    put(core, 1, keep_ref, send_ref, slice(half - width, half), dot_tn(mixed_ref[...], round_ref[...]).astype(LOW))
    finished(copies)
    up_ref[...] = dot_nt(round_ref[...], columns_of(weight_ref, slice(3 * width, 4 * width))).astype(LOW)
    each = rows // frames
    valid = space_valid(each, pad, all_places // quarters, True)
    finished(packed_copies)

    for pair in range(HEADS // 2):
        for start in range(0, rows, each):
            pair_backward(packed_ref, up_ref, grad_ref, slice(start, start + each), pair, width, valid)
    finished(others)
    back = dot_nt(grad_ref[:, 0:width], columns_of(weight_ref, slice(0, width)))
    for part in range(1, 3):
        at = slice(part * width, (part + 1) * width)
        back += dot_nt(grad_ref[:, at], columns_of(weight_ref, at))
    gain = vector(vec_ref, SPACE_GAIN)
    _, normed, inverse = norm(after_time_ref[...], gain, vector(vec_ref, SPACE_SHIFT))
    sum_ref[...] = space_sum_ref[...] + norm_back(back, normed, inverse, gain)
    stores = mover.start_rows(sum_ref, time_sum_ref)
    from_frames(sum_ref, time_round_ref)
    grad_vec_ref[...] = jnp.zeros_like(grad_vec_ref)
    grad_vec_ref[0:1, :] = column_sum(back * normed)
    grad_vec_ref[1:2, :] = column_sum(back)
    grad_vec_ref[2:3, :] = column_sum(round_ref[...].astype(HIGH))
    stores.append(mover.start(grad_vec_ref, vec_out))
    for part in range(3):
        at = slice(part * width, (part + 1) * width)
        value = dot_tn(entry_ref[...], grad_ref[:, at]).astype(LOW)
        start = part * width % half
        put(core, part * width // half, keep_ref, send_ref, slice(start, start + width), value)
    finished(stores)


def time_backward_kernel(place_ref, time_round_ref, vec_in, space_vec_in, feed_vec_in, *refs):
    *kept, inward_ref, keep_ref, send_ref = refs[:-15]
    kept, pieces = kept[:5], kept[5:]
    *held, tiles_ref, round_ref, up_ref, grad_ref, vectors_ref, vec_ref, space_vec_ref, feed_vec_ref, weight_ref, sems = refs[-15:]
    tokens_ref, entry_ref, packed_ref, mixed_ref, middle_ref = held
    frames, _, width = time_round_ref.shape
    rows = entry_ref.shape[0]
    core = place_ref[0]
    half = keep_ref.shape[1]
    mover = Mover(sems)
    middle_copies = mover.start_rows(kept[4], middle_ref)
    copies = weight_copies(place_ref, pieces, weight_ref, mover)
    mixed_copies, packed_copies = mover.start_rows(kept[3], mixed_ref), mover.start_rows(kept[2], packed_ref)
    others = mover.start_rows(kept[1], entry_ref) + mover.start_rows(kept[0], tokens_ref, 8)
    for source, target in ((vec_in, vec_ref), (space_vec_in, space_vec_ref), (feed_vec_in, feed_vec_ref)):
        others.append(mover.start(source, target))
    rounded = to_places(time_round_ref, tiles_ref)
    round_ref[...] = rounded.astype(LOW)
    vectors_ref[...] = jnp.zeros_like(vectors_ref)
    vectors_ref[MIXER_BIAS : MIXER_BIAS + 1, :] = column_sum(rounded)
    tail = 3 * width - half
    at = slice(tail + width, tail + 2 * width)
    finished(middle_copies)
    put(core, 1, keep_ref, send_ref, at, dot_tn(middle_ref[...], round_ref[...]).astype(LOW))
    finished(copies)
    up_ref[...] = dot_nt(round_ref[...], columns_of(weight_ref, slice(4 * width, 5 * width))).astype(LOW)
    vectors_ref[MERGE_BIAS : MERGE_BIAS + 1, :] = column_sum(up_ref[...].astype(HIGH))
    at = slice(tail, tail + width)
    finished(mixed_copies)
    put(core, 1, keep_ref, send_ref, at, dot_tn(mixed_ref[...], up_ref[...]).astype(LOW))
    up_ref[...] = dot_nt(up_ref[...], columns_of(weight_ref, slice(3 * width, 4 * width))).astype(LOW)
    valid = time_valid(TIME_BLOCK, frames, True)
    finished(packed_copies)

    for pair in range(HEADS // 2):
        for start in range(0, rows, TIME_BLOCK):
            pair_backward(packed_ref, up_ref, grad_ref, slice(start, start + TIME_BLOCK), pair, width, valid)
    finished(others)
    for start, stop in ((0, half), (half, 3 * width)):
        value = dot_tn(entry_ref[...], grad_ref[:, start:stop]).astype(LOW)
        put(core, start // half, keep_ref, send_ref, slice(0, stop - start), value)
    back = dot_nt(grad_ref[:, 0:width], columns_of(weight_ref, slice(0, width)))
    for part in range(1, 3):
        at = slice(part * width, (part + 1) * width)
        back += dot_nt(grad_ref[:, at], columns_of(weight_ref, at))
    tokens = to_places(tokens_ref, tiles_ref)
    gain = vector(vec_ref, TIME_GAIN)
    _, normed, inverse = norm(tokens, gain, vector(vec_ref, TIME_SHIFT))
    vectors_ref[TIME_GAIN : TIME_GAIN + 1, :] = column_sum(back * normed)
    vectors_ref[TIME_SHIFT : TIME_SHIFT + 1, :] = column_sum(back)
    for start, stop, source in ((SPACE_GAIN, FEED_GAIN, space_vec_ref), (FEED_GAIN, VECTORS, feed_vec_ref)):
        for row in range(start, stop):
            vectors_ref[row : row + 1, :] = source[row - start : row - start + 1, :]
    columns = jnp.transpose(vectors_ref[...]).astype(LOW)
    put(core, 1, keep_ref, send_ref, slice(half - 2 * LANES, half - LANES), columns)
    put(core, 1, keep_ref, send_ref, slice(half - LANES, half), jnp.zeros_like(columns))
    from_places(norm_back(back, normed, inverse, gain), tiles_ref, inward_ref)


def first_route_kernel(place_ref, *refs):
    *pairs, left_send, left_keep, right_send, right_keep = refs
    x, y = place_ref[1], place_ref[2]
    begin = 0
    for keep_ref, got_ref in zip(pairs[::2], pairs[1::2]):
        quarter = keep_ref.shape[-1] // 2
        left, right = slice(0, quarter), slice(quarter, 2 * quarter)
        to = slice(begin, begin + quarter)
        begin += quarter

        def total(at_x, at_y, columns):
            return added(keep_ref[0, at_x, at_y, :, columns], got_ref[0, at_x, at_y, :, columns])

        for other in range(2):
            left_send[0, other, :, to] = total(other, 1 - y, left)
            right_send[0, other, :, to] = total(1 - x, other, right)
            left_keep[0, other, :, to] = total(other, y, left)
            right_keep[0, other, :, to] = total(x, other, right)


def second_route_kernel(place_ref, *refs):
    *fours, left_send, left_keep, right_send, right_keep = refs
    x, y = place_ref[1], place_ref[2]
    begin = 0
    for at in range(0, len(fours), 4):
        left_ref, left_got, right_ref, right_got = fours[at : at + 4]
        to = slice(begin, begin + left_ref.shape[-1])
        begin = to.stop
        left_send[0, :, to] = added(left_ref[0, 1 - x], left_got[0, 1 - x])
        right_send[0, :, to] = added(right_ref[0, 1 - y], right_got[0, 1 - y])
        left_keep[0, :, to] = added(left_ref[0, x], left_got[0, x])
        right_keep[0, :, to] = added(right_ref[0, y], right_got[0, y])


def third_route_kernel(place_ref, left_ref, left_got, right_ref, right_got, *sends):
    quarter = left_ref.shape[-1]
    count = left_ref.shape[0]
    for distance, send in enumerate(sends):
        at = lax.rem(place_ref[3] + distance, count) if len(sends) > 1 else 0
        rows = at if len(sends) > 1 else slice(None)
        send[..., 0:quarter] = added(left_ref[rows], left_got[rows], send.dtype)
        send[..., quarter : 2 * quarter] = added(right_ref[rows], right_got[rows], send.dtype)


def last_kernel(place_ref, *refs):
    *parts, mine_ref, other_ref = refs
    total = sum(part[...].astype(HIGH) for part in parts)
    rows = mine_ref.shape[0]
    near, far = total[:rows], total[rows:]
    mine_ref[...] = jnp.where(place_ref[0] == 0, near, far)
    other_ref[...] = jnp.where(place_ref[0] == 0, far, near)


def owned_kernel(halves, spans, place_ref, mine_ref, other_ref, *refs):
    core = place_ref[0]
    half = sum(halves)
    outs, table_ref = refs[:-1], refs[-1]
    begin, wholes = 0, []
    for each in halves:
        quarters = [slice(at, at + each // 2) for at in (begin, half // 2 + begin)]
        begin += each // 2
        low = [jnp.where(core == 0, mine_ref[:, at], other_ref[:, at]) for at in quarters]
        high = [jnp.where(core == 0, other_ref[:, at], mine_ref[:, at]) for at in quarters]
        wholes.append(jnp.concatenate(low + high, 1))
    for (matrix, start, stop), out_ref in zip(spans, outs):
        value = wholes[matrix][:, start:stop]
        if out_ref.shape == value.shape:
            out_ref[...] = value
        else:
            table_ref[...] = jnp.zeros_like(table_ref)
            table_ref[0 : value.shape[0], :] = value
            out_ref[...] = jnp.transpose(table_ref[...])[: out_ref.shape[0], : out_ref.shape[1]]


def feed_owned_kernel(place_ref, owned_ref, last_expand_ref, last_reduce_ref, expand_ref, reduce_ref, table_ref, turned_ref):
    rows, hidden = expand_ref.shape
    width = reduce_ref.shape[1]
    blocks, count = hidden // width, width // rows
    before = hidden - width
    for block in range(blocks - 1):
        at = slice(before + block * width, before + (block + 1) * width)
        reduce_ref[block * rows : (block + 1) * rows, :] = owned_ref[:, at].astype(HIGH)
    reduce_ref[(blocks - 1) * rows :, :] = last_reduce_ref[...]
    table_ref[...] = jnp.zeros_like(table_ref)
    table_ref[0:rows, 0:before] = owned_ref[:, 0:before].astype(HIGH)
    table_ref[0:rows, before:] = last_expand_ref[...]
    turned = jnp.transpose(table_ref[...])
    for block in range(blocks):
        for owner in range(count):
            to = (owner * blocks + block) * rows
            at = block * width + owner * rows
            turned_ref[to : to + rows, :] = turned[at : at + rows]
    expand_ref[...] = jnp.transpose(turned_ref[...])[0:rows]


def arranged_kernel(place_ref, *refs):
    *blocks, left_ref, right_ref = refs
    count, _, quarter = left_ref.shape
    for distance, block in enumerate(blocks):
        at = lax.rem(place_ref[3] + distance, count)
        left_ref[at] = block[:, 0:quarter]
        right_ref[at] = block[:, quarter : 2 * quarter]


def prepare_kernel(place_ref, vectors_ref, *refs):
    *sources, time_mine, time_send, space_mine, space_send = refs[:-7]
    *held, table_ref, sems = refs[-7:]
    heads_ref, merge_ref, mixer_ref, space_heads_ref, space_merge_ref = held
    mover = Mover(sems)
    copies = [mover.start(source, target) for source, target in zip(sources, held)]
    width = merge_ref.shape[1]
    rows, half = time_mine.shape
    table_ref[...] = jnp.zeros_like(table_ref)
    table_ref[0 : vectors_ref.shape[0], 0:rows] = vectors_ref[...].astype(HIGH)
    columns = jnp.transpose(table_ref[...])[0:rows].astype(LOW)
    finished(copies)

    def fill(low, high, space_low, space_high):
        low[...] = heads_ref[:, 0:half]
        rest = 3 * width - half
        high[:, 0:rest] = heads_ref[:, half:]
        high[:, rest : rest + width] = merge_ref[...]
        high[:, rest + width : rest + 2 * width] = mixer_ref[...]
        high[:, half - 2 * LANES : half - LANES] = columns
        high[:, half - LANES :] = jnp.zeros_like(columns)
        space_half = space_low.shape[1]
        space_low[...] = space_heads_ref[:, 0:space_half]
        space_high[:, 0 : 3 * width - space_half] = space_heads_ref[:, space_half:]
        space_high[:, 3 * width - space_half :] = space_merge_ref[...]

    @pl.when(place_ref[0] == 0)
    def _():
        fill(time_mine, time_send, space_mine, space_send)

    @pl.when(place_ref[0] != 0)
    def _():
        fill(time_send, time_mine, space_send, space_mine)


def in_hbm(value):
    return pltpu.with_memory_space_constraint(value, pltpu.HBM)


def call(kernel, outs, kept, scratch, flops, name):
    def run(place, blocks, streamed, weights):
        args = (place, *blocks, *streamed)
        every = outs + kept
        moved = sum(a.size * a.dtype.itemsize for a in args)
        moved += sum(s.size * s.dtype.itemsize for s in every)
        in_vmem, in_place = pl.BlockSpec(memory_space=pltpu.VMEM), pl.BlockSpec(memory_space=pltpu.HBM)
        return pl.pallas_call(
            kernel,
            out_shape=outs + tuple(out if out.size > 3000000 else pltpu.HBM(out.shape, out.dtype) for out in kept),
            in_specs=[pl.BlockSpec(memory_space=pltpu.SMEM)]
            + [in_vmem] * len(blocks)
            + [in_place] * len(streamed),
            out_specs=(in_vmem,) * len(outs) + (in_place,) * len(kept),
            scratch_shapes=scratch + weights + [pltpu.SemaphoreType.DMA((96,))],
            compiler_params=pltpu.CompilerParams(vmem_limit_bytes=VMEM_BYTES),
            cost_estimate=pl.CostEstimate(flops=flops, bytes_accessed=moved, transcendentals=0),
            name=name,
        )(place, *blocks, *(in_hbm(value) for value in streamed))

    return run


def weight_scratch(pieces):
    if len(pieces) == 1:
        return pltpu.VMEM(pieces[0].shape, LOW)
    _, count, rows, quarter = pieces[0].shape
    return pltpu.VMEM((count, 4, rows, 4 * quarter), LOW)


def route(kernel, outs, name, place, blocks, whole=False, scratch=()):
    def spec(dims):
        if whole:
            return pl.BlockSpec(memory_space=pltpu.VMEM)
        return pl.BlockSpec((1,) + tuple(dims[1:]), lambda step: (step,) + (0,) * (len(dims) - 1))

    return pl.pallas_call(
        kernel,
        grid=() if whole else (blocks[0].shape[0],),
        out_shape=outs,
        in_specs=[pl.BlockSpec(memory_space=pltpu.SMEM)] + [spec(b.shape) for b in blocks],
        out_specs=tuple(spec(o.shape) for o in outs),
        scratch_shapes=scratch,
        compiler_params=pltpu.CompilerParams(vmem_limit_bytes=VMEM_BYTES),
        name=name,
    )(place, *blocks)


def shape(dims, dtype=LOW):
    return jax.ShapeDtypeStruct(dims, dtype)


SWAP = ((0, 1), (1, 0))


def swapped(value, axis):
    return lax.ppermute(value, axis, SWAP)


def added(left, right, dtype=LOW):
    return (left.astype(HIGH) + right.astype(HIGH)).astype(dtype)


def picked(value, index, axis):
    return lax.dynamic_index_in_dim(value, index, axis, keepdims=False)


def tied(value):
    return lax.optimization_barrier(value)


def synced(groups, *others):
    states, others = tied(([group.state for group in groups], others))
    for group, state in zip(groups, states):
        group.state = state
    return others if len(others) != 1 else others[0]


def shifted(value, distance):
    count = lax.axis_size("z")
    return lax.ppermute(value, "z", [(k, (k - distance) % count) for k in range(count)])


FEW = 4


class Sum:
    def __init__(self, place, keep, send, name):
        self.place, self.name = place, name
        self.count = lax.axis_size("z")
        self.rows = keep.shape[0] // (self.count * 4)
        self.halves = (keep.shape[1],)
        self.state = (keep, swapped(send, "core"))

    def joined(self, other):
        self.halves += other.halves
        self.state += other.state

    def first(self, kept_in=jax.ShapeDtypeStruct):
        part = shape((self.count, 2, self.rows, sum(self.halves) // 2))
        kept = kept_in(part.shape, part.dtype)
        left, left_keep, right, right_keep = route(
            first_route_kernel, (part, kept, part, kept), self.name + "_first", self.place,
            [value.reshape(self.count, 2, 2, self.rows, -1) for value in self.state],
        )
        self.state = (left_keep, left, right_keep, right)

    def first_sent(self):
        left_keep, left, right_keep, right = self.state
        self.state = (left_keep, swapped(left, "y"), right_keep, swapped(right, "x"))

    def second(self):
        self.half = sum(self.halves)
        part = shape((self.count, self.rows, self.half // 2))
        left, left_keep, right, right_keep = route(
            second_route_kernel, (part,) * 4, self.name + "_second", self.place, self.state
        )
        self.state = (left_keep, left, right_keep, right)

    def second_sent(self):
        left_keep, left, right_keep, right = self.state
        self.state = (left_keep, swapped(left, "x"), right_keep, swapped(right, "y"))

    def third(self):
        one = (self.rows, self.half)
        if self.count > FEW:
            outs = (shape((self.count, *one)),)
        else:
            outs = (shape(one, HIGH),) + (shape(one),) * (self.count - 1)
        self.state = tuple(route(third_route_kernel, outs, self.name + "_third", self.place, self.state, True))

    def third_sent(self):
        mine, *sends = self.state
        if sends:
            self.state = (mine, *(shifted(send, -1 - k) for k, send in enumerate(sends)))
        else:
            arrived = lax.all_to_all(mine, "z", split_axis=0, concat_axis=0, tiled=True)
            self.state = (arrived.astype(HIGH).sum(0),)

    def last(self):
        part = shape((self.rows // 2, self.half), HIGH)
        mine, other = route(last_kernel, (part, part), self.name + "_last", self.place, self.state, True)
        self.state = (mine, swapped(other, "core"))

    def owned(self, spans):
        rows = self.rows // 2
        outs = tuple(
            shape((ROWS_OF_VECTORS, rows) if stop is None else (rows, stop - start), HIGH)
            for _, start, stop in spans
        )
        spans = tuple((which, start, start + LANES if stop is None else stop) for which, start, stop in spans)
        kernel = functools.partial(owned_kernel, self.halves, spans)
        table = [pltpu.VMEM((LANES, LANES), HIGH)]
        return route(kernel, outs, self.name + "_owned", self.place, self.state, True, table)


class Spread:
    def __init__(self, place, chip):
        self.place = place
        self.state = chip
        self.rows, self.half = chip.shape

    def first(self):
        count = lax.axis_size("z")
        if count > FEW:
            column = jnp.broadcast_to(self.state[None], (count, self.rows, self.half))
            self.state = lax.all_to_all(column, "z", split_axis=0, concat_axis=0, tiled=True)
        else:
            self.state = (self.state, *(shifted(self.state, k) for k in range(1, count)))

    def second(self):
        if isinstance(self.state, tuple):
            part = shape((len(self.state), self.rows, self.half // 2))
            left, right = route(arranged_kernel, (part, part), "arranged", self.place, self.state, True)
        else:
            left, right = self.state[..., : self.half // 2], self.state[..., self.half // 2 :]
        self.state = (left, swapped(left, "x"), right, swapped(right, "y"))

    def third(self):
        left, right = jnp.stack(self.state[:2]), jnp.stack(self.state[2:])
        own = (left, swapped(left, "y"), right, swapped(right, "x"))
        self.state = own + (swapped(left, "core"), swapped(right, "core"))

    def fourth(self):
        left, left_got, right, right_got, left_far, right_far = self.state
        far = (left_far, swapped(left_got, "core"), right_far, swapped(right_got, "core"))
        self.state = (left, left_got, right, right_got) + far

    def pieces(self):
        if self.rows % 16 == 0:
            return self.state
        core, x, y = lax.axis_index("core"), lax.axis_index("x"), lax.axis_index("y")

        def placed(near, far, side):
            piece = jnp.stack([near, far], side)
            piece = jnp.where(y == 0, piece, piece[::-1])
            return jnp.where(x == 0, piece, piece[:, ::-1])

        own, far = (
            jnp.concatenate(
                [placed(*self.state[k : k + 2], 0), placed(*self.state[k + 2 : k + 4], 1)], -1
            )
            for k in (0, 4)
        )
        whole = jnp.where(core == 0, jnp.concatenate([own, far], -1), jnp.concatenate([far, own], -1))
        return (whole.transpose(2, 1, 0, 3, 4).reshape(-1, 2 * self.half),)


def regrouped(tokens):
    return lax.all_to_all(tokens, ("y", "core"), split_axis=0, concat_axis=0, tiled=True)


def in_quarters(tokens, quarters, pad):
    _, frames, places, width = tokens.shape
    tokens = tokens.reshape(frames, quarters, places // quarters, width).swapaxes(0, 1)
    return jnp.pad(tokens, ((0, 0), (0, 0), (0, pad - places // quarters), (0, 0)))


def body(
    clips, time_gain, time_shift, time_heads, time_merge, merge_bias, time_mixer, mixer_bias,
    space_gain, space_shift, space_heads, space_merge, space_bias,
    feed_gain, feed_shift, feed_expand, expand_bias, feed_reduce, reduce_bias, cotangent,
):
    everyone = ("z", "x", "y", "core")
    _, near, all_places, width = clips.shape
    quarters = lax.axis_size("y") * lax.axis_size("core")
    frames, places = near * quarters, all_places // quarters
    pad = -(-places // 8) * 8
    rows = frames * pad
    hidden = feed_expand.shape[1]
    blocks = hidden // width
    share = feed_expand.shape[0]
    count = width // share
    core = lax.axis_index("core")
    place = jnp.stack([core, *(lax.axis_index(axis) for axis in ("x", "y", "z"))]).astype(jnp.int32)

    tall, tokens = (rows, width), (frames, pad, width)
    tiles = (width // LANES, rows, LANES)
    token_flops = 2 * rows * width * width
    vec_shape = shape((ROWS_OF_VECTORS, width), HIGH)
    space_half = 2 * width

    clips_in = in_quarters(clips, quarters, pad)
    by_place = regrouped(clips_in).reshape(tokens)
    vectors = jnp.concatenate(
        [
            jnp.stack(
                [
                    time_gain, time_shift, merge_bias, mixer_bias, space_gain, space_shift, space_bias,
                    feed_gain, feed_shift, reduce_bias,
                ]
            ),
            expand_bias.reshape(blocks, share),
        ],
        0,
    )
    time_half = 5 * width // 2 + LANES
    time_part, space_part = shape((share, time_half)), shape((share, space_half))
    sources = (time_heads, time_merge, time_mixer, space_heads, space_merge)
    time_mine, time_send, space_mine, space_send = call(
        prepare_kernel,
        (time_part, time_part, space_part, space_part),
        (),
        [pltpu.VMEM(source.shape, LOW) for source in sources] + [pltpu.VMEM((LANES, LANES), HIGH)],
        0,
        "prepare",
    )(place, (vectors,), sources, [])

    def spread(mine, send):
        got = swapped(send, "core")
        chip = jnp.where(core == 0, jnp.concatenate([mine, got], 0), jnp.concatenate([got, mine], 0))
        return Spread(place, chip)

    time = spread(time_mine, time_send)
    feed_expand, feed_reduce, cotangent = synced([time], feed_expand, feed_reduce, cotangent)
    time.first()
    space = spread(space_mine, space_send)
    expand = feed_expand.reshape(share, count, blocks, share).swapaxes(1, 2).reshape(share, hidden)
    feed_pack = jnp.concatenate([expand, *feed_reduce.reshape(blocks, share, width)], 1)
    feed_pack = synced([time, space], feed_pack)
    feed = lax.all_gather(feed_pack, everyone, axis=0, tiled=True)
    time.second()
    space.first()
    upstream_in = in_quarters(cotangent, quarters, pad)
    by_place, upstream_in = synced([time, space], by_place, upstream_in)
    time.third()
    synced([time])
    time.fourth()
    space.second()
    synced([time, space])
    space.third()
    low, high = pltpu.VMEM(tall, LOW), pltpu.VMEM(tall, HIGH)
    wide = pltpu.VMEM((rows, 3 * width), LOW)
    vec_block = pltpu.VMEM(vec_shape.shape, HIGH)
    branch, *time_kept, vec = call(
        time_forward_kernel,
        (shape(tokens),),
        (shape(tall), shape(wide.shape), shape(tall), shape(tall), vec_shape),
        [pltpu.VMEM(tiles, HIGH), low, wide, low, low, vec_block],
        6 * token_flops,
        "time_forward",
    )(place, (by_place,), time.pieces(), [weight_scratch(time.pieces())])
    branch = synced([space], branch)
    by_frame = regrouped(branch.reshape(clips_in.shape))
    space.fourth()
    *space_kept, after_space = call(
        functools.partial(space_forward_kernel, all_places),
        (),
        (shape(tall, HIGH), shape(tall), shape(wide.shape), shape(tall), shape(tall, HIGH)),
        [high, high, low, wide, low, vec_block],
        6 * token_flops,
        "space_forward",
    )(place, (clips_in, by_frame), (vec, *space.pieces()), [weight_scratch(space.pieces())])
    last_keep, last_send, result, space_sum, feed_vec, feed_grad = call(
        feed_kernel,
        (shape((width, width)), shape((width, width))),
        (shape(clips_in.shape), shape(tall, HIGH), vec_shape, shape((width, 2 * (hidden - width)))),
        [high, low, low, high, high, pltpu.VMEM(clips_in.shape, LOW), high, vec_block, vec_block],
        24 * token_flops,
        "feed",
    )(
        place, (upstream_in,), (after_space, vec, feed),
        [pltpu.VMEM((blocks, 2, width, width), LOW), pltpu.VMEM((2, 2, width, width), LOW)],
    )
    feed_owned = lax.psum_scatter(feed_grad, everyone, scatter_dimension=0, tiled=True)
    last_sums = Sum(place, last_keep, last_send, "last")
    time_round, space_keep, space_send, time_sum, space_vec = call(
        functools.partial(space_backward_kernel, all_places),
        (shape(clips_in.shape), shape((width, space_half)), shape((width, space_half))),
        (shape(tall, HIGH), vec_shape),
        [high, low, wide, low, high, low, low, wide, high, vec_block, vec_block],
        12 * token_flops,
        "space_backward",
    )(place, (), (space_sum, vec, *space_kept, *space.pieces()), [weight_scratch(space.pieces())])
    space_sums = Sum(place, space_keep, space_send, "space")
    time_round = regrouped(time_round)
    space_sums.joined(last_sums)
    space_sums.first(pltpu.HBM)
    space_sums.first_sent()
    inward, time_keep, time_send = call(
        time_backward_kernel,
        (shape(tokens), shape((width, time_half)), shape((width, time_half))),
        (),
        [
            pltpu.VMEM(tokens, LOW), low, wide, low, low,
            pltpu.VMEM(tiles, HIGH), low, low, wide, pltpu.VMEM((LANES, width), HIGH),
            vec_block, vec_block, vec_block,
        ],
        14 * token_flops,
        "time_backward",
    )(
        place, (time_round.reshape(tokens),),
        (vec, space_vec, feed_vec, by_place, *time_kept, *time.pieces()), [weight_scratch(time.pieces())],
    )
    inward, time_keep, time_send = synced([space_sums], inward, time_keep, time_send)
    time_sums = Sum(place, time_keep, time_send, "time")
    space_sums.second()
    space_sums.second_sent()
    time_sums.first()
    synced([time_sums, space_sums])
    time_sums.first_sent()
    space_sums.third()
    space_sums.third_sent()
    time_sums.second()
    synced([time_sums, space_sums])
    time_sums.second_sent()
    inward = synced([time_sums], inward)
    time_sums.third()
    result = synced([time_sums, space_sums], result)
    time_sums.third_sent()
    entry_round = regrouped(inward.reshape(clips_in.shape))
    time_sum = time_sum.reshape(near, quarters, pad, width)
    grad_clips = (time_sum + entry_round.swapaxes(0, 1).astype(HIGH)).astype(LOW)
    grad_clips = grad_clips[:, :, :places].reshape(clips.shape)
    layer_output = result[:, :, :places].swapaxes(0, 1).reshape(clips.shape)
    space_sums.last()
    space_grads = space_sums.owned(
        [(0, 0, 3 * width), (0, 3 * width, 4 * width), (1, 0, width), (1, width, 2 * width)]
    )
    layer_output, grad_clips, *space_grads = synced([time_sums], layer_output, grad_clips, *space_grads)
    grad_space_heads, grad_space_merge, last_expand, last_reduce = space_grads
    time_sums.last()
    grad_time_heads, grad_time_merge, grad_time_mixer, vector_grads = time_sums.owned(
        [(0, 0, 3 * width), (0, 3 * width, 4 * width), (0, 4 * width, 5 * width), (0, 5 * width, None)]
    )
    vector_grads = vector_grads[:VECTORS]
    if share % 8 == 0:
        grad_expand, grad_reduce = route(
            feed_owned_kernel, (shape((share, hidden), HIGH), shape((blocks * share, width), HIGH)), "feed_owned",
            place, (feed_owned, last_expand, last_reduce), True, [pltpu.VMEM((LANES, hidden), HIGH), pltpu.VMEM((hidden, LANES), HIGH)],
        )
    else:
        feed_owned = feed_owned.astype(HIGH)
        before = hidden - width
        grad_expand = jnp.concatenate([feed_owned[:, :before], last_expand], 1)
        grad_expand = grad_expand.reshape(share, blocks, count, share).swapaxes(1, 2).reshape(share, hidden)
        grad_reduce = [feed_owned[:, before + k * width : before + (k + 1) * width] for k in range(blocks - 1)]
        grad_reduce = jnp.concatenate([*grad_reduce, last_reduce], 0)
    return (
        layer_output,
        grad_clips,
        vector_grads[TIME_GAIN],
        vector_grads[TIME_SHIFT],
        grad_time_heads,
        grad_time_merge,
        vector_grads[MERGE_BIAS],
        grad_time_mixer,
        vector_grads[MIXER_BIAS],
        vector_grads[SPACE_GAIN],
        vector_grads[SPACE_SHIFT],
        grad_space_heads,
        grad_space_merge,
        vector_grads[SPACE_BIAS],
        vector_grads[FEED_GAIN],
        vector_grads[FEED_SHIFT],
        grad_expand,
        vector_grads[EXPAND_BIAS:].reshape(-1),
        grad_reduce,
        vector_grads[REDUCE_BIAS],
    )


def solution(mesh):
    clip, st = mesh.shape["clip"], mesh.shape["st"]
    finer = Mesh(mesh.devices.reshape(clip // 2, 2, st // 2, 2), ("z", "x", "y", "core"))
    token = P(("z", "x"), ("y", "core"), None, None)
    vec = P(("z", "x", "y", "core"))
    mat = P(("z", "x", "y", "core"), None)
    in_specs = (
        token, vec, vec, mat, mat, vec, mat, vec, vec, vec, mat, mat, vec, vec, vec, mat, vec, mat, vec, token,
    )
    out_specs = (
        token, token, vec, vec, mat, mat, vec, mat, vec, vec, vec, mat, mat, vec, vec, vec, mat, vec, mat, vec,
    )
    return jax.shard_map(body, mesh=finer, in_specs=in_specs, out_specs=out_specs, check_vma=False)
```
